32 devices in a mesh: seq: 8 (over y, x, core), rows: 4 (over z).
Axes of the slice: x: 2, y: 2, z: 4, core: 2. Of those that a mesh axis runs over, the one named last changes fastest.
Arguments:
- hidden: bfloat16 [16, 1024, 768], P('rows', 'seq'), may hold values from -6 to 6
- lengths: int32 [16, 4], P('rows'), may hold values from 1 to 1021, as said below
- cotangent: bfloat16 [16, 1024, 768], P('rows', 'seq'), may hold values from -6 to 6
- first_gain: float32 [768], replicated, may hold values from 0.1 to 1.9
- first_shift: float32 [768], replicated, may hold values from -1.75 to 1.75
- second_gain: float32 [768], replicated, may hold values from 0.1 to 1.9
- second_shift: float32 [768], replicated, may hold values from -1.75 to 1.75
- query_weight: bfloat16 [768, 768], replicated, may hold values from -0.21875 to 0.21875
- query_bias: float32 [768], replicated, may hold values from -3 to 3
- keyvalue_weight: bfloat16 [768, 128], replicated, may hold values from -0.21875 to 0.21875
- keyvalue_bias: float32 [128], replicated, may hold values from -3 to 3
- output_weight: bfloat16 [768, 768], replicated, may hold values from -0.875 to 0.875
- output_bias: float32 [768], replicated, may hold values from -3 to 3
- up_weight: bfloat16 [768, 3072], replicated, may hold values from -0.21875 to 0.21875
- up_bias: float32 [3072], replicated, may hold values from -3 to 3
- down_weight: bfloat16 [3072, 768], replicated, may hold values from -0.109375 to 0.109375
- down_bias: float32 [768], replicated, may hold values from -3 to 3
Outputs:
- layer_output: bfloat16 [16, 1024, 768], P('rows', 'seq')
- input_grad: bfloat16 [16, 1024, 768], P('rows', 'seq')
- grad_first_gain: float32 [768], replicated
- grad_first_shift: float32 [768], replicated
- grad_second_gain: float32 [768], replicated
- grad_second_shift: float32 [768], replicated
- grad_query_weight: float32 [768, 768], P('seq')
- grad_query_bias: float32 [768], replicated
- grad_keyvalue_weight: float32 [768, 128], P('seq')
- grad_keyvalue_bias: float32 [128], replicated
- grad_output_weight: float32 [768, 768], P('seq')
- grad_output_bias: float32 [768], replicated
- grad_up_weight: float32 [768, 3072], P('seq')
- grad_up_bias: float32 [3072], replicated
- grad_down_weight: float32 [3072, 768], P('seq')
- grad_down_bias: float32 [768], replicated
The draws below stay inside these ranges and needn't reach their ends.
Inputs may be any that keep to these rules, and one draw needn't show every extreme that they name: `lengths`: each row has 4 documents of 1 or more positions that together fill its 1024 positions.
All inputs are finite; a program needn't handle non-finite values.
Results may differ from the reference program's by a relative error of at most 0.015.
Values may be sent and summed in bfloat16 or wider, within the bound.
A program may use at most 192 MiB of HBM per device.

```python
import jax
import jax.numpy as jnp
from jax import lax

D = 768
H = 12
HD = 64
ROT = 16
FF = 3072
BLOCK = 128
ROWS_DEV = 4
LEN = 1024
ROWS = 16


def draw_lengths(key, part):
    key = jax.random.fold_in(key, 11)
    subkeys = jax.random.split(key, 5)
    row_keys = jax.random.split(subkeys[0], ROWS)
    picked = jax.vmap(lambda single: jax.random.permutation(single, LEN - 1)[:3])(row_keys) + 1
    loose = jnp.sort(picked.astype(jnp.int32), axis=1)
    early = 1 + jax.random.randint(subkeys[1], (ROWS,), 0, BLOCK // 2)
    late = LEN - 2 - jax.random.randint(subkeys[2], (ROWS,), 0, BLOCK // 2)
    tail_cut = late + 1 + jax.random.randint(subkeys[3], (ROWS,), 0, LEN - 1 - late)
    spanning = jnp.stack([early, late, tail_cut], axis=1).astype(jnp.int32)
    chosen = jax.random.randint(subkeys[4], (ROWS // ROWS_DEV,), 0, ROWS_DEV)
    row_slot = jnp.arange(ROWS, dtype=jnp.int32)
    is_long = row_slot % ROWS_DEV == jnp.repeat(chosen, ROWS_DEV)
    cut_points = jnp.where(is_long[:, None], spanning, loose).astype(jnp.int32)
    fixed_cuts = jnp.arange(1, 4, dtype=jnp.int32)
    cut_points = jnp.where((row_slot == 0)[:, None], fixed_cuts[None, :], cut_points).astype(jnp.int32)
    bounds = jnp.concatenate([jnp.zeros((ROWS, 1), jnp.int32), cut_points, jnp.full((ROWS, 1), LEN, jnp.int32)], axis=1)
    return (bounds[:, 1:] - bounds[:, :-1]).astype(jnp.int32)


def block_levels(stream_key, extent, pieces, low, largest):
    loudness, own = 1.0, jax.random.fold_in(stream_key, 6)
    for dim, parts in pieces:
        heights = jnp.exp(jax.random.uniform(jax.random.fold_in(own, dim), (parts,), jnp.float32, low / len(pieces), largest / len(pieces)))
        loudness = loudness * jnp.repeat(heights, extent[dim] // parts).reshape([-1 if axis == dim else 1 for axis in range(len(extent))])
    return loudness


def normal_values(stream_key, extent, width, reach, pieces=(), kind=jnp.bfloat16):
    drawn = jax.random.normal(stream_key, extent, jnp.float32) * width
    if len(pieces) > 0:
        drawn = block_levels(stream_key, extent, pieces, -0.22, 0.18) * drawn
    return jnp.clip(drawn, min=-reach, max=reach).astype(kind)


def setup_inputs(seed: int = 0) -> dict:
    key_list = jax.random.split(jax.random.key(seed), 18)
    hidden = normal_values(key_list[0], (ROWS, LEN, D), 1.0, 6.0, ((0, 4), (1, 8)))
    lengths = draw_lengths(jax.random.fold_in(key_list[17], 71), 0)
    cotangent = normal_values(key_list[2], (ROWS, LEN, D), 1.0, 6.0, ((0, 4), (1, 8)))
    first_gain = jnp.clip(1.0 + 0.18 * jax.random.normal(key_list[3], (D,), jnp.float32), 0.1, 1.9)
    first_shift = normal_values(key_list[4], (D,), 0.3, 1.75, (), jnp.float32)
    second_gain = jnp.clip(1.0 + 0.18 * jax.random.normal(key_list[5], (D,), jnp.float32), 0.1, 1.9)
    second_shift = normal_values(key_list[6], (D,), 0.3, 1.75, (), jnp.float32)
    query_weight = normal_values(key_list[7], (D, D), D ** -0.5, 0.21875)
    query_bias = normal_values(key_list[8], (D,), 0.5, 3.0, (), jnp.float32)
    keyvalue_weight = normal_values(key_list[9], (D, 2 * HD), D ** -0.5, 0.21875)
    keyvalue_bias = normal_values(key_list[10], (2 * HD,), 0.5, 3.0, (), jnp.float32)
    output_weight = normal_values(key_list[11], (D, D), (D // 16) ** -0.5, 0.875)
    output_bias = normal_values(key_list[12], (D,), 0.5, 3.0, (), jnp.float32)
    up_weight = normal_values(key_list[13], (D, FF), D ** -0.5, 0.21875)
    up_bias = normal_values(key_list[14], (FF,), 0.5, 3.0, (), jnp.float32)
    down_weight = normal_values(key_list[15], (FF, D), FF ** -0.5, 0.109375)
    down_bias = normal_values(key_list[16], (D,), 0.5, 3.0, (), jnp.float32)
    return dict(hidden=hidden, lengths=lengths, cotangent=cotangent, first_gain=first_gain, first_shift=first_shift, second_gain=second_gain, second_shift=second_shift, query_weight=query_weight, query_bias=query_bias, keyvalue_weight=keyvalue_weight, keyvalue_bias=keyvalue_bias, output_weight=output_weight, output_bias=output_bias, up_weight=up_weight, up_bias=up_bias, down_weight=down_weight, down_bias=down_bias)


@jax.custom_vjp
def low(v):
    return lax.optimization_barrier(v.astype(jnp.bfloat16)).astype(jnp.float32)

@jax.custom_vjp
def low_back(v):
    return v

def low_keep(v):
    return (low(v), None)

def low_pass(kept, grad):
    return (grad,)

def back_keep(v):
    return (v, None)

def back_low(kept, grad):
    return (low(grad),)
low.defvjp(low_keep, low_pass)
low_back.defvjp(back_keep, back_low)
norm_eps = 1e-05
highest = lax.Precision.HIGHEST

def layer_norm(values, gain, shift):
    centred = values - lax.optimization_barrier(jnp.mean(values, axis=-1, keepdims=True))
    factor = lax.rsqrt(lax.optimization_barrier(jnp.mean(centred * centred, axis=-1, keepdims=True)) + norm_eps)
    return centred * factor * gain + shift

def doc_layout(doc_lengths, row_len):
    ends = jnp.cumsum(doc_lengths, axis=-1).astype(jnp.int32)
    starts = (ends - doc_lengths).astype(jnp.int32)
    places = jnp.arange(row_len, dtype=jnp.int32)
    segment = lax.optimization_barrier(jnp.sum((places[None, :, None] >= ends[:, None, :]).astype(jnp.int32), axis=-1))
    owners = segment[:, :, None] == jnp.arange(doc_lengths.shape[-1], dtype=jnp.int32)[None, None, :]
    begin = lax.optimization_barrier(jnp.sum(jnp.where(owners, starts[:, None, :], 0), axis=-1))
    return (segment.astype(jnp.int32), (places[None, :] - begin).astype(jnp.int32))

def rotary_tables(positions, rot_dims):
    half_dims = rot_dims // 2
    freqs = jnp.power(10000.0, -2.0 * jnp.arange(half_dims, dtype=jnp.float32) / rot_dims)
    angles = positions.astype(jnp.float32)[..., None] * freqs
    return (jnp.cos(angles), jnp.sin(angles))

def rotate(values, cosine, sine):
    half_dims = cosine.shape[-1]
    front = values[..., :half_dims]
    behind = values[..., half_dims:2 * half_dims]
    remain = values[..., 2 * half_dims:]
    return jnp.concatenate([front * cosine - behind * sine, behind * cosine + front * sine, remain], axis=-1)

def gelu_exact(values):
    return 0.5 * values * (1.0 + lax.erf(values * 0.7071067811865476))

def row_layer(params, row_input, row_lengths):
    first_gain, first_shift, second_gain, second_shift, query_weight, query_bias, keyvalue_weight, keyvalue_bias, output_weight, output_bias, up_weight, up_bias, down_weight, down_bias = params
    segment, positions = doc_layout(row_lengths[None, :], LEN)
    segment = segment[0]
    positions = positions[0]
    first_norm = low(layer_norm(row_input, first_gain, first_shift))
    second_norm = low(layer_norm(row_input, second_gain, second_shift))
    queries = low_back(jnp.dot(first_norm, query_weight, precision=highest, preferred_element_type=jnp.float32) + query_bias)
    key_vals = low_back(jnp.dot(first_norm, keyvalue_weight, precision=highest, preferred_element_type=jnp.float32) + keyvalue_bias)
    cosine, sine = rotary_tables(positions, ROT)
    query_rot = low(rotate(queries.reshape(LEN, H, HD), cosine[:, None, :], sine[:, None, :]))
    key_rot = low(rotate(key_vals[:, :HD], cosine, sine))
    value_low = low(key_vals[:, HD:])
    scores = low_back(jnp.einsum('thd,sd->hts', query_rot, key_rot, precision=highest) * 0.125)
    places = jnp.arange(LEN, dtype=jnp.int32)
    visible = (places[None, :] <= places[:, None]) & (segment[None, :] == segment[:, None])
    scores = jnp.where(visible[None, :, :], scores, -1e+30)
    row_max = lax.optimization_barrier(jnp.max(scores, axis=-1, keepdims=True))
    expo = jnp.exp(scores - row_max)
    probs = low(expo / lax.optimization_barrier(jnp.sum(expo, axis=-1, keepdims=True)))
    mixed = jnp.einsum('hts,sd->thd', probs, value_low, precision=highest).reshape(LEN, D)
    mixed_low = low(low_back(mixed))
    attn_out = jnp.dot(mixed_low, output_weight, precision=highest, preferred_element_type=jnp.float32) + output_bias
    up_pre = low_back(jnp.dot(second_norm, up_weight, precision=highest, preferred_element_type=jnp.float32) + up_bias)
    act = low(gelu_exact(up_pre))
    ffn_out = jnp.dot(act, down_weight, precision=highest, preferred_element_type=jnp.float32) + down_bias
    return row_input + attn_out + ffn_out

def reference(hidden, lengths, cotangent, first_gain, first_shift, second_gain, second_shift, query_weight, query_bias, keyvalue_weight, keyvalue_bias, output_weight, output_bias, up_weight, up_bias, down_weight, down_bias):
    params = tuple((item.astype(jnp.float32) for item in (first_gain, first_shift, second_gain, second_shift, query_weight, query_bias, keyvalue_weight, keyvalue_bias, output_weight, output_bias, up_weight, up_bias, down_weight, down_bias)))
    inputs = hidden.astype(jnp.float32)

    def forward(weights, values):
        layer = jax.checkpoint(lambda row_input, row_lengths: row_layer(weights, row_input, row_lengths))
        return lax.map(lambda pair: layer(pair[0], pair[1]), (values, lengths))
    result, pull = jax.vjp(forward, params, inputs)
    grads, grad_inputs = pull(cotangent.astype(jnp.float32))
    return (result.astype(jnp.bfloat16), grad_inputs.astype(jnp.bfloat16), grads[0], grads[1], grads[2], grads[3], grads[4], grads[5], grads[6], grads[7], grads[8], grads[9], grads[10], grads[11], grads[12], grads[13])
```

```python
import functools

import jax
import jax.numpy as jnp
from jax import lax
from jax.experimental import pallas as pl
from jax.experimental.pallas import tpu as pltpu
from jax.sharding import PartitionSpec as P

HD = 64
ROT = 16
BLK = 128
NEG = -1e30
EPS = 1e-05
F32 = jnp.float32
BF = jnp.bfloat16


def dot(a, b):
    return jnp.dot(a, b, preferred_element_type=F32)


def dot_nt(a, b):
    return lax.dot_general(a, b, (((1,), (1,)), ((), ())), preferred_element_type=F32)


def dot_tn(a, b):
    return lax.dot_general(a, b, (((0,), (0,)), ((), ())), preferred_element_type=F32)


def doc_start(place, cuts):
    begin = jnp.where(place >= cuts[0], cuts[0], 0)
    for cut in cuts[1:]:
        begin = jnp.where(place >= cut, cut, begin)
    return begin


def attn_kernel(
    own_ref, len_ref, q_ref, do_ref, kv_ref, cos_ref, sin_ref,
    mt_ref, mx_ref, dq_ref, dkv_ref,
    s_ref, e_ref, qz, dz, m_ref, l_ref, o_ref, dqa,
):
    row = pl.program_id(0)
    own = own_ref[0]
    lanes = q_ref.shape[-1]
    heads = lanes // BLK
    cuts = []
    for i in range(len_ref.shape[1] - 1):
        cuts.append(len_ref[row, i] + (cuts[-1] if cuts else 0))
    t0 = own * BLK
    low = doc_start(t0, cuts) // BLK
    place = t0 + lax.broadcasted_iota(jnp.int32, (BLK, BLK), 1)
    begin = doc_start(place, cuts)
    key_iota = lax.broadcasted_iota(jnp.int32, (BLK, BLK), 0)
    qz[:HD, :] = q_ref[0]
    qz[HD:, :] = jnp.zeros((HD, lanes), BF)
    dz[HD:, :] = do_ref[0]
    dz[:HD, :] = jnp.zeros((HD, lanes), BF)
    m_ref[...] = jnp.full(m_ref.shape, NEG, F32)
    l_ref[...] = jnp.zeros(l_ref.shape, F32)
    o_ref[...] = jnp.zeros(o_ref.shape, F32)
    dqa[...] = jnp.zeros(dqa.shape, F32)
    dkv_ref[...] = jnp.zeros(dkv_ref.shape, dkv_ref.dtype)

    def scores(j, _):
        kv = kv_ref[0, pl.ds(pl.multiple_of(j * BLK, BLK), BLK), :]
        keys = j * BLK + key_iota
        bias = jnp.where((keys <= place) & (keys >= begin), 0.0, NEG)
        s = dot(kv, qz[...]) + jnp.concatenate([bias] * heads, axis=1)
        s_ref[j] = s
        m_ref[...] = jnp.maximum(m_ref[...], jnp.max(s.reshape(BLK // 8, 8, lanes), axis=0))
        return 0

    lax.fori_loop(low, own + 1, scores, 0)
    m_ref[0:1, :] = jnp.max(m_ref[...], axis=0, keepdims=True)

    def mix(j, _):
        v_t = kv_ref[0, pl.ds(pl.multiple_of(j * BLK, BLK), BLK), :].T[HD:]
        e = jnp.exp(s_ref[j] - m_ref[0:1, :])
        l_ref[...] += jnp.sum(e.reshape(BLK // 8, 8, lanes), axis=0)
        e_low = e.astype(BF)
        e_ref[j] = e_low
        o_ref[...] += dot(v_t, e_low)
        return 0

    lax.fori_loop(low, own + 1, mix, 0)
    inv = 1.0 / jnp.sum(l_ref[...], axis=0, keepdims=True)
    o = o_ref[...] * inv
    l_ref[0:1, :] = inv
    m_ref[0:1, :] = jnp.sum(o * dz[HD:, :].astype(F32), axis=0, keepdims=True)
    for h in range(0, heads, 2):
        pair = jnp.concatenate(
            [o[:, h * BLK : (h + 1) * BLK], o[:, (h + 1) * BLK : (h + 2) * BLK]], axis=0
        )
        mt_ref[0, h * HD : (h + 2) * HD, :] = pair.astype(BF)
        mx_ref[0, :, h * HD : (h + 2) * HD] = pair.T.astype(BF)

    def back(j, _):
        rows = pl.ds(pl.multiple_of(j * BLK, BLK), BLK)
        kv = kv_ref[0, rows, :]
        k_t = kv.T[:HD]
        dp = dot(kv, dz[...])
        p = e_ref[j].astype(F32) * l_ref[0:1, :]
        ds = (p * (dp - m_ref[0:1, :])).astype(BF)
        acc = dot_nt(ds, qz[...]) + dot_nt(p.astype(BF), dz[...])
        dqa[...] += dot(k_t, ds)
        dkv_ref[0, rows, :] = acc.astype(dkv_ref.dtype)
        return 0

    lax.fori_loop(low, own + 1, back, 0)
    cosine, sine = cos_ref[0], sin_ref[0]
    for h in range(0, heads, 2):
        parts = []
        for g in (h, h + 1):
            d = dqa[:, g * BLK : (g + 1) * BLK]
            front, behind = d[0:8], d[8:16]
            parts += [front * cosine + behind * sine, behind * cosine - front * sine, d[16:]]
        dq_ref[0, :, h * HD : (h + 2) * HD] = (jnp.concatenate(parts, axis=0) * 0.125).T.astype(BF)


def attention(own, lengths, q, do, kv, cosine, sine):
    rows, length, _ = kv.shape
    lanes = q.shape[-1]
    width = lanes // BLK * HD
    blocks = length // BLK

    def per_row(*shape):
        return pl.BlockSpec((1,) + shape, lambda r, *_: (r,) + (0,) * len(shape))

    return pl.pallas_call(
        attn_kernel,
        grid_spec=pltpu.PrefetchScalarGridSpec(
            num_scalar_prefetch=2,
            grid=(rows,),
            in_specs=[
                per_row(HD, lanes), per_row(HD, lanes), per_row(length, 2 * HD),
                per_row(8, BLK), per_row(8, BLK),
            ],
            out_specs=[
                per_row(width, BLK), per_row(BLK, width), per_row(BLK, width),
                per_row(length, 2 * HD),
            ],
            scratch_shapes=[
                pltpu.VMEM((blocks, BLK, lanes), F32),
                pltpu.VMEM((blocks, BLK, lanes), BF),
                pltpu.VMEM((2 * HD, lanes), BF),
                pltpu.VMEM((2 * HD, lanes), BF),
                pltpu.VMEM((8, lanes), F32),
                pltpu.VMEM((8, lanes), F32),
                pltpu.VMEM((HD, lanes), F32),
                pltpu.VMEM((HD, lanes), F32),
            ],
        ),
        out_shape=[
            jax.ShapeDtypeStruct((rows, width, BLK), BF),
            jax.ShapeDtypeStruct((rows, BLK, width), BF),
            jax.ShapeDtypeStruct((rows, BLK, width), BF),
            jax.ShapeDtypeStruct((rows, length, 2 * HD), BF),
        ],
        compiler_params=pltpu.CompilerParams(
            vmem_limit_bytes=50 * 2**20, dimension_semantics=("arbitrary",)
        ),
        cost_estimate=pl.CostEstimate(
            flops=10 * rows * length * lanes * HD, bytes_accessed=8 * 2**20,
            transcendentals=rows * length * lanes,
        ),
        name="attention",
    )(own, lengths, q, do, kv, cosine, sine)


def ffn_kernel(h_ref, ht_ref, dy_ref, wu_ref, wd_ref, bu_ref, fo_ref, dh_ref, gu_ref, gd_ref, gb_ref):
    step = pl.program_id(0)
    h, dy, wu, wd = h_ref[...], dy_ref[...], wu_ref[...], wd_ref[...]
    up = dot(h, wu) + bu_ref[...]
    d_act = dot_nt(dy, wd)
    cdf = 0.5 + 0.5 * lax.erf(up * 0.7071067811865476)
    act = (up * cdf).astype(BF)
    pdf = jnp.exp(-0.5 * up * up) * 0.3989422804014327
    d_up = (d_act * (cdf + up * pdf)).astype(BF)
    gb_ref[...] = jnp.sum(d_up.astype(F32), axis=0, keepdims=True)

    @pl.when(step == 0)
    def _():
        fo_ref[...] = jnp.zeros_like(fo_ref)
        dh_ref[...] = jnp.zeros_like(dh_ref)

    fo_ref[...] += dot(act, wd)
    dh_ref[...] += dot_nt(d_up, wu)
    gu_ref[...] = dot(ht_ref[...], d_up).astype(BF)
    gd_ref[...] = dot_tn(act, dy).astype(BF)


def ffn(h, dy, wu, wd, bu, cols=768):
    toks, width = h.shape
    hidden = wu.shape[1]

    def full(*shape):
        return pl.BlockSpec(shape, lambda i: (0,) * len(shape))

    up_spec = pl.BlockSpec((width, cols), lambda i: (0, i))
    down_spec = pl.BlockSpec((cols, width), lambda i: (i, 0))
    bias_spec = pl.BlockSpec((1, cols), lambda i: (0, i))
    return pl.pallas_call(
        ffn_kernel,
        grid=(hidden // cols,),
        in_specs=[full(toks, width), full(width, toks), full(toks, width), up_spec, down_spec, bias_spec],
        out_specs=[full(toks, width), full(toks, width), up_spec, down_spec, bias_spec],
        out_shape=[
            jax.ShapeDtypeStruct((toks, width), F32),
            jax.ShapeDtypeStruct((toks, width), F32),
            jax.ShapeDtypeStruct((width, hidden), BF),
            jax.ShapeDtypeStruct((hidden, width), BF),
            jax.ShapeDtypeStruct((1, hidden), F32),
        ],
        compiler_params=pltpu.CompilerParams(
            vmem_limit_bytes=50 * 2**20, dimension_semantics=("arbitrary",)
        ),
        cost_estimate=pl.CostEstimate(
            flops=12 * toks * width * hidden, bytes_accessed=8 * width * hidden, transcendentals=2 * toks * hidden
        ),
        name="feed_forward",
    )(h, h.T, dy, wu, wd, bu[None, :])


def rotate_t(values, cosine, sine):
    front, behind = values[:, :, :8], values[:, :, 8:16]
    return jnp.concatenate(
        [front * cosine - behind * sine, behind * cosine + front * sine, values[:, :, 16:]], axis=2
    )


def shards(
    hidden, lengths, cotangent, first_gain, first_shift, second_gain, second_shift,
    query_weight, query_bias, keyvalue_weight, keyvalue_bias, output_weight, output_bias,
    up_weight, up_bias, down_weight, down_bias,
):
    rows, block, width = hidden.shape
    heads = width // HD
    toks = rows * block
    own = lax.axis_index("seq")
    cuts = [jnp.sum(lengths[:, : i + 1], axis=1)[:, None] for i in range(lengths.shape[1] - 1)]
    place = own * block + jnp.arange(block, dtype=jnp.int32)[None, :]
    positions = place - doc_start(place, cuts)
    freqs = jnp.power(10000.0, -2.0 * jnp.arange(ROT // 2, dtype=F32) / ROT)
    angles = positions.astype(F32)[:, None, :] * freqs[None, :, None]
    cosine, sine = jnp.cos(angles), jnp.sin(angles)

    x = hidden.astype(F32).reshape(toks, width)
    dy = cotangent.reshape(toks, width)
    dy32 = dy.astype(F32)
    centred = x - jnp.mean(x, axis=-1, keepdims=True)
    factor = lax.rsqrt(jnp.mean(centred * centred, axis=-1, keepdims=True) + EPS)
    xhat = centred * factor
    h1 = (xhat * first_gain + first_shift).astype(BF)
    h2 = (xhat * second_gain + second_shift).astype(BF)

    kv = (dot(h1, keyvalue_weight) + keyvalue_bias).reshape(rows, block, 2 * HD)
    cos_k, sin_k = cosine.swapaxes(1, 2), sine.swapaxes(1, 2)
    front, behind = kv[..., :8], kv[..., 8:16]
    kv_low = jnp.concatenate(
        [front * cos_k - behind * sin_k, behind * cos_k + front * sin_k, kv[..., 16:]], axis=-1
    ).astype(BF)
    kv_full = lax.all_gather(kv_low, "seq", axis=1, tiled=True)

    ffn_out, second_grad, g_up, g_down, g_up_bias = ffn(h2, dy, up_weight, down_weight, up_bias)

    q = jnp.einsum("rtd,de->ret", h1.reshape(rows, block, width), query_weight, preferred_element_type=F32)
    q = (q + query_bias[None, :, None]).reshape(rows, heads, HD, block)
    q = (rotate_t(q, cosine[:, None], sine[:, None]).astype(BF) * 0.125).astype(BF)
    q = q.transpose(0, 2, 1, 3).reshape(rows, HD, heads * block)
    do = jnp.einsum("rtd,ed->ret", dy.reshape(rows, block, width), output_weight, preferred_element_type=F32)
    do = do.astype(BF).reshape(rows, heads, HD, block).transpose(0, 2, 1, 3).reshape(rows, HD, heads * block)

    mixed_t, mixed, dq, dkv = attention(own[None], lengths, q, do, kv_full, cosine, sine)
    mixed = mixed.reshape(toks, width)
    dq = dq.reshape(toks, width)
    layer_output = x + dot(mixed, output_weight) + output_bias + ffn_out + down_bias
    layer_output = layer_output.astype(BF).reshape(rows, block, width)
    g_out = jnp.einsum("ret,rtd->ed", mixed_t, cotangent, preferred_element_type=F32)
    g_query = dot_tn(h1, dq)

    dkv = lax.psum_scatter(dkv, "seq", scatter_dimension=1, tiled=True).astype(F32)
    front, behind = dkv[..., :8], dkv[..., 8:16]
    d_kv = jnp.concatenate(
        [front * cos_k + behind * sin_k, behind * cos_k - front * sin_k, dkv[..., 16:]], axis=-1
    ).astype(BF).reshape(toks, 2 * HD)
    g_kv = dot_tn(h1, d_kv)
    first_grad = dot_nt(dq, query_weight) + dot_nt(d_kv, keyvalue_weight)

    def norm_back(grad, gain):
        g = grad * gain
        return factor * (
            g - jnp.mean(g, axis=-1, keepdims=True) - xhat * jnp.mean(g * xhat, axis=-1, keepdims=True)
        )

    input_grad = dy32 + norm_back(first_grad, first_gain) + norm_back(second_grad, second_gain)
    input_grad = input_grad.astype(BF).reshape(rows, block, width)

    seq_size = lax.axis_size("seq")

    def by_owner(g):
        return g.astype(BF).reshape(seq_size, -1, 512)

    def summed(parts):
        joined = jnp.concatenate([by_owner(g) for g in parts], axis=1)
        part = lax.psum_scatter(joined, "seq", scatter_dimension=0, tiled=True)[0]
        return lax.psum(part, "rows").astype(F32)

    first = summed([g_up, g_down])
    second = summed([g_out, g_query, g_kv])

    def split(part, shapes):
        outs, at = [], 0
        for shape in shapes:
            n = shape[0] * shape[1] // 512
            outs.append(part[at : at + n].reshape(shape))
            at += n
        return outs

    sub = width // seq_size
    hid = up_weight.shape[1]
    s_up, s_down = split(first, [(sub, hid), (hid // seq_size, width)])
    s_out, s_query, s_kv = split(second, [(sub, width), (sub, width), (sub, 2 * HD)])

    small = lax.psum(
        jnp.concatenate([
            jnp.sum(first_grad * xhat, axis=0), jnp.sum(first_grad, axis=0),
            jnp.sum(second_grad * xhat, axis=0), jnp.sum(second_grad, axis=0),
            jnp.sum(dq.astype(F32), axis=0), jnp.sum(d_kv.astype(F32), axis=0),
            jnp.sum(dy32, axis=0), g_up_bias[0],
        ]),
        ("seq", "rows"),
    )
    sizes = [width] * 5 + [2 * HD, width, hid]
    pieces, at = [], 0
    for size in sizes:
        pieces.append(small[at : at + size])
        at += size
    s_fg, s_fs, s_sg, s_ss, s_qb, s_kb, s_ob, s_ub = pieces
    return (
        layer_output, input_grad, s_fg, s_fs, s_sg, s_ss, s_query, s_qb, s_kv, s_kb,
        s_out, s_ob, s_up, s_ub, s_down, s_ob,
    )


def solution(mesh):
    tokens = P("rows", "seq", None)
    weight = P("seq", None)
    return jax.shard_map(
        shards,
        mesh=mesh,
        in_specs=(tokens, P("rows", None), tokens) + (P(),) * 14,
        out_specs=(
            tokens, tokens, P(), P(), P(), P(), weight, P(), weight, P(), weight, P(), weight, P(), weight, P(),
        ),
        check_vma=False,
    )
```

```python
import functools

import jax
import jax.numpy as jnp
from jax import lax
from jax.experimental import pallas as pl
from jax.experimental.pallas import tpu as pltpu
from jax.sharding import PartitionSpec as P

HD = 64
ROT = 16
BLK = 128
NEG = -1e30
EPS = 1e-05
F32 = jnp.float32
BF = jnp.bfloat16


def dot(a, b):
    return jnp.dot(a, b, preferred_element_type=F32)


def dot_nt(a, b):
    return lax.dot_general(a, b, (((1,), (1,)), ((), ())), preferred_element_type=F32)


def dot_tn(a, b):
    return lax.dot_general(a, b, (((0,), (0,)), ((), ())), preferred_element_type=F32)


def doc_start(place, cuts):
    begin = jnp.where(place >= cuts[0], cuts[0], 0)
    for cut in cuts[1:]:
        begin = jnp.where(place >= cut, cut, begin)
    return begin


def attn_kernel(
    own_ref, len_ref, q_ref, do_ref, kv_ref, cos_ref, sin_ref,
    mt_ref, mx_ref, dq_ref, dkv_ref,
    s_ref, e_ref, qz, dz, m_ref, l_ref, o_ref, dqa,
):
    row = pl.program_id(0)
    own = own_ref[0]
    lanes = q_ref.shape[-1]
    heads = lanes // BLK
    cuts = []
    for i in range(len_ref.shape[1] - 1):
        cuts.append(len_ref[row, i] + (cuts[-1] if cuts else 0))
    t0 = own * BLK
    low = doc_start(t0, cuts) // BLK
    place = t0 + lax.broadcasted_iota(jnp.int32, (BLK, BLK), 1)
    begin = doc_start(place, cuts)
    key_iota = lax.broadcasted_iota(jnp.int32, (BLK, BLK), 0)
    qz[:HD, :] = q_ref[0]
    qz[HD:, :] = jnp.zeros((HD, lanes), BF)
    dz[HD:, :] = do_ref[0]
    dz[:HD, :] = jnp.zeros((HD, lanes), BF)
    m_ref[...] = jnp.full(m_ref.shape, NEG, F32)
    l_ref[...] = jnp.zeros(l_ref.shape, F32)
    o_ref[...] = jnp.zeros(o_ref.shape, F32)
    dqa[...] = jnp.zeros(dqa.shape, F32)
    dkv_ref[...] = jnp.zeros(dkv_ref.shape, dkv_ref.dtype)

    def scores(j, _):
        kv = kv_ref[0, pl.ds(pl.multiple_of(j * BLK, BLK), BLK), :]
        keys = j * BLK + key_iota
        bias = jnp.where((keys <= place) & (keys >= begin), 0.0, NEG)
        s = dot(kv, qz[...]) + jnp.concatenate([bias] * heads, axis=1)
        s_ref[j] = s
        m_ref[...] = jnp.maximum(m_ref[...], jnp.max(s.reshape(BLK // 8, 8, lanes), axis=0))
        return 0

    lax.fori_loop(low, own + 1, scores, 0)
    m_ref[0:1, :] = jnp.max(m_ref[...], axis=0, keepdims=True)

    def mix(j, _):
        v_t = kv_ref[0, pl.ds(pl.multiple_of(j * BLK, BLK), BLK), :].T[HD:]
        e = jnp.exp(s_ref[j] - m_ref[0:1, :])
        l_ref[...] += jnp.sum(e.reshape(BLK // 8, 8, lanes), axis=0)
        e_low = e.astype(BF)
        e_ref[j] = e_low
        o_ref[...] += dot(v_t, e_low)
        return 0

    lax.fori_loop(low, own + 1, mix, 0)
    inv = 1.0 / jnp.sum(l_ref[...], axis=0, keepdims=True)
    o = o_ref[...] * inv
    l_ref[0:1, :] = inv
    m_ref[0:1, :] = jnp.sum(o * dz[HD:, :].astype(F32), axis=0, keepdims=True)
    for h in range(0, heads, 2):
        pair = jnp.concatenate(
            [o[:, h * BLK : (h + 1) * BLK], o[:, (h + 1) * BLK : (h + 2) * BLK]], axis=0
        )
        mt_ref[0, h * HD : (h + 2) * HD, :] = pair.astype(BF)
        mx_ref[0, :, h * HD : (h + 2) * HD] = pair.T.astype(BF)

    def back(j, _):
        rows = pl.ds(pl.multiple_of(j * BLK, BLK), BLK)
        kv = kv_ref[0, rows, :]
        k_t = kv.T[:HD]
        dp = dot(kv, dz[...])
        p = e_ref[j].astype(F32) * l_ref[0:1, :]
        ds = (p * (dp - m_ref[0:1, :])).astype(BF)
        acc = dot_nt(ds, qz[...]) + dot_nt(p.astype(BF), dz[...])
        dqa[...] += dot(k_t, ds)
        dkv_ref[0, rows, :] = acc.astype(dkv_ref.dtype)
        return 0

    lax.fori_loop(low, own + 1, back, 0)
    cosine, sine = cos_ref[0], sin_ref[0]
    for h in range(0, heads, 2):
        parts = []
        for g in (h, h + 1):
            d = dqa[:, g * BLK : (g + 1) * BLK]
            front, behind = d[0:8], d[8:16]
            parts += [front * cosine + behind * sine, behind * cosine - front * sine, d[16:]]
        dq_ref[0, :, h * HD : (h + 2) * HD] = (jnp.concatenate(parts, axis=0) * 0.125).T.astype(BF)


def attention(own, lengths, q, do, kv, cosine, sine):
    rows, length, _ = kv.shape
    lanes = q.shape[-1]
    width = lanes // BLK * HD
    blocks = length // BLK

    def per_row(*shape):
        return pl.BlockSpec((1,) + shape, lambda r, *_: (r,) + (0,) * len(shape))

    return pl.pallas_call(
        attn_kernel,
        grid_spec=pltpu.PrefetchScalarGridSpec(
            num_scalar_prefetch=2,
            grid=(rows,),
            in_specs=[
                per_row(HD, lanes), per_row(HD, lanes), per_row(length, 2 * HD),
                per_row(8, BLK), per_row(8, BLK),
            ],
            out_specs=[
                per_row(width, BLK), per_row(BLK, width), per_row(BLK, width),
                per_row(length, 2 * HD),
            ],
            scratch_shapes=[
                pltpu.VMEM((blocks, BLK, lanes), F32),
                pltpu.VMEM((blocks, BLK, lanes), BF),
                pltpu.VMEM((2 * HD, lanes), BF),
                pltpu.VMEM((2 * HD, lanes), BF),
                pltpu.VMEM((8, lanes), F32),
                pltpu.VMEM((8, lanes), F32),
                pltpu.VMEM((HD, lanes), F32),
                pltpu.VMEM((HD, lanes), F32),
            ],
        ),
        out_shape=[
            jax.ShapeDtypeStruct((rows, width, BLK), BF),
            jax.ShapeDtypeStruct((rows, BLK, width), BF),
            jax.ShapeDtypeStruct((rows, BLK, width), BF),
            jax.ShapeDtypeStruct((rows, length, 2 * HD), BF),
        ],
        compiler_params=pltpu.CompilerParams(
            vmem_limit_bytes=50 * 2**20, dimension_semantics=("arbitrary",)
        ),
        cost_estimate=pl.CostEstimate(
            flops=10 * rows * length * lanes * HD, bytes_accessed=8 * 2**20,
            transcendentals=rows * length * lanes,
        ),
        name="attention",
    )(own, lengths, q, do, kv, cosine, sine)


MESH = pl.DeviceIdType.MESH
RING = 5
SLOTS = 3


def bits_of(value, count):
    return [value // 2**i % 2 for i in range(count)]


class Net:
    def __init__(self, seq_bits, row_bits):
        self.a, self.b = seq_bits, row_bits
        self.me, self.row = lax.axis_index("seq"), lax.axis_index("rows")
        self.sb, self.rb = bits_of(self.me, seq_bits), bits_of(self.row, row_bits)

    def seq_xor(self, mask):
        out = self.me
        for i in range(self.a):
            if mask >> i & 1:
                out = out + (1 - 2 * self.sb[i]) * 2**i
        return {"seq": out}

    def row_xor(self, mask):
        out = self.row
        for i in range(self.b):
            if mask >> i & 1:
                out = out + (1 - 2 * self.rb[i]) * 2**i
        return {"rows": out}

    def greet(self):
        barrier = pltpu.get_barrier_semaphore()
        peers = [self.seq_xor(m) for m in range(1, 2**self.a)] + [self.row_xor(m) for m in range(1, 2**self.b)]
        for peer in peers:
            pl.semaphore_signal(barrier, inc=1, device_id=peer, device_id_type=MESH)
        pl.semaphore_wait(barrier, len(peers))

    def pick(self, left, bit, mine):
        own = self.sb[bit]
        return tuple((own if mine else 1 - own) if i == bit else slice(None) for i in left)


def remote(src, dst, send_sem, recv_sem, peer):
    return pltpu.make_async_remote_copy(
        src_ref=src, dst_ref=dst, send_sem=send_sem, recv_sem=recv_sem, device_id=peer, device_id_type=MESH
    )


class Ring:
    def __init__(self, net, total, grads, recs, recz, fin, send_sem, recv_sem):
        self.net, self.total = net, total
        self.grads, self.recs, self.recz, self.fin = grads, recs, recz, fin
        self.send_sem, self.recv_sem = send_sem, recv_sem
        a, b = net.a, net.b
        self.halves = min(b, 2)
        self.stages = [("first", 0)] + [("seq", k) for k in range(1, a)]
        self.stages += [("split", i) for i in range(self.halves)]
        self.stages += [("whole", i) for i in range(2, b)]
        self.stages += [("back", i) for i in reversed(range(self.halves))]
        self.sem_at, n = [], 0
        for kind, _ in self.stages:
            self.sem_at.append(n)
            n += 2 if kind == "seq" else 1

    def moves(self, stage, ch):
        net, a = self.net, self.net.a
        kind, k = self.stages[stage]
        if kind == "first":
            left = range(a - 1, -1, -1)
            slot, at = (ch % SLOTS,), (ch % RING,)
            return [(self.grads.at[slot + net.pick(left, 0, False)], self.recs[0].at[at], net.seq_xor(1),
                     (self.grads, slot + net.pick(left, 0, True)), (self.recs[0], at))]
        if kind == "seq":
            out = []
            prev, here = self.recs[k - 1], self.recs[k]
            for half in (0, 1):
                if half == 0:
                    bit, left = k, range(a - 1, k - 1, -1)
                else:
                    bit, left = a - k, range(a - k, 0, -1)
                if k == 1:
                    base, tail = (ch % RING,), (half,)
                else:
                    base, tail = (ch, half), ()
                out.append((prev.at[base + net.pick(left, bit, False) + tail], here.at[ch, half], net.seq_xor(1 << bit),
                            (prev, base + net.pick(left, bit, True) + tail), (here, (ch, half))))
            return out
        if kind == "split":
            prev = self.recs[a - 1] if k == 0 else self.recz[k - 1]
            return [(prev.at[ch, 1 - net.rb[k]], self.recz[k].at[ch], net.row_xor(1 << k),
                     (prev, (ch, net.rb[k])), (self.recz[k], (ch,)))]
        if kind == "whole":
            prev = self.recz[k - 1]
            return [(prev.at[ch], self.recz[k].at[ch], net.row_xor(1 << k), (prev, (ch,)), (self.recz[k], (ch,)))]
        at = (ch,) + tuple(net.rb[: k + 1])
        return [(self.fin.at[at], self.fin.at[at], net.row_xor(1 << k), None, None)]

    def copies(self, stage, ch):
        out = []
        for i, (src, dst, peer, _, _) in enumerate(self.moves(stage, ch)):
            sem = self.sem_at[stage] + i
            out.append(remote(src, dst, self.send_sem.at[ch, sem], self.recv_sem.at[ch, sem], peer))
        return out

    def start(self, stage, ch):
        for copy in self.copies(stage, ch):
            copy.start()

    def finish(self, stage, ch):
        for copy in self.copies(stage, ch):
            copy.wait()
        kind, _ = self.stages[stage]
        if kind != "back":
            last = self.stages[stage + 1][0] == "back"
            for _, _, _, (src, src_at), (dst, dst_at) in self.moves(stage, ch):
                total = src[src_at] + dst[dst_at]
                if last:
                    self.fin[(ch,) + tuple(self.net.rb[: self.halves])] = total
                else:
                    dst[dst_at] = total
        if stage + 1 < len(self.stages):
            self.start(stage + 1, ch)

    def tick(self, t):
        for stage in reversed(range(len(self.stages))):
            ch = t - 1 - stage
            if isinstance(ch, int):
                if 0 <= ch < self.total:
                    self.finish(stage, ch)
            else:

                @pl.when((ch >= 0) & (ch < self.total))
                def _():
                    self.finish(stage, ch)


CHUNK = 512
QUARTER = 128


def put_chunk(grads, slot, a, owner, sub, value, quarters):
    at = (slot,) + tuple(reversed(bits_of(owner, a)))
    for i, q in enumerate(quarters):
        grads[at + (q // 2, q % 2)] = value[:, i * QUARTER : (i + 1) * QUARTER].astype(BF)


def gelu_parts(up):
    cdf = 0.5 + 0.5 * lax.erf(up * 0.7071067811865476)
    pdf = jnp.exp(-0.5 * up * up) * 0.3989422804014327
    return cdf, up * pdf


def lanes_mean(v):
    return jnp.mean(v, axis=-1, keepdims=True)


def tail_kernel(
    seq_bits, row_bits,
    x_ref, dy_ref, h1_ref, h2_ref, mt_ref, mx_ref, dq_ref, dkv_ref, turn_ref, vec_ref, bu_ref,
    wq_hbm, wkv_hbm, wo_hbm, wu_hbm, wd_hbm,
    lo_ref, ig_ref, gup_ref, gdown_ref, gout_ref, gq_ref, gkv_ref, small_ref,
    wq, wkv, wo, wu, wd, load_sem,
    h1t, h2t, act, act_t, dup, gub,
    grads, *rest,
):
    a, n = seq_bits, 2**seq_bits
    recs, rest = rest[:a], rest[a:]
    recz, rest = rest[:row_bits], rest[row_bits:]
    fin, send_sem, recv_sem, rest = rest[0], rest[1], rest[2], rest[3:]
    kvr, rest = rest[:a], rest[a:]
    kv_send, kv_recv, own_kv, seq_kv, row_kv, own_small, seq_small, row_small, m_send, m_recv = rest
    net = Net(seq_bits, row_bits)
    total = 2 * 6 + 3
    ring = Ring(net, total, grads, recs, recz, fin, send_sem, recv_sem)
    toks, width = x_ref.shape
    hidden = wu.shape[1]
    sub = width // n
    loads = []
    for i, (src, dst) in enumerate(((wu_hbm, wu), (wd_hbm, wd), (wo_hbm, wo), (wq_hbm, wq), (wkv_hbm, wkv))):
        loads.append(pltpu.make_async_copy(src, dst, load_sem.at[i]))
        loads[-1].start()
    net.greet()

    def kv_moves(k):
        out = []
        for half in (0, 1):
            if k == 0:
                bit, left = 0, range(a - 1, -1, -1)
            elif half == 0:
                bit, left = k, range(a - 1, k - 1, -1)
            else:
                bit, left = a - k, range(a - k, 0, -1)
            prev = dkv_ref if k == 0 else kvr[k - 1]
            sem = 2 * k + half
            at = (half, slice(None))
            out.append((remote(prev.at[at + net.pick(left, bit, False)], kvr[k].at[half],
                               kv_send.at[sem], kv_recv.at[sem], net.seq_xor(1 << bit)),
                        prev, at + net.pick(left, bit, True), half))
        return out

    def kv_start(k):
        for copy, *_ in kv_moves(k):
            copy.start()

    def kv_finish(k):
        for copy, prev, at, half in kv_moves(k):
            copy.wait()
            kvr[k][half] = kvr[k][half] + prev[at]
        if k + 1 < a:
            kv_start(k + 1)

    kv_start(0)

    h1t[...] = h1_ref[...].T
    h2t[...] = h2_ref[...].T
    dy = dy_ref[...]

    def rows_of(ref, owner):
        return ref[owner * sub : (owner + 1) * sub, :]

    for owner in range(n):
        put_chunk(grads, 0, a, owner, sub, dot(rows_of(mt_ref, owner), dy[:, :CHUNK]), (0, 1, 2, 3))
    ring.start(0, 0)
    ring.tick(0)
    kv_finish(0)
    for owner in range(n):
        put_chunk(grads, 1, a, owner, sub, dot(rows_of(mt_ref, owner), dy[:, CHUNK:]), (0, 1))
        put_chunk(grads, 1, a, owner, sub, dot(rows_of(h1t, owner), dq_ref[:, :256]), (2, 3))
    ring.start(0, 1)
    ring.tick(1)
    kv_finish(1)
    for owner in range(n):
        put_chunk(grads, 2, a, owner, sub, dot(rows_of(h1t, owner), dq_ref[:, 256:]), (0, 1, 2, 3))
    ring.start(0, 2)
    ring.tick(2)
    for k in range(2, a):
        kv_finish(k)
    loads[0].wait()
    loads[1].wait()

    def feed(f, _):
        cols = pl.ds(pl.multiple_of(f * CHUNK, CHUNK), CHUNK)
        ch = 3 + f
        up = dot(h2_ref[...], wu[:, cols]) + bu_ref[:, cols]
        d_act = dot_nt(dy_ref[...], wd[cols, :])
        cdf, slope = gelu_parts(up)
        low = (up * cdf).astype(BF)
        d_up = (d_act * (cdf + slope)).astype(BF)
        act[:, cols] = low
        act_t[cols, :] = low.T
        dup[:, cols] = d_up
        gub[:, cols] = jnp.sum(d_up.astype(F32), axis=0, keepdims=True)
        for owner in range(n):
            put_chunk(grads, ch % SLOTS, a, owner, sub, dot(rows_of(h2t, owner), d_up), (0, 1, 2, 3))
        ring.start(0, ch)
        ring.tick(ch)
        return 0

    lax.fori_loop(0, hidden // CHUNK, feed, 0)

    def down(i, _):
        cols = pl.ds(pl.multiple_of(i * 256, 256), 256)
        part = dy_ref[:, cols]
        for owner in range(n):
            g = dot(act_t[owner * 4 * sub : (owner + 1) * 4 * sub, :], part)
            at = tuple(reversed(bits_of(owner, a)))
            for u in (0, 1):
                for q in range(4):
                    grads[((9 + 2 * i + u) % SLOTS,) + at + (q // 2, q % 2)] = g[
                        q * sub : (q + 1) * sub, u * 128 : (u + 1) * 128
                    ].astype(BF)
        for u in (0, 1):
            ring.start(0, 9 + 2 * i + u)
            ring.tick(9 + 2 * i + u)
        return 0

    lax.fori_loop(0, width // 256, down, 0)

    d_kv = kvr[a - 1][...].reshape(toks, 2 * HD).astype(F32)
    d_kv = d_kv * turn_ref[0] + pltpu.roll(d_kv, 2 * HD - 8, 1) * turn_ref[1] + pltpu.roll(d_kv, 8, 1) * turn_ref[2]
    d_kv = d_kv.astype(BF)
    for owner in range(n):
        own_kv[owner] = dot(rows_of(h1t, owner), d_kv).astype(BF)
    ring.tick(total)
    second_grad = dot_nt(dup[...], wu[...])
    ring.tick(total + 1)
    for load in loads[2:]:
        load.wait()
    first_grad = dot_nt(dq_ref[...], wq[...]) + dot_nt(d_kv, wkv[...])
    x = x_ref[...].astype(F32)
    centred = x - lanes_mean(x)
    factor = lax.rsqrt(lanes_mean(centred * centred) + EPS)
    xhat = centred * factor
    at = 0

    def keep(vector):
        nonlocal at
        for i in range(vector.shape[1] // 128):
            own_small[at : at + 1, :] = vector[:, i * 128 : (i + 1) * 128]
            at += 1

    def column_sum(v):
        return jnp.sum(v, axis=0, keepdims=True)

    own_small[...] = jnp.zeros(own_small.shape, F32)
    dy32 = dy_ref[...].astype(F32)
    result = dy32
    for grad, gain in ((first_grad, vec_ref[0:1, :]), (second_grad, vec_ref[1:2, :])):
        keep(column_sum(grad * xhat))
        keep(column_sum(grad))
        g = grad * gain
        result = result + factor * (g - lanes_mean(g) - xhat * lanes_mean(g * xhat))
    ig_ref[...] = result.astype(BF)
    keep(column_sum(dq_ref[...].astype(F32)))
    keep(column_sum(d_kv.astype(F32)))
    keep(column_sum(dy32))
    keep(gub[...])

    def narrow(step):
        out = []
        if step == 0:
            for m in range(1, n):
                peer = net.seq_xor(m)
                out.append(remote(own_kv.at[peer["seq"]], seq_kv.at[m - 1], m_send.at[m - 1], m_recv.at[m - 1], peer))
                out.append(remote(own_small, seq_small.at[net.me], m_send.at[n + m - 2], m_recv.at[n + m - 2], peer))
            return out
        base = 2 * (n - 1)
        count = 2**row_bits
        for m in range(1, count):
            peer = net.row_xor(m)
            k = base + 2 * (m - 1)
            out.append(remote(row_kv.at[net.row], row_kv.at[net.row], m_send.at[k], m_recv.at[k], peer))
            out.append(remote(row_small.at[net.row], row_small.at[net.row], m_send.at[k + 1], m_recv.at[k + 1], peer))
        return out

    for copy in narrow(0):
        copy.start()
    ring.tick(total + 2)
    ffn_out = dot(act[...], wd[...])
    ring.tick(total + 3)
    for copy in narrow(0):
        copy.wait()
    seq_small[net.me] = own_small[...]
    sums = own_kv[net.me].astype(F32)
    for m in range(1, n):
        sums = sums + seq_kv[m - 1].astype(F32)
    row_kv[net.row] = sums.astype(BF)
    sums = seq_small[0]
    for i in range(1, n):
        sums = sums + seq_small[i]
    row_small[net.row] = sums
    for copy in narrow(1):
        copy.start()
    ring.tick(total + 4)
    lo_ref[...] = (x + dot(mx_ref[...], wo[...]) + ffn_out + vec_ref[2:3, :]).astype(BF)
    for t in range(total + 5, total + len(ring.stages) + 1):
        ring.tick(t)
    for copy in narrow(1):
        copy.wait()
    sums, kv_sums = row_small[0], row_kv[0].astype(F32)
    for i in range(1, 2**row_bits):
        sums = sums + row_small[i]
        kv_sums = kv_sums + row_kv[i].astype(F32)
    small_ref[...] = sums
    gkv_ref[...] = kv_sums
    for q in range(4):
        def piece(ch):
            return fin[ch, q // 2, q % 2].astype(F32)

        lanes = slice(q * 128, (q + 1) * 128)
        gout_ref[:, lanes] = piece(0)
        gq_ref[:, 256 + q * 128 : 384 + q * 128] = piece(2)
        if q < 2:
            gout_ref[:, CHUNK + q * 128 : CHUNK + (q + 1) * 128] = piece(1)
        else:
            gq_ref[:, (q - 2) * 128 : (q - 1) * 128] = piece(1)
        for f in range(hidden // CHUNK):
            gup_ref[:, f * CHUNK + q * 128 : f * CHUNK + (q + 1) * 128] = piece(3 + f)
        for j in range(width // 128):
            gdown_ref[q * sub : (q + 1) * sub, j * 128 : (j + 1) * 128] = piece(3 + hidden // CHUNK + j)


def tail(net_bits, x, dy, h1, h2, mixed_t, mixed, dq, dkv, turn, vec, bu, wq, wkv, wo, wu, wd):
    a, b = net_bits
    n, count = 2**a, 2**b
    toks, width = x.shape
    hidden = wu.shape[1]
    sub = width // n
    total = 3 + hidden // CHUNK + width // 128
    rows = dkv.shape[1] * 2
    two = (2,)
    vm = pltpu.VMEM
    dma = pltpu.SemaphoreType.DMA
    n_sems = 1 + 2 * (a - 1) + b + min(b, 2)
    scratch = [
        vm(wq.shape, BF), vm(wkv.shape, BF), vm(wo.shape, BF), vm(wu.shape, BF), vm(wd.shape, BF), dma((5,)),
        vm((width, toks), BF), vm((width, toks), BF), vm((toks, hidden), BF), vm((hidden, toks), BF), vm((toks, hidden), BF),
        vm((1, hidden), F32),
        vm((SLOTS,) + two * a + (2, 2, sub, 128), BF),
        vm((RING,) + two * (a - 1) + (2, 2, sub, 128), BF),
    ]
    scratch += [vm((total, 2) + two * (a - 1 - k) + (2, sub, 128), BF) for k in range(1, a)]
    scratch += [vm((total, 2, sub, 128), BF)] + [vm((total, sub, 128), BF) for _ in range(1, b)]
    scratch += [vm((total, 2, 2, sub, 128), BF), dma((total, n_sems)), dma((total, n_sems))]
    scratch += [vm((2, rows // 2) + two * (a - 1 - k) + (BLK, 2 * HD), BF) for k in range(a)]
    scratch += [
        dma((2 * a,)), dma((2 * a,)),
        vm((n, sub, 128), BF), vm((n - 1, sub, 128), BF), vm((count, sub, 128), BF),
        vm((64, 128), F32), vm((n, 64, 128), F32), vm((count, 64, 128), F32),
        dma((2 * (n + count),)), dma((2 * (n + count),)),
    ]
    vmem = pl.BlockSpec(memory_space=pltpu.VMEM)
    hbm = pl.BlockSpec(memory_space=pl.ANY)
    shape = jax.ShapeDtypeStruct
    return pl.pallas_call(
        functools.partial(tail_kernel, a, b),
        out_shape=[
            shape((toks, width), BF), shape((toks, width), BF),
            shape((sub, hidden), F32), shape((4 * sub, width), F32), shape((sub, width), F32), shape((sub, width), F32),
            shape((sub, 2 * HD), F32), shape((64, 128), F32),
        ],
        in_specs=[vmem] * 11 + [hbm] * 5,
        out_specs=[vmem] * 8,
        scratch_shapes=scratch,
        compiler_params=pltpu.CompilerParams(collective_id=0, has_side_effects=True, vmem_limit_bytes=60 * 2**20),
        name="tail",
    )(x, dy, h1, h2, mixed_t, mixed, dq, dkv, turn, vec, bu, wq, wkv, wo, wu, wd)


def rotate_t(values, cosine, sine):
    front, behind = values[:, :, :8], values[:, :, 8:16]
    return jnp.concatenate(
        [front * cosine - behind * sine, behind * cosine + front * sine, values[:, :, 16:]], axis=2
    )


def shards(
    hidden, lengths, cotangent, first_gain, first_shift, second_gain, second_shift,
    query_weight, query_bias, keyvalue_weight, keyvalue_bias, output_weight, output_bias,
    up_weight, up_bias, down_weight, down_bias,
):
    rows, block, width = hidden.shape
    heads = width // HD
    toks = rows * block
    own = lax.axis_index("seq")
    cuts = [jnp.sum(lengths[:, : i + 1], axis=1)[:, None] for i in range(lengths.shape[1] - 1)]
    place = own * block + jnp.arange(block, dtype=jnp.int32)[None, :]
    positions = place - doc_start(place, cuts)
    freqs = jnp.power(10000.0, -2.0 * jnp.arange(ROT // 2, dtype=F32) / ROT)
    angles = positions.astype(F32)[:, None, :] * freqs[None, :, None]
    cosine, sine = jnp.cos(angles), jnp.sin(angles)

    x = hidden.astype(F32).reshape(toks, width)
    dy = cotangent.reshape(toks, width)
    dy32 = dy.astype(F32)
    centred = x - jnp.mean(x, axis=-1, keepdims=True)
    factor = lax.rsqrt(jnp.mean(centred * centred, axis=-1, keepdims=True) + EPS)
    xhat = centred * factor
    h1 = (xhat * first_gain + first_shift).astype(BF)
    h2 = (xhat * second_gain + second_shift).astype(BF)

    kv = (dot(h1, keyvalue_weight) + keyvalue_bias).reshape(rows, block, 2 * HD)
    cos_k, sin_k = cosine.swapaxes(1, 2), sine.swapaxes(1, 2)
    front, behind = kv[..., :8], kv[..., 8:16]
    kv_low = jnp.concatenate(
        [front * cos_k - behind * sin_k, behind * cos_k + front * sin_k, kv[..., 16:]], axis=-1
    ).astype(BF)
    kv_full = lax.all_gather(kv_low, "seq", axis=1, tiled=True)

    q = jnp.einsum("rtd,de->ret", h1.reshape(rows, block, width), query_weight, preferred_element_type=F32)
    q = (q + query_bias[None, :, None]).reshape(rows, heads, HD, block)
    q = (rotate_t(q, cosine[:, None], sine[:, None]).astype(BF) * 0.125).astype(BF)
    q = q.transpose(0, 2, 1, 3).reshape(rows, HD, heads * block)
    do = jnp.einsum("rtd,ed->ret", dy.reshape(rows, block, width), output_weight, preferred_element_type=F32)
    do = do.astype(BF).reshape(rows, heads, HD, block).transpose(0, 2, 1, 3).reshape(rows, HD, heads * block)

    mixed_t, mixed, dq, dkv = attention(own[None], lengths, q, do, kv_full, cosine, sine)
    seq_bits = lax.axis_size("seq").bit_length() - 1
    row_bits = lax.axis_size("rows").bit_length() - 1
    ones = jnp.ones((rows, block, 2 * HD - ROT), F32)
    zeros = jnp.zeros((rows, block, 8), F32)
    far = jnp.zeros((rows, block, 2 * HD - ROT), F32)
    turn = jnp.stack([
        jnp.concatenate([cos_k, cos_k, ones], axis=-1),
        jnp.concatenate([sin_k, zeros, far], axis=-1),
        jnp.concatenate([zeros, -sin_k, far], axis=-1),
    ]).reshape(3, toks, 2 * HD)
    vec = jnp.stack([first_gain, second_gain, output_bias + down_bias])
    layer_output, input_grad, s_up, s_down, s_out, s_query, s_kv, small = tail(
        (seq_bits, row_bits), hidden.reshape(toks, width), dy, h1, h2,
        mixed_t.swapaxes(0, 1).reshape(width, toks), mixed.reshape(toks, width), dq.reshape(toks, width),
        dkv.reshape((2, rows // 2) + (2,) * seq_bits + (block, 2 * HD)), turn, vec, up_bias[None, :],
        query_weight, keyvalue_weight, output_weight, up_weight, down_weight,
    )
    sizes = [width] * 5 + [2 * HD, width, up_weight.shape[1]]
    small = small.reshape(-1)
    pieces, at = [], 0
    for size in sizes:
        pieces.append(small[at : at + size])
        at += size
    s_fg, s_fs, s_sg, s_ss, s_qb, s_kb, s_ob, s_ub = pieces
    return (
        layer_output.reshape(hidden.shape), input_grad.reshape(hidden.shape),
        s_fg, s_fs, s_sg, s_ss, s_query, s_qb, s_kv, s_kb, s_out, s_ob, s_up, s_ub, s_down, s_ob,
    )


def solution(mesh):
    tokens = P("rows", "seq", None)
    weight = P("seq", None)
    return jax.shard_map(
        shards,
        mesh=mesh,
        in_specs=(tokens, P("rows", None), tokens) + (P(),) * 14,
        out_specs=(
            tokens, tokens, P(), P(), P(), P(), weight, P(), weight, P(), weight, P(), weight, P(), weight, P(),
        ),
        check_vma=False,
    )
```

```python
import functools

import jax
import jax.numpy as jnp
from jax import lax
from jax.experimental import pallas as pl
from jax.experimental.pallas import tpu as pltpu
from jax.sharding import PartitionSpec as P

HD = 64
ROT = 16
BLK = 128
NEG = -1e30
EPS = 1e-05
F32 = jnp.float32
BF = jnp.bfloat16
MESH = pl.DeviceIdType.MESH
CHUNK = 512
QUARTER = 128
LAG = 2
SLOTS = LAG + 1
RING = 3 * LAG + 2


def dot(a, b):
    return jnp.dot(a, b, preferred_element_type=F32)


def dot_nt(a, b):
    return lax.dot_general(a, b, (((1,), (1,)), ((), ())), preferred_element_type=F32)


def dot_tn(a, b):
    return lax.dot_general(a, b, (((0,), (0,)), ((), ())), preferred_element_type=F32)


def lanes_mean(v):
    return jnp.mean(v, axis=-1, keepdims=True)


def column_sum(v):
    return jnp.sum(v, axis=0, keepdims=True)


def doc_start(place, cuts):
    begin = jnp.where(place >= cuts[0], cuts[0], 0)
    for cut in cuts[1:]:
        begin = jnp.where(place >= cut, cut, begin)
    return begin


def rotate(values, cosine, sine):
    front, behind = values[:8], values[8:16]
    return jnp.concatenate([front * cosine - behind * sine, behind * cosine + front * sine, values[16:]], axis=0)


def gelu_parts(up):
    cdf = 0.5 + 0.5 * lax.erf(up * 0.7071067811865476)
    pdf = jnp.exp(-0.5 * up * up) * 0.3989422804014327
    return cdf, up * pdf


def bits_of(value, count):
    return [value // 2**i % 2 for i in range(count)]


def remote(src, dst, send_sem, recv_sem, peer):
    return pltpu.make_async_remote_copy(
        src_ref=src, dst_ref=dst, send_sem=send_sem, recv_sem=recv_sem, device_id=peer, device_id_type=MESH
    )


class Net:
    def __init__(self, seq_bits, row_bits):
        self.a, self.b = seq_bits, row_bits
        self.me, self.row = lax.axis_index("seq"), lax.axis_index("rows")
        self.sb, self.rb = bits_of(self.me, seq_bits), bits_of(self.row, row_bits)

    def seq_xor(self, mask):
        out = self.me
        for i in range(self.a):
            if mask >> i & 1:
                out = out + (1 - 2 * self.sb[i]) * 2**i
        return {"seq": out}

    def row_xor(self, mask):
        out = self.row
        for i in range(self.b):
            if mask >> i & 1:
                out = out + (1 - 2 * self.rb[i]) * 2**i
        return {"rows": out}

    def peers(self):
        return [self.seq_xor(m) for m in range(1, 2**self.a)] + [self.row_xor(m) for m in range(1, 2**self.b)]

    def pick(self, left, bit, mine):
        own = self.sb[bit]
        return tuple((own if mine else 1 - own) if i == bit else slice(None) for i in left)


class Ring:
    def __init__(self, net, early, late, grads, recs, recz, fin, send_sem, recv_sem):
        self.net, self.early, self.late = net, early, late
        self.grads, self.recs, self.recz, self.fin = grads, recs, recz, fin
        self.send_sem, self.recv_sem = send_sem, recv_sem
        a, b = net.a, net.b
        self.halves = min(b, 2)
        self.stages = [("first", 0)] + [("seq", k) for k in range(1, a)]
        self.stages += [("split", i) for i in range(self.halves)]
        self.stages += [("whole", i) for i in range(2, b)]
        self.stages += [("back", i) for i in reversed(range(self.halves))]
        self.sem_at, n = [], 0
        for kind, _ in self.stages:
            self.sem_at.append(n)
            n += 2 if kind == "seq" else 1

    def place(self, ch):
        if isinstance(ch, int) and ch in self.late:
            return self.early + self.late.index(ch)
        return ch

    def slot(self, ch):
        if isinstance(ch, int) and ch in self.late:
            return RING + self.late.index(ch)
        return ch % RING

    def moves(self, stage, ch):
        net, a = self.net, self.net.a
        kind, k = self.stages[stage]
        at = (self.slot(ch),)
        if kind == "first":
            left = range(a - 1, -1, -1)
            slot = (ch % SLOTS,)
            return [(self.grads.at[slot + net.pick(left, 0, False)], self.recs[0].at[at], net.seq_xor(1),
                     (self.grads, slot + net.pick(left, 0, True)), (self.recs[0], at))]
        if kind == "seq":
            out = []
            prev, here = self.recs[k - 1], self.recs[k]
            for half in (0, 1):
                if half == 0:
                    bit, left = k, range(a - 1, k - 1, -1)
                else:
                    bit, left = a - k, range(a - k, 0, -1)
                base, tail = (at, (half,)) if k == 1 else (at + (half,), ())
                out.append((prev.at[base + net.pick(left, bit, False) + tail], here.at[at + (half,)],
                            net.seq_xor(1 << bit), (prev, base + net.pick(left, bit, True) + tail), (here, at + (half,))))
            return out
        if kind == "split":
            prev = self.recs[a - 1] if k == 0 else self.recz[k - 1]
            return [(prev.at[at + (1 - net.rb[k],)], self.recz[k].at[at], net.row_xor(1 << k),
                     (prev, at + (net.rb[k],)), (self.recz[k], at))]
        if kind == "whole":
            prev = self.recz[k - 1]
            return [(prev.at[at], self.recz[k].at[at], net.row_xor(1 << k), (prev, at), (self.recz[k], at))]
        at = (self.place(ch),) + tuple(net.rb[: k + 1])
        return [(self.fin.at[at], self.fin.at[at], net.row_xor(1 << k), None, None)]

    def copies(self, stage, ch):
        out = []
        at = self.place(ch)
        for i, (src, dst, peer, _, _) in enumerate(self.moves(stage, ch)):
            sem = self.sem_at[stage] + i
            out.append(remote(src, dst, self.send_sem.at[at, sem], self.recv_sem.at[at, sem], peer))
        return out

    def start(self, stage, ch):
        for copy in self.copies(stage, ch):
            copy.start()

    def finish(self, stage, ch):
        for copy in self.copies(stage, ch):
            copy.wait()
        kind, _ = self.stages[stage]
        if kind != "back":
            last = self.stages[stage + 1][0] == "back"
            for _, _, _, (src, src_at), (dst, dst_at) in self.moves(stage, ch):
                total = src[src_at] + dst[dst_at]
                if last:
                    self.fin[(self.place(ch),) + tuple(self.net.rb[: self.halves])] = total
                else:
                    dst[dst_at] = total
        if stage + 1 < len(self.stages):
            self.start(stage + 1, ch)

    def tick(self, t):
        for stage in reversed(range(len(self.stages))):
            ch = t - LAG * (stage + 1)
            if isinstance(ch, int):
                if 0 <= ch < self.early or ch in self.late:
                    self.finish(stage, ch)
            else:

                @pl.when((ch >= 0) & (ch < self.early))
                def _():
                    self.finish(stage, ch)

    def last_tick(self):
        return max(self.late) + LAG * len(self.stages)


def layer_kernel(
    seq_bits, row_bits, late,
    len_ref, x_ref, dy_ref, fg_ref, fs_ref, sg_ref, ss_ref, bq_ref, bo_ref, bd_ref, bkv_ref, bu_ref, wq_hbm, wkv_hbm, wo_hbm, wu_hbm, wd_hbm,
    lo_ref, ig_ref, fin, small_ref,
    wq, wkv, wo, wu, wd, load_sem, vec_ref, wide_ref,
    h1, h2, act, act_t, dup, gub, q_all, do_all, cs, kv_all, kv_send, kv_recv,
    s_ref, e_ref, qz, dz, m_ref, l_ref, o_ref, dqa, mt, mx, dq, dkv, dkv_in, dkv_sum, dkv_send, dkv_recv,
    grads, *rest,
):
    a, n, count = seq_bits, 2**seq_bits, 2**row_bits
    recs, rest = rest[:a], rest[a:]
    recz, rest = rest[:row_bits], rest[row_bits:]
    send_sem, recv_sem, own_small, seq_small, row_small, m_send, m_recv = rest
    toks, width = x_ref.shape
    hidden = wu.shape[1]
    sub = width // n
    heads = width // HD
    lanes = s_ref.shape[-1]
    groups = heads * BLK // lanes
    near = lanes // BLK
    rows = toks // BLK
    n_up, n_down = hidden // CHUNK, width // QUARTER
    net = Net(seq_bits, row_bits)
    me = net.me
    ring = Ring(net, n_up + n_down, late, grads, recs, recz, fin, send_sem, recv_sem)

    barrier = pltpu.get_barrier_semaphore()
    for peer in net.peers():
        pl.semaphore_signal(barrier, inc=1, device_id=peer, device_id_type=MESH)
    loads = {}
    for i, (name, src, dst) in enumerate(
        (("kv", wkv_hbm, wkv), ("q", wq_hbm, wq), ("o", wo_hbm, wo), ("u", wu_hbm, wu), ("d", wd_hbm, wd))
    ):
        loads[name] = pltpu.make_async_copy(src, dst, load_sem.at[i])
        loads[name].start()

    for i, ref in enumerate((fg_ref, fs_ref, sg_ref, ss_ref, bq_ref)):
        vec_ref[i : i + 1, :] = ref[...].reshape(1, width)
    vec_ref[5:6, :] = (bo_ref[...] + bd_ref[...]).reshape(1, width)
    wide_ref[...] = bu_ref[...].reshape(1, hidden)

    def put_chunk(ch, owner, value, quarters):
        at = (ch % SLOTS,) + tuple(reversed(bits_of(owner, a)))
        for i, q in enumerate(quarters):
            grads[at + (q // 2, q % 2)] = value[:, i * QUARTER : (i + 1) * QUARTER].astype(BF)

    def part(owner):
        return slice(owner * sub, (owner + 1) * sub)

    def row_cuts(r):
        cuts = []
        for i in range(len_ref.shape[1] - 1):
            cuts.append(len_ref[r, i] + (cuts[-1] if cuts else 0))
        return cuts

    place = me * BLK + lax.broadcasted_iota(jnp.int32, (8, BLK), 1)
    which = lax.broadcasted_iota(jnp.int32, (8, BLK), 0)
    freqs = jnp.ones((8, BLK), F32)
    for i in range(1, 8):
        freqs = jnp.where(which == i, 10000.0 ** (-2.0 * i / ROT), freqs)
    for r in range(rows):
        angles = (place - doc_start(place, row_cuts(r))).astype(F32) * freqs
        cs[r, 0] = jnp.cos(angles)
        cs[r, 1] = jnp.sin(angles)

    def row_span(r):
        return pl.ds(pl.multiple_of(r * BLK, BLK), BLK)

    def normalized(r):
        x = x_ref[row_span(r), :].astype(F32)
        centred = x - lanes_mean(x)
        factor = lax.rsqrt(lanes_mean(centred * centred) + EPS)
        return x, centred * factor, factor

    def norms(r, _):
        xhat = normalized(r)[1]
        h1[row_span(r), :] = (xhat * vec_ref[0:1, :] + vec_ref[1:2, :]).astype(BF)
        h2[row_span(r), :] = (xhat * vec_ref[2:3, :] + vec_ref[3:4, :]).astype(BF)
        return 0

    lax.fori_loop(0, rows, norms, 0)

    per_block = lanes // width

    def spare(k, r, cols=None):
        cols = slice(0, width) if cols is None else cols
        at = k % per_block * width
        return k // per_block * rows + r, slice(None), slice(at + cols.start, at + cols.stop)

    def by_rows(k, value):
        for r in range(rows):
            s_ref[spare(k, r)] = value[r * BLK : (r + 1) * BLK]

    loads["kv"].wait()
    kv = dot(h1[...], wkv[...]) + bkv_ref[...].reshape(1, 2 * HD)
    group = rows // 2

    def at_bits(value):
        return tuple(reversed(bits_of(value, a)))

    def kv_at(j, r):
        return at_bits(j) + (r // group, r % group)

    for r in range(rows):
        turned = rotate(kv[r * BLK : (r + 1) * BLK].T, cs[r, 0], cs[r, 1])
        kv_all[kv_at(me, r)] = turned.T.astype(BF)
    pl.semaphore_wait(barrier, n + count - 2)

    def kv_copies(k):
        out = []
        for half in (0, 1):
            order = list(range(1, a)) if half == 0 else list(range(a - 1, 0, -1))
            order.append(0)
            at = tuple(slice(None) if i in order[:k] else net.sb[i] for i in reversed(range(a))) + (half,)
            sem = 2 * k + half
            out.append(remote(kv_all.at[at], kv_all.at[at], kv_send.at[sem], kv_recv.at[sem], net.seq_xor(1 << order[k])))
        return out

    def kv_step(k):
        if k > 0:
            for copy in kv_copies(k - 1):
                copy.wait()
        if k < a:
            for copy in kv_copies(k):
                copy.start()

    kv_step(0)

    loads["q"].wait()
    by_rows(0, dot(h1[...], wq[...]) + vec_ref[4:5, :])
    loads["o"].wait()
    by_rows(1, dot_nt(dy_ref[...], wo[...]))
    kv_step(1)

    def heads_apart(r, _):
        for h in range(0, heads, 2):
            pair = s_ref[spare(0, r, slice(h * HD, (h + 2) * HD))].T
            d_pair = s_ref[spare(1, r, slice(h * HD, (h + 2) * HD))].T.astype(BF)
            for i in (0, 1):
                span = slice((h + i) * BLK, (h + i + 1) * BLK)
                turned = rotate(pair[i * HD : (i + 1) * HD], cs[r, 0], cs[r, 1]).astype(BF).astype(F32)
                q_all[r, :, span] = (turned * 0.125).astype(BF)
                do_all[r, :, span] = d_pair[i * HD : (i + 1) * HD]
        return 0

    lax.fori_loop(0, rows, heads_apart, 0)
    kv_step(2)
    loads["u"].wait()
    loads["d"].wait()

    def feed(f):
        cols = pl.ds(pl.multiple_of(f * CHUNK, CHUNK), CHUNK)
        up = dot(h2[...], wu[:, cols]) + wide_ref[:, cols]
        d_act = dot_nt(dy_ref[...], wd[cols, :])
        cdf, slope = gelu_parts(up)
        low = (up * cdf).astype(BF)
        d_up = (d_act * (cdf + slope)).astype(BF)
        act[:, cols] = low
        act_t[cols, :] = low.T
        dup[:, cols] = d_up
        gub[:, cols] = column_sum(d_up.astype(F32))
        g = dot_tn(h2[...], d_up)
        for owner in range(n):
            put_chunk(f, owner, g[part(owner)], range(4))

    def down(j):
        cols = dy_ref[:, pl.ds(pl.multiple_of(j * QUARTER, QUARTER), QUARTER)]
        for owner in range(n):
            g = dot(act_t[owner * 4 * sub : (owner + 1) * 4 * sub, :], cols).astype(BF)
            at = ((n_up + j) % SLOTS,) + at_bits(owner)
            for i in range(4):
                grads[at + (i // 2, i % 2)] = g[i * sub : (i + 1) * sub]

    n_pre = n_up + n_down - 3 * (rows - 1)

    def feed_step(t, _):
        feed(t)
        ring.start(0, t)
        ring.tick(t)
        return 0

    lax.fori_loop(0, n_pre, feed_step, 0)
    for k in range(3, a + 1):
        kv_step(k)

    key_iota = lax.broadcasted_iota(jnp.int32, (BLK, BLK), 0)
    query_place = me * BLK + lax.broadcasted_iota(jnp.int32, (BLK, BLK), 1)

    def scores_pass(r, g):
        span = slice(g * lanes, (g + 1) * lanes)
        qz[:HD, :] = q_all[r, :, span]
        qz[HD:, :] = jnp.zeros((HD, lanes), BF)
        dz[HD:, :] = do_all[r, :, span]
        dz[:HD, :] = jnp.zeros((HD, lanes), BF)
        m_ref[...] = jnp.full(m_ref.shape, NEG, F32)
        l_ref[...] = jnp.zeros(l_ref.shape, F32)
        o_ref[...] = jnp.zeros(o_ref.shape, F32)
        dqa[...] = jnp.zeros(dqa.shape, F32)
        begin = doc_start(query_place, row_cuts(r))

        def body(j, _):
            keys = j * BLK + key_iota
            bias = jnp.where((keys <= query_place) & (keys >= begin), 0.0, NEG)
            s = dot(kv_all[kv_at(j, r)], qz[...]) + jnp.concatenate([bias] * near, axis=1)
            s_ref[j] = s
            m_ref[...] = jnp.maximum(m_ref[...], jnp.max(s.reshape(BLK // 8, 8, lanes), axis=0))
            return 0

        lax.fori_loop(0, me + 1, body, 0)
        m_ref[0:1, :] = jnp.max(m_ref[...], axis=0, keepdims=True)

    def mix_pass(r, g):
        def body(j, _):
            v_t = kv_all[kv_at(j, r)].T[HD:]
            e = jnp.exp(s_ref[j] - m_ref[0:1, :])
            l_ref[...] += jnp.sum(e.reshape(BLK // 8, 8, lanes), axis=0)
            e_low = e.astype(BF)
            e_ref[j] = e_low
            o_ref[...] += dot(v_t, e_low)
            return 0

        lax.fori_loop(0, me + 1, body, 0)
        inv = 1.0 / jnp.sum(l_ref[...], axis=0, keepdims=True)
        o = o_ref[...] * inv
        l_ref[0:1, :] = inv
        m_ref[0:1, :] = jnp.sum(o * dz[HD:, :].astype(F32), axis=0, keepdims=True)
        span = row_span(r)
        for h in range(0, near, 2):
            pair = jnp.concatenate(
                [o[:, h * BLK : (h + 1) * BLK], o[:, (h + 1) * BLK : (h + 2) * BLK]], axis=0
            )
            at = slice((g * near + h) * HD, (g * near + h + 2) * HD)
            mt[at, span] = pair.astype(BF)
            mx[span, at] = pair.T.astype(BF)

    def back_pass(r, g, start, stop):
        def body(j, _):
            kv = kv_all[kv_at(j, r)]
            k_t = kv.T[:HD]
            dp = dot(kv, dz[...])
            p = e_ref[j].astype(F32) * l_ref[0:1, :]
            ds = (p * (dp - m_ref[0:1, :])).astype(BF)
            total = dot_nt(ds, qz[...]) + dot_nt(p.astype(BF), dz[...])
            if g > 0:
                total = total + dkv[j, r].astype(F32)
            dkv[j, r] = total.astype(BF)
            dqa[...] += dot(k_t, ds)
            return 0

        lax.fori_loop(start, stop, body, 0)

    def dkv_copies(r):
        out = []
        for m in range(1, n):
            peer = net.seq_xor(m)
            out.append((peer["seq"], remote(
                dkv.at[peer["seq"], r], dkv_in.at[m - 1, r], dkv_send.at[m - 1, r], dkv_recv.at[m - 1, r], peer)))
        return out

    def leave_pass(r, g):
        if g == groups - 1:
            for other, copy in dkv_copies(r):

                @pl.when(other < me)
                def _():
                    copy.start()

        cosine, sine = cs[r, 0], cs[r, 1]
        span = row_span(r)
        for h in range(0, near, 2):
            pair = jnp.concatenate(
                [rotate(dqa[:, i * BLK : (i + 1) * BLK], cosine, -sine) for i in (h, h + 1)], axis=0
            )
            dq[span, (g * near + h) * HD : (g * near + h + 2) * HD] = (pair * 0.125).T.astype(BF)

    def first_groups(r):
        for g in range(groups - 1):
            scores_pass(r, g)
            mix_pass(r, g)
            back_pass(r, g, 0, me + 1)
            leave_pass(r, g)

    def chunk_step(t):
        @pl.when(t < n_up)
        def _():
            feed(t)

        @pl.when(t >= n_up)
        def _():
            down(t - n_up)

        ring.start(0, t)
        ring.tick(t)

    def row_step(r, _):
        t = n_pre + 3 * r
        first_groups(r)
        scores_pass(r, groups - 1)
        chunk_step(t)
        mix_pass(r, groups - 1)
        chunk_step(t + 1)
        back_pass(r, groups - 1, 0, me + 1)
        leave_pass(r, groups - 1)
        chunk_step(t + 2)
        return 0

    lax.fori_loop(0, rows - 1, row_step, 0)
    r, t = rows - 1, n_up + n_down
    first_groups(r)
    scores_pass(r, groups - 1)
    ring.tick(t)
    mix_pass(r, groups - 1)
    g = dot(mt[...], dy_ref[:, :CHUNK])
    for owner in range(n):
        put_chunk(late[0], owner, g[part(owner)], range(4))
    ring.start(0, late[0])
    ring.tick(late[0])
    g = dot(mt[...], dy_ref[:, CHUNK:])
    for owner in range(n):
        put_chunk(late[1], owner, g[part(owner)], range(2))
    ring.start(0, late[1])
    ring.tick(late[1])
    back_pass(r, groups - 1, 0, (me + 1) // 2)
    ring.tick(late[1] + 1)
    back_pass(r, groups - 1, (me + 1) // 2, me + 1)
    leave_pass(r, groups - 1)
    ring.tick(late[1] + 2)
    g = dot_tn(h1[...], dq[:, :CHUNK])
    for owner in range(n):
        put_chunk(late[2], owner, g[part(owner)], range(4))
    ring.start(0, late[2])
    ring.tick(late[2])
    g = dot_tn(h1[...], dq[:, CHUNK:])
    for owner in range(n):
        put_chunk(late[3], owner, g[part(owner)], range(2))
    by_rows(0, dot_nt(dup[...], wu[...]))

    dkv_sum[...] = dkv[me].astype(F32)
    for r in range(rows):
        for m, (other, copy) in enumerate(dkv_copies(r)):

            @pl.when(other < me)
            def _():
                copy.wait_send()

            @pl.when(other > me)
            def _():
                copy.wait_recv()
                dkv_sum[r] += dkv_in[m, r].astype(F32)

    d_kv = jnp.concatenate(
        [rotate(dkv_sum[r].T, cs[r, 0], -cs[r, 1]).T.astype(BF) for r in range(rows)], axis=0
    )
    g = dot_tn(h1[...], d_kv)
    for owner in range(n):
        put_chunk(late[3], owner, g[part(owner)], (2,))
        put_chunk(late[3], owner, jnp.zeros((sub, QUARTER), F32), (3,))
    ring.start(0, late[3])
    ring.tick(late[3])

    by_rows(1, dot_nt(dq[...], wq[...]) + dot_nt(d_kv, wkv[...]))
    own_small[...] = jnp.zeros(own_small.shape, F32)
    per = width // 128

    def add_small(at, vector):
        for i in range(vector.shape[1] // 128):
            own_small[at + i : at + i + 1, :] += vector[:, i * 128 : (i + 1) * 128]

    def norms_back(r, _):
        _, xhat, factor = normalized(r)
        dy32 = dy_ref[row_span(r), :].astype(F32)
        result = dy32
        for k, gain in enumerate((vec_ref[0:1, :], vec_ref[2:3, :])):
            grad = s_ref[spare(1 - k, r)]
            add_small(2 * k * per, column_sum(grad * xhat))
            add_small((2 * k + 1) * per, column_sum(grad))
            g = grad * gain
            result = result + factor * (g - lanes_mean(g) - xhat * lanes_mean(g * xhat))
        h2[row_span(r), :] = result.astype(BF)
        add_small(4 * per, column_sum(dq[row_span(r), :].astype(F32)))
        add_small(5 * per + 1, column_sum(dy32))
        return 0

    lax.fori_loop(0, rows, norms_back, 0)
    ig_copy = pltpu.make_async_copy(h2, ig_ref, load_sem.at[5])
    ig_copy.start()
    add_small(5 * per, column_sum(d_kv.astype(F32)))
    add_small(6 * per + 1, gub[...])

    def narrow(step):
        if step == 0:
            return [
                remote(own_small, seq_small.at[me], m_send.at[m - 1], m_recv.at[m - 1], net.seq_xor(m)) for m in range(1, n)
            ]
        spot = row_small.at[net.row]
        return [
            remote(spot, spot, m_send.at[n + m - 2], m_recv.at[n + m - 2], net.row_xor(m)) for m in range(1, count)
        ]

    for copy in narrow(0):
        copy.start()
    ring.tick(late[3] + 1)
    by_rows(2, dot(act[...], wd[...]) + vec_ref[5:6, :])
    ring.tick(late[3] + 2)
    for copy in narrow(0):
        copy.wait()
    seq_small[me] = own_small[...]
    sums = seq_small[0]
    for i in range(1, n):
        sums = sums + seq_small[i]
    row_small[net.row] = sums
    for copy in narrow(1):
        copy.start()
    ring.tick(late[3] + 3)
    by_rows(3, dot(mx[...], wo[...]))

    def layer_out(r, _):
        total = x_ref[row_span(r), :].astype(F32) + s_ref[spare(2, r)] + s_ref[spare(3, r)]
        h1[row_span(r), :] = total.astype(BF)
        return 0

    lax.fori_loop(0, rows, layer_out, 0)
    lo_copy = pltpu.make_async_copy(h1, lo_ref, load_sem.at[6])
    lo_copy.start()
    for t in range(late[3] + 4, ring.last_tick() + 1):
        ring.tick(t)
    for copy in narrow(1):
        copy.wait()
    sums = row_small[0]
    for i in range(1, count):
        sums = sums + row_small[i]
    small_ref[...] = sums
    ig_copy.wait()
    lo_copy.wait()


def layer(net_bits, lengths, x, dy, vectors, wq, wkv, wo, wu, wd):
    a, b = net_bits
    n, count = 2**a, 2**b
    toks, width = x.shape
    hidden = wu.shape[1]
    sub = width // n
    rows = toks // BLK
    all_lanes = width // HD * BLK
    lanes = all_lanes // max(1, n // 8)
    n_up, n_down = hidden // CHUNK, width // QUARTER
    last_row = n_up + n_down
    late = [last_row + 1, last_row + 2, last_row + 5, last_row + 6]
    total = n_up + n_down + len(late)
    slots = RING + len(late)
    two = (2,)
    vm = pltpu.VMEM
    dma = pltpu.SemaphoreType.DMA
    n_sems = 1 + 2 * (a - 1) + b + min(b, 2)
    scratch = [
        vm(wq.shape, BF), vm(wkv.shape, BF), vm(wo.shape, BF), vm(wu.shape, BF), vm(wd.shape, BF), dma((7,)),
        vm((8, width), F32), vm((1, hidden), F32),
        vm((toks, width), BF), vm((toks, width), BF),
        vm((toks, hidden), BF), vm((hidden, toks), BF), vm((toks, hidden), BF), vm((1, hidden), F32),
        vm((rows, HD, all_lanes), BF), vm((rows, HD, all_lanes), BF), vm((rows, 2, 8, BLK), F32),
        vm(two * a + (2, rows // 2, BLK, 2 * HD), BF), dma((2 * a,)), dma((2 * a,)),
        vm((n, BLK, lanes), F32), vm((n, BLK, lanes), BF), vm((2 * HD, lanes), BF), vm((2 * HD, lanes), BF),
        vm((8, lanes), F32), vm((8, lanes), F32), vm((HD, lanes), F32), vm((HD, lanes), F32),
        vm((width, toks), BF), vm((toks, width), BF), vm((toks, width), BF),
        vm((n, rows, BLK, 2 * HD), BF), vm((n - 1, rows, BLK, 2 * HD), BF), vm((rows, BLK, 2 * HD), F32),
        dma((n - 1, rows)), dma((n - 1, rows)),
        vm((SLOTS,) + two * a + (2, 2, sub, 128), BF),
        vm((slots,) + two * (a - 1) + (2, 2, sub, 128), BF),
    ]
    scratch += [vm((slots, 2) + two * (a - 1 - k) + (2, sub, 128), BF) for k in range(1, a)]
    scratch += [vm((slots, 2, sub, 128), BF)] + [vm((slots, sub, 128), BF) for _ in range(1, b)]
    scratch += [
        dma((total, n_sems)), dma((total, n_sems)),
        vm((64, 128), F32), vm((n, 64, 128), F32), vm((count, 64, 128), F32),
        dma((n + count,)), dma((n + count,)),
    ]
    vmem = pl.BlockSpec(memory_space=pltpu.VMEM)
    hbm = pl.BlockSpec(memory_space=pl.ANY)
    shape = jax.ShapeDtypeStruct
    return pl.pallas_call(
        functools.partial(layer_kernel, a, b, late),
        out_shape=[
            shape((toks, width), BF), shape((toks, width), BF),
            shape((total, 2, 2, sub, 128), BF), shape((64, 128), F32),
        ],
        in_specs=[pl.BlockSpec(memory_space=pltpu.SMEM)] + [vmem] * (2 + len(vectors)) + [hbm] * 5,
        out_specs=[hbm, hbm, vmem, vmem],
        scratch_shapes=scratch,
        compiler_params=pltpu.CompilerParams(collective_id=0, has_side_effects=True, vmem_limit_bytes=64 * 2**20),
        name="layer",
    )(lengths, x, dy, *vectors, wq, wkv, wo, wu, wd)


def finish_kernel(n_up, sizes, lo_in, ig_in, fin_in, small_in, lo, ig, gup, gdown, gout, gq, gkv, *rest):
    vectors, (fin, small, vlo, vig, vup, vdown, vout, vq, vkv, sem) = rest[: len(sizes)], rest[len(sizes) :]
    sub, width = gout.shape
    n_down = width // QUARTER
    late = n_up + n_down

    def move(i, src, dst):
        copy = pltpu.make_async_copy(src, dst, sem.at[i])
        copy.start()
        return copy

    loads = [move(0, fin_in, fin), move(1, small_in, small)]
    loads += [move(2, lo_in, vlo), move(3, ig_in, vig)]
    for load in loads:
        load.wait()
    moves = [move(9, vlo, lo), move(10, vig, ig)]

    def piece(ch, q):
        return fin[ch, q // 2, q % 2].astype(F32)

    def span(at, q):
        return slice(at + q * QUARTER, at + (q + 1) * QUARTER)

    for q in range(4):
        for f in range(n_up):
            vup[:, span(f * CHUNK, q)] = piece(f, q)
    moves.append(move(4, vup, gup))
    for q in range(4):
        for j in range(n_down):
            vdown[q * sub : (q + 1) * sub, j * QUARTER : (j + 1) * QUARTER] = piece(n_up + j, q)
    moves.append(move(5, vdown, gdown))
    for q in range(4):
        vout[:, span(0, q)] = piece(late, q)
        vq[:, span(0, q)] = piece(late + 2, q)
        if q < 2:
            vout[:, span(CHUNK, q)] = piece(late + 1, q)
            vq[:, span(CHUNK, q)] = piece(late + 3, q)
    vkv[...] = piece(late + 3, 2)
    moves += [move(6, vout, gout), move(7, vq, gq), move(8, vkv, gkv)]
    at = 0
    for size, ref in zip(sizes[:-1], vectors):
        for i in range(size // 128):
            ref[i * 128 : (i + 1) * 128] = small[at + i, :]
        at += size // 128
    vectors[-1][...] = vectors[-3][...]
    for copy in moves:
        copy.wait()


def finish(lo, ig, fin, small, sub, width, hidden):
    sizes = [width] * 5 + [2 * HD, width, hidden, width]
    shape = jax.ShapeDtypeStruct
    hbm = pl.BlockSpec(memory_space=pl.ANY)
    grads = [(sub, hidden), (4 * sub, width), (sub, width), (sub, width), (sub, 2 * HD)]
    return pl.pallas_call(
        functools.partial(finish_kernel, hidden // CHUNK, sizes),
        out_shape=[shape(lo.shape, BF), shape(ig.shape, BF)]
        + [shape(g, F32) for g in grads] + [shape((size,), F32) for size in sizes],
        in_specs=[hbm] * 4,
        out_specs=[hbm] * 7 + [pl.BlockSpec(memory_space=pltpu.VMEM)] * len(sizes),
        scratch_shapes=[pltpu.VMEM(fin.shape, BF), pltpu.VMEM(small.shape, F32), pltpu.VMEM(lo.shape, BF), pltpu.VMEM(ig.shape, BF)]
        + [pltpu.VMEM(g, F32) for g in grads] + [pltpu.SemaphoreType.DMA((11,))],
        compiler_params=pltpu.CompilerParams(vmem_limit_bytes=64 * 2**20),
        name="finish",
    )(lo, ig, fin, small)


def shards(
    hidden, lengths, cotangent, first_gain, first_shift, second_gain, second_shift,
    query_weight, query_bias, keyvalue_weight, keyvalue_bias, output_weight, output_bias,
    up_weight, up_bias, down_weight, down_bias,
):
    rows, block, width = hidden.shape
    toks = rows * block
    n, count = lax.axis_size("seq"), lax.axis_size("rows")
    vectors = (
        first_gain, first_shift, second_gain, second_shift, query_bias, output_bias, down_bias, keyvalue_bias, up_bias,
    )
    lo, ig, fin, small = layer(
        (n.bit_length() - 1, count.bit_length() - 1), lengths,
        hidden.reshape(toks, width), cotangent.reshape(toks, width), vectors,
        query_weight, keyvalue_weight, output_weight, up_weight, down_weight,
    )
    lo, ig, g_up, g_down, g_out, g_q, g_kv, *sums = finish(lo, ig, fin, small, width // n, width, up_weight.shape[1])
    s_fg, s_fs, s_sg, s_ss, s_qb, s_kb, s_ob, s_ub, s_db = sums
    return (
        lo.reshape(hidden.shape), ig.reshape(hidden.shape),
        s_fg, s_fs, s_sg, s_ss, g_q, s_qb, g_kv, s_kb, g_out, s_ob, g_up, s_ub, g_down, s_db,
    )


def solution(mesh):
    tokens = P("rows", "seq", None)
    weight = P("seq", None)
    return jax.shard_map(
        shards,
        mesh=mesh,
        in_specs=(tokens, P("rows", None), tokens) + (P(),) * 14,
        out_specs=(
            tokens, tokens, P(), P(), P(), P(), weight, P(), weight, P(), weight, P(), weight, P(), weight, P(),
        ),
        check_vma=False,
    )
```

```python
import functools

import jax
import jax.numpy as jnp
from jax import lax
from jax.experimental import pallas as pl
from jax.experimental.pallas import tpu as pltpu
from jax.sharding import PartitionSpec as P

HD = 64
PAIR = 4
ROT = 16
BLK = 128
NEG = -1e30
EPS = 1e-05
F32 = jnp.float32
BF = jnp.bfloat16
MESH = pl.DeviceIdType.MESH
CHUNK = 512
QUARTER = 128
LAG = 2
SLOTS = LAG + 1
RING = 3 * LAG + 2


def dot(a, b):
    return jnp.dot(a, b, preferred_element_type=F32)


def dot_nt(a, b):
    return lax.dot_general(a, b, (((1,), (1,)), ((), ())), preferred_element_type=F32)


def dot_tn(a, b):
    return lax.dot_general(a, b, (((0,), (0,)), ((), ())), preferred_element_type=F32)


def lanes_mean(v):
    return jnp.mean(v, axis=-1, keepdims=True)


def column_sum(v):
    return jnp.sum(v, axis=0, keepdims=True)


def doc_start(place, cuts):
    begin = jnp.where(place >= cuts[0], cuts[0], 0)
    for cut in cuts[1:]:
        begin = jnp.where(place >= cut, cut, begin)
    return begin


def rotate(values, cosine, sine):
    front, behind = values[:8], values[8:16]
    return jnp.concatenate([front * cosine - behind * sine, behind * cosine + front * sine, values[16:]], axis=0)


def gelu_parts(up):
    cdf = 0.5 + 0.5 * lax.erf(up * 0.7071067811865476)
    pdf = jnp.exp(-0.5 * up * up) * 0.3989422804014327
    return cdf, up * pdf


def bits_of(value, count):
    return [value // 2**i % 2 for i in range(count)]


def remote(src, dst, send_sem, recv_sem, peer):
    return pltpu.make_async_remote_copy(
        src_ref=src, dst_ref=dst, send_sem=send_sem, recv_sem=recv_sem, device_id=peer, device_id_type=MESH
    )


class Net:
    def __init__(self, seq_bits, row_bits):
        self.a, self.b = seq_bits, row_bits
        self.me, self.row = lax.axis_index("seq"), lax.axis_index("rows")
        self.sb, self.rb = bits_of(self.me, seq_bits), bits_of(self.row, row_bits)

    def seq_xor(self, mask):
        out = self.me
        for i in range(self.a):
            if mask >> i & 1:
                out = out + (1 - 2 * self.sb[i]) * 2**i
        return {"seq": out}

    def row_xor(self, mask):
        out = self.row
        for i in range(self.b):
            if mask >> i & 1:
                out = out + (1 - 2 * self.rb[i]) * 2**i
        return {"rows": out}

    def peers(self):
        return [self.seq_xor(m) for m in range(1, 2**self.a)] + [self.row_xor(m) for m in range(1, 2**self.b)]

    def pick(self, left, bit, mine):
        own = self.sb[bit]
        return tuple((own if mine else 1 - own) if i == bit else slice(None) for i in left)


class Ring:
    def __init__(self, net, early, grads, recs, recz, fin, send_sem, recv_sem):
        self.net, self.early = net, early
        self.grads, self.recs, self.recz, self.fin = grads, recs, recz, fin
        self.send_sem, self.recv_sem = send_sem, recv_sem
        a, b = net.a, net.b
        self.halves = min(b, 2)
        self.stages = [("first", 0)] + [("seq", k) for k in range(1, a)]
        self.stages += [("split", i) for i in range(self.halves)]
        self.stages += [("whole", i) for i in range(2, b)]
        self.stages += [("back", i) for i in reversed(range(self.halves))]
        self.sem_at, n = [], 0
        for kind, _ in self.stages:
            self.sem_at.append(n)
            n += 2 if kind == "seq" else 1

    def moves(self, stage, ch):
        net, a = self.net, self.net.a
        kind, k = self.stages[stage]
        at = (ch % RING,)
        if kind == "first":
            left = range(a - 1, -1, -1)
            slot = (ch % SLOTS,)
            return [(self.grads.at[slot + net.pick(left, 0, False)], self.recs[0].at[at], net.seq_xor(1),
                     (self.grads, slot + net.pick(left, 0, True)), (self.recs[0], at))]
        if kind == "seq":
            out = []
            prev, here = self.recs[k - 1], self.recs[k]
            for half in (0, 1):
                if half == 0:
                    bit, left = k, range(a - 1, k - 1, -1)
                else:
                    bit, left = a - k, range(a - k, 0, -1)
                base, tail = (at, (half,)) if k == 1 else (at + (half,), ())
                out.append((prev.at[base + net.pick(left, bit, False) + tail], here.at[at + (half,)],
                            net.seq_xor(1 << bit), (prev, base + net.pick(left, bit, True) + tail), (here, at + (half,))))
            return out
        if kind == "split":
            prev = self.recs[a - 1] if k == 0 else self.recz[k - 1]
            return [(prev.at[at + (1 - net.rb[k],)], self.recz[k].at[at], net.row_xor(1 << k),
                     (prev, at + (net.rb[k],)), (self.recz[k], at))]
        if kind == "whole":
            prev = self.recz[k - 1]
            return [(prev.at[at], self.recz[k].at[at], net.row_xor(1 << k), (prev, at), (self.recz[k], at))]
        at = (ch,) + tuple(net.rb[: k + 1])
        return [(self.fin.at[at], self.fin.at[at], net.row_xor(1 << k), None, None)]

    def copies(self, stage, ch):
        out = []
        for i, (src, dst, peer, _, _) in enumerate(self.moves(stage, ch)):
            sem = self.sem_at[stage] + i
            out.append(remote(src, dst, self.send_sem.at[ch, sem], self.recv_sem.at[ch, sem], peer))
        return out

    def start(self, stage, ch):
        for copy in self.copies(stage, ch):
            copy.start()

    def finish(self, stage, ch):
        for copy in self.copies(stage, ch):
            copy.wait()
        kind, _ = self.stages[stage]
        if kind != "back":
            last = self.stages[stage + 1][0] == "back"
            for _, _, _, (src, src_at), (dst, dst_at) in self.moves(stage, ch):
                total = src[src_at] + dst[dst_at]
                if last:
                    self.fin[(ch,) + tuple(self.net.rb[: self.halves])] = total
                else:
                    dst[dst_at] = total
        if stage + 1 < len(self.stages):
            self.start(stage + 1, ch)

    def tick(self, t):
        for stage in reversed(range(len(self.stages))):
            ch = t - LAG * (stage + 1)
            if isinstance(ch, int):
                if 0 <= ch < self.early:
                    self.finish(stage, ch)
            else:

                @pl.when((ch >= 0) & (ch < self.early))
                def _():
                    self.finish(stage, ch)

    def last_tick(self):
        return self.early - 1 + LAG * len(self.stages)


class Late:
    def __init__(self, net, first, grads, pair, wide, part, quarter, cross, fin, send_sem, recv_sem):
        self.net, self.first, self.fin = net, first, fin
        self.grads, self.pair, self.wide, self.part = grads, pair, wide, part
        self.quarter, self.cross = quarter, cross
        self.send_sem, self.recv_sem = send_sem, recv_sem
        self.low = min(net.b, 2)
        self.stages = ["core", "chips", "split"] + (["cross"] if net.b > 2 else []) + ["back"]

    def copies(self, c, kind):
        net, a = self.net, self.net.a
        mine = tuple(net.rb[: self.low])
        moves = []
        if kind == "core":
            left = range(a - 1, -1, -1)
            moves.append((self.grads.at[(c % 2,) + net.pick(left, 0, False)], self.pair.at[c], net.seq_xor(1)))
        elif kind == "chips":
            for m in range(1, 2 ** (a - 1)):
                spot = tuple((1 - net.sb[i] if m >> (i - 1) & 1 else net.sb[i]) for i in range(a - 1, 0, -1))
                moves.append((self.pair.at[(c,) + spot], self.wide.at[c, m - 1], net.seq_xor(2 * m)))
        elif kind == "split":
            for m in range(1, 2**self.low):
                spot = tuple((1 - net.rb[i] if m >> i & 1 else net.rb[i]) for i in range(self.low))
                moves.append((self.part.at[(c,) + spot], self.quarter.at[c, m - 1], net.row_xor(m)))
        elif kind == "cross":
            spot = self.cross.at[c, net.row // 4]
            for m in range(1, 2 ** (net.b - 2)):
                moves.append((spot, spot, net.row_xor(4 * m)))
        else:
            spot = self.fin.at[(self.first + c,) + mine]
            for m in range(1, 2**self.low):
                moves.append((spot, spot, net.row_xor(m)))
        base = sum(len(self.copies(c, k)) for k in self.stages[: self.stages.index(kind)])
        return [
            remote(src, dst, self.send_sem.at[c, base + i], self.recv_sem.at[c, base + i], peer)
            for i, (src, dst, peer) in enumerate(moves)
        ]

    def start(self, c, kind="core"):
        for copy in self.copies(c, kind):
            copy.start()

    def finish(self, c, kind):
        net, a = self.net, self.net.a
        for copy in self.copies(c, kind):
            copy.wait()
        mine = tuple(net.rb[: self.low])
        at = self.stages.index(kind)
        if kind == "core":
            self.pair[c] = self.pair[c] + self.grads[(c % 2,) + net.pick(range(a - 1, -1, -1), 0, True)]
        elif kind == "chips":
            total = self.pair[(c,) + tuple(net.sb[i] for i in range(a - 1, 0, -1))].astype(F32)
            for m in range(1, 2 ** (a - 1)):
                total = total + self.wide[c, m - 1].astype(F32)
            self.part[c] = total.astype(BF)
        elif kind == "split":
            total = self.part[(c,) + mine].astype(F32)
            for m in range(1, 2**self.low):
                total = total + self.quarter[c, m - 1].astype(F32)
            if net.b > 2:
                self.cross[c, net.row // 4] = total.astype(BF)
            else:
                self.fin[(self.first + c,) + mine] = total.astype(BF)
        elif kind == "cross":
            total = self.cross[c, 0].astype(F32)
            for i in range(1, 2 ** (net.b - 2)):
                total = total + self.cross[c, i].astype(F32)
            self.fin[(self.first + c,) + mine] = total.astype(BF)
        if at + 1 < len(self.stages):
            self.start(c, self.stages[at + 1])


def layer_kernel(
    seq_bits, row_bits,
    len_ref, x_ref, dy_ref, fg_ref, fs_ref, sg_ref, ss_ref, bq_ref, bo_ref, bd_ref, bkv_ref, bu_ref, wq_hbm, wkv_hbm, wo_hbm, wu_hbm, wd_hbm,
    lo_ref, ig_ref, fin, small_ref, gkv_ref,
    wq, wkv, wo, wu, wd, load_sem, vec_ref, wide_ref,
    h1, h2, act, act_t, dup, gub, q_all, do_all, cs, kv_all, kv_send, kv_recv,
    s_ref, e_ref, qz, dz, m_ref, l_ref, o_ref, dqa, mt, dq, dkv, dkv_in, dkv_core, dkv_chip, dkv_sum, dkv_send, dkv_recv,
    grads, *rest,
):
    a, n, count = seq_bits, 2**seq_bits, 2**row_bits
    recs, rest = rest[:a], rest[a:]
    recz, rest = rest[:row_bits], rest[row_bits:]
    send_sem, recv_sem, rest = rest[0], rest[1], rest[2:]
    late_refs, rest = rest[:8], rest[8:]
    own_small, seq_small, row_small, own_kv, seq_kv, row_kv, m_send, m_recv = rest
    toks, width = x_ref.shape
    hidden = wu.shape[1]
    sub = width // n
    heads = width // HD
    lanes = s_ref.shape[-1]
    groups = heads * BLK // lanes
    near = lanes // BLK
    rows = toks // BLK
    n_up, n_down = hidden // CHUNK, width // QUARTER
    net = Net(seq_bits, row_bits)
    me = net.me
    n_early = n_up + n_down
    ring = Ring(net, n_early, grads, recs, recz, fin, send_sem, recv_sem)
    late = Late(net, n_early, *late_refs[:6], fin, *late_refs[6:])

    barrier = pltpu.get_barrier_semaphore()
    for peer in net.peers():
        pl.semaphore_signal(barrier, inc=1, device_id=peer, device_id_type=MESH)
    loads = {}
    head, tail = slice(0, CHUNK), slice(CHUNK, hidden)
    for i, (name, src, dst) in enumerate((
        ("kv", wkv_hbm, wkv), ("u0", wu_hbm.at[:, head], wu.at[:, head]), ("d0", wd_hbm.at[head], wd.at[head]),
        ("q", wq_hbm, wq), ("o", wo_hbm, wo), ("u", wu_hbm.at[:, tail], wu.at[:, tail]), ("d", wd_hbm.at[tail], wd.at[tail]),
    )):
        loads[name] = pltpu.make_async_copy(src, dst, load_sem.at[i])
        loads[name].start()

    for i, ref in enumerate((fg_ref, fs_ref, sg_ref, ss_ref, bq_ref)):
        vec_ref[i : i + 1, :] = ref[...].reshape(1, width)
    vec_ref[5:6, :] = (bo_ref[...] + bd_ref[...]).reshape(1, width)
    wide_ref[...] = bu_ref[...].reshape(1, hidden)

    def put_chunk(ref, ch, value, quarters=range(4)):
        for owner in range(n):
            at = (ch,) + tuple(reversed(bits_of(owner, a)))
            for i, q in enumerate(quarters):
                piece = value[owner * sub : (owner + 1) * sub, i * QUARTER : (i + 1) * QUARTER]
                ref[at + (q // 2, q % 2)] = piece.astype(BF)

    def row_cuts(r):
        cuts = []
        for i in range(len_ref.shape[1] - 1):
            cuts.append(len_ref[r, i] + (cuts[-1] if cuts else 0))
        return cuts

    place = me * BLK + lax.broadcasted_iota(jnp.int32, (8, BLK), 1)
    which = lax.broadcasted_iota(jnp.int32, (8, BLK), 0)
    freqs = jnp.ones((8, BLK), F32)
    for i in range(1, 8):
        freqs = jnp.where(which == i, 10000.0 ** (-2.0 * i / ROT), freqs)
    for r in range(rows):
        angles = (place - doc_start(place, row_cuts(r))).astype(F32) * freqs
        cs[r, 0] = jnp.cos(angles)
        cs[r, 1] = jnp.sin(angles)

    def row_span(r):
        return pl.ds(pl.multiple_of(r * BLK, BLK), BLK)

    def normalized(r):
        x = x_ref[row_span(r), :].astype(F32)
        centred = x - lanes_mean(x)
        factor = lax.rsqrt(lanes_mean(centred * centred) + EPS)
        return x, centred * factor, factor

    def norms(r, _):
        xhat = normalized(r)[1]
        h1[row_span(r), :] = (xhat * vec_ref[0:1, :] + vec_ref[1:2, :]).astype(BF)
        h2[row_span(r), :] = (xhat * vec_ref[2:3, :] + vec_ref[3:4, :]).astype(BF)
        return 0

    lax.fori_loop(0, rows, norms, 0)

    per_block = lanes // width

    def spare(k, r, cols=None):
        cols = slice(0, width) if cols is None else cols
        at = k % per_block * width
        return k // per_block * rows + r, slice(None), slice(at + cols.start, at + cols.stop)

    def by_rows(k, value):
        for r in range(rows):
            s_ref[spare(k, r)] = value[r * BLK : (r + 1) * BLK]

    loads["kv"].wait()
    kv = dot(h1[...], wkv[...]) + bkv_ref[...].reshape(1, 2 * HD)
    group = rows // 2

    def at_bits(value):
        return tuple(reversed(bits_of(value, a)))

    def kv_at(j, r):
        return at_bits(j) + (r // group, r % group)

    for r in range(rows):
        turned = rotate(kv[r * BLK : (r + 1) * BLK].T, cs[r, 0], cs[r, 1])
        kv_all[kv_at(me, r)] = turned.T.astype(BF)
    pl.semaphore_wait(barrier, n + count - 2)

    def kv_copies(k):
        out = []
        for half in (0, 1):
            order = list(range(1, a)) if half == 0 else list(range(a - 1, 0, -1))
            order.append(0)
            at = tuple(slice(None) if i in order[:k] else net.sb[i] for i in reversed(range(a))) + (half,)
            sem = 2 * k + half
            out.append(remote(kv_all.at[at], kv_all.at[at], kv_send.at[sem], kv_recv.at[sem], net.seq_xor(1 << order[k])))
        return out

    def kv_step(k):
        if k > 0:
            for copy in kv_copies(k - 1):
                copy.wait()
        if k < a:
            for copy in kv_copies(k):
                copy.start()

    kv_step(0)

    def feed(f):
        cols = pl.ds(pl.multiple_of(f * CHUNK, CHUNK), CHUNK)
        up = dot(h2[...], wu[:, cols]) + wide_ref[:, cols]
        d_act = dot_nt(dy_ref[...], wd[cols, :])
        cdf, slope = gelu_parts(up)
        low = (up * cdf).astype(BF)
        d_up = (d_act * (cdf + slope)).astype(BF)
        act[:, cols] = low
        act_t[cols, :] = low.T
        dup[:, cols] = d_up
        gub[:, cols] = column_sum(d_up.astype(F32))
        g = dot_tn(h2[...], d_up)
        put_chunk(grads, f % SLOTS, g)

    def down(j):
        cols = dy_ref[:, pl.ds(pl.multiple_of(j * QUARTER, QUARTER), QUARTER)]
        for owner in range(n):
            g = dot(act_t[owner * 4 * sub : (owner + 1) * 4 * sub, :], cols).astype(BF)
            at = ((n_up + j) % SLOTS,) + at_bits(owner)
            for i in range(4):
                grads[at + (i // 2, i % 2)] = g[i * sub : (i + 1) * sub]

    n_pre = 3
    dkv[...] = jnp.zeros(dkv.shape, BF)

    def feed_step(t, _):
        feed(t)
        ring.start(0, t)
        ring.tick(t)
        return 0

    loads["u0"].wait()
    loads["d0"].wait()
    feed_step(0, 0)

    loads["q"].wait()
    by_rows(0, dot(h1[...], wq[...]) + vec_ref[4:5, :])
    loads["o"].wait()
    by_rows(1, dot_nt(dy_ref[...], wo[...]))
    kv_step(1)

    def heads_apart(r, _):
        for h in range(0, heads, 2):
            pair = s_ref[spare(0, r, slice(h * HD, (h + 2) * HD))].T
            d_pair = s_ref[spare(1, r, slice(h * HD, (h + 2) * HD))].T.astype(BF)
            for i in (0, 1):
                span = slice((h + i) * BLK, (h + i + 1) * BLK)
                turned = rotate(pair[i * HD : (i + 1) * HD], cs[r, 0], cs[r, 1]).astype(BF).astype(F32)
                q_all[r, :, span] = (turned * 0.125).astype(BF)
                do_all[r, :, span] = d_pair[i * HD : (i + 1) * HD]
        return 0

    lax.fori_loop(0, rows, heads_apart, 0)
    kv_step(2)

    loads["u"].wait()
    loads["d"].wait()
    lax.fori_loop(1, n_pre, feed_step, 0)
    for k in range(3, a + 1):
        kv_step(k)

    keys_at_once = PAIR * BLK
    steps = me // PAIR + 1
    key_iota = lax.broadcasted_iota(jnp.int32, (keys_at_once, BLK), 0)
    query_place = me * BLK + lax.broadcasted_iota(jnp.int32, (keys_at_once, BLK), 1)

    def kv_blocks(i, r):
        return jnp.concatenate([kv_all[kv_at(PAIR * i + k, r)] for k in range(PAIR)], axis=0)

    def scores_pass(r, g):
        span = slice(g * lanes, (g + 1) * lanes)
        qz[:HD, :] = q_all[r, :, span]
        qz[HD:, :] = jnp.zeros((HD, lanes), BF)
        dz[HD:, :] = do_all[r, :, span]
        dz[:HD, :] = jnp.zeros((HD, lanes), BF)
        m_ref[...] = jnp.full(m_ref.shape, NEG, F32)
        l_ref[...] = jnp.zeros(l_ref.shape, F32)
        o_ref[...] = jnp.zeros(o_ref.shape, F32)
        dqa[...] = jnp.zeros(dqa.shape, F32)
        begin = doc_start(query_place, row_cuts(r))

        def body(i, _):
            keys = i * keys_at_once + key_iota
            bias = jnp.where((keys <= query_place) & (keys >= begin), 0.0, NEG)
            s = dot(kv_blocks(i, r), qz[...]) + jnp.concatenate([bias] * near, axis=1)
            s_ref[pl.ds(PAIR * i, PAIR)] = s.reshape(PAIR, BLK, lanes)
            m_ref[...] = jnp.maximum(m_ref[...], jnp.max(s.reshape(keys_at_once // 8, 8, lanes), axis=0))
            return 0

        lax.fori_loop(0, steps, body, 0)
        m_ref[0:1, :] = jnp.max(m_ref[...], axis=0, keepdims=True)

    def mix_pass(r, g):
        def body(i, _):
            v_t = kv_blocks(i, r).T[HD:]
            e = jnp.exp(s_ref[pl.ds(PAIR * i, PAIR)].reshape(keys_at_once, lanes) - m_ref[0:1, :])
            l_ref[...] += jnp.sum(e.reshape(keys_at_once // 8, 8, lanes), axis=0)
            e_low = e.astype(BF)
            e_ref[pl.ds(PAIR * i, PAIR)] = e_low.reshape(PAIR, BLK, lanes)
            o_ref[...] += dot(v_t, e_low)
            return 0

        lax.fori_loop(0, steps, body, 0)
        inv = 1.0 / jnp.sum(l_ref[...], axis=0, keepdims=True)
        o = o_ref[...] * inv
        l_ref[0:1, :] = inv
        m_ref[0:1, :] = jnp.sum(o * dz[HD:, :].astype(F32), axis=0, keepdims=True)
        span = row_span(r)
        for h in range(0, near, 2):
            pair = jnp.concatenate(
                [o[:, h * BLK : (h + 1) * BLK], o[:, (h + 1) * BLK : (h + 2) * BLK]], axis=0
            )
            at = slice((g * near + h) * HD, (g * near + h + 2) * HD)
            mt[at, span] = pair.astype(BF)

    def back_pass(r, g, start, stop):
        def body(i, _):
            kv = kv_blocks(i, r)
            k_t = kv.T[:HD]
            dp = dot(kv, dz[...])
            p = e_ref[pl.ds(PAIR * i, PAIR)].reshape(keys_at_once, lanes).astype(F32) * l_ref[0:1, :]
            ds = (p * (dp - m_ref[0:1, :])).astype(BF)
            total = dot_nt(ds, qz[...]) + dot_nt(p.astype(BF), dz[...])
            for k in range(PAIR):
                block = total[k * BLK : (k + 1) * BLK]
                if g > 0:
                    block = block + dkv[at_bits(PAIR * i + k) + (r,)].astype(F32)
                dkv[at_bits(PAIR * i + k) + (r,)] = block.astype(BF)
            dqa[...] += dot(k_t, ds)
            return 0

        lax.fori_loop(start, stop, body, 0)

    upper = range(a - 1, 0, -1)

    def dkv_pair(r):
        src = dkv.at[net.pick(range(a - 1, -1, -1), 0, False) + (r,)]
        return remote(src, dkv_core.at[r], dkv_send.at[r, 0], dkv_recv.at[r, 0], net.seq_xor(1))

    def dkv_chips(r):
        out = []
        for m in range(1, 2 ** (a - 1)):
            spot = tuple((1 - net.sb[i] if m >> (i - 1) & 1 else net.sb[i]) for i in upper)
            out.append(remote(dkv_core.at[(r,) + spot], dkv_chip.at[m - 1, r], dkv_send.at[r, m], dkv_recv.at[r, m],
                              net.seq_xor(2 * m)))
        return out

    def dkv_on(r):
        dkv_pair(r).wait()
        dkv_core[r] = dkv_core[r] + dkv[net.pick(range(a - 1, -1, -1), 0, True) + (r,)]
        for copy in dkv_chips(r):
            copy.start()

    def dkv_straight():
        out = []
        for m in range(1, n):
            peer = net.seq_xor(m)
            out.append((peer["seq"], remote(
                dkv.at[at_bits(peer["seq"]) + (rows - 1,)], dkv_in.at[m - 1],
                dkv_send.at[rows - 1, m - 1], dkv_recv.at[rows - 1, m - 1], peer)))
        return out

    def leave_pass(r, g):
        if g == groups - 1:
            if isinstance(r, int):
                for other, copy in dkv_straight():

                    @pl.when(other < me)
                    def _():
                        copy.start()

                dkv_on(r - 1)
            else:
                dkv_pair(r).start()

                @pl.when(r > 0)
                def _():
                    dkv_on(r - 1)

        cosine, sine = cs[r, 0], cs[r, 1]
        span = row_span(r)
        for h in range(0, near, 2):
            pair = jnp.concatenate(
                [rotate(dqa[:, i * BLK : (i + 1) * BLK], cosine, -sine) for i in (h, h + 1)], axis=0
            )
            dq[span, (g * near + h) * HD : (g * near + h + 2) * HD] = (pair * 0.125).T.astype(BF)

    def first_groups(r):
        for g in range(groups - 1):
            scores_pass(r, g)
            mix_pass(r, g)
            back_pass(r, g, 0, steps)
            leave_pass(r, g)

    def chunk_step(t):
        if isinstance(t, int):
            down(t - n_up)
            ring.start(0, t)
            ring.tick(t)
            return

        @pl.when(t < n_up)
        def _():
            feed(t)

        @pl.when(t >= n_up)
        def _():
            down(t - n_up)

        ring.start(0, t)
        ring.tick(t)

    def row_step(r, _):
        t = n_pre + 3 * r
        first_groups(r)
        scores_pass(r, groups - 1)
        chunk_step(t)
        mix_pass(r, groups - 1)
        chunk_step(t + 1)
        back_pass(r, groups - 1, 0, steps)
        leave_pass(r, groups - 1)
        chunk_step(t + 2)
        return 0

    lax.fori_loop(0, rows - 1, row_step, 0)
    r, t = rows - 1, n_up + n_down
    now = [t]

    def advance(count):
        for _ in range(count):
            if now[0] <= ring.last_tick():
                ring.tick(now[0])
                now[0] += 1

    first_groups(r)
    scores_pass(r, groups - 1)
    advance(1)
    mix_pass(r, groups - 1)
    put_chunk(late.grads, 0, dot(mt[...], dy_ref[:, :CHUNK]))
    late.start(0)
    advance(2)
    back_pass(r, groups - 1, 0, steps // 2)
    late.finish(0, "core")
    put_chunk(late.grads, 0, dot(mt[...], dy_ref[:, CHUNK:]), (0, 1))
    advance(2)
    back_pass(r, groups - 1, steps // 2, steps)
    leave_pass(r, groups - 1)
    advance(2)
    put_chunk(late.grads, 1, dot_tn(h1[...], dq[:, :CHUNK]))
    late.start(1)
    late.finish(0, "chips")
    put_chunk(late.grads, 0, dot_tn(h1[...], dq[:, CHUNK:]), (2, 3))
    late.start(2)
    advance(2)
    late.finish(1, "core")
    by_rows(0, dot_nt(dup[...], wu[...]))
    late.finish(2, "core")
    advance(2)
    for kind in late.stages[2:-1]:
        late.finish(0, kind)

    def narrow(step):
        if step == 0:
            return [
                remote(own_small, seq_small.at[me], m_send.at[m - 1], m_recv.at[m - 1], net.seq_xor(m)) for m in range(1, n)
            ]
        spot, base = row_small.at[net.row], n - 2
        return [
            remote(spot, spot, m_send.at[base + m], m_recv.at[base + m], net.row_xor(m)) for m in range(1, count)
        ]

    def narrow_kv(step):
        base = n + count - 2
        if step == 0:
            out = []
            for m in range(1, n):
                peer = net.seq_xor(m)
                out.append(remote(own_kv.at[peer["seq"]], seq_kv.at[m - 1],
                                  m_send.at[base + m - 1], m_recv.at[base + m - 1], peer))
            return out
        spot, base = row_kv.at[net.row], base + n - 2
        return [
            remote(spot, spot, m_send.at[base + m], m_recv.at[base + m], net.row_xor(m)) for m in range(1, count)
        ]

    dkv_sum[rows - 1] = dkv[at_bits(me) + (rows - 1,)].astype(F32)
    for r in range(rows - 1):
        total = dkv_core[(r,) + tuple(net.sb[i] for i in upper)].astype(F32)
        for m, copy in enumerate(dkv_chips(r)):
            copy.wait()
            total = total + dkv_chip[m, r].astype(F32)
        dkv_sum[r] = total
    for m, (other, copy) in enumerate(dkv_straight()):

        @pl.when(other < me)
        def _():
            copy.wait_send()

        @pl.when(other > me)
        def _():
            copy.wait_recv()
            dkv_sum[rows - 1] += dkv_in[m].astype(F32)

    d_kv = jnp.concatenate(
        [rotate(dkv_sum[r].T, cs[r, 0], -cs[r, 1]).T.astype(BF) for r in range(rows)], axis=0
    )
    g = dot_tn(h1[...], d_kv)
    for owner in range(n):
        own_kv[owner] = g[owner * sub : (owner + 1) * sub].astype(BF)
    for copy in narrow_kv(0):
        copy.start()

    by_rows(1, dot_nt(dq[...], wq[...]) + dot_nt(d_kv, wkv[...]))
    own_small[...] = jnp.zeros(own_small.shape, F32)
    per = width // 128

    def add_small(at, vector):
        for i in range(vector.shape[1] // 128):
            own_small[at + i : at + i + 1, :] += vector[:, i * 128 : (i + 1) * 128]

    def norms_back(r, _):
        _, xhat, factor = normalized(r)
        dy32 = dy_ref[row_span(r), :].astype(F32)
        result = dy32
        for k, gain in enumerate((vec_ref[0:1, :], vec_ref[2:3, :])):
            grad = s_ref[spare(1 - k, r)]
            add_small(2 * k * per, column_sum(grad * xhat))
            add_small((2 * k + 1) * per, column_sum(grad))
            g = grad * gain
            result = result + factor * (g - lanes_mean(g) - xhat * lanes_mean(g * xhat))
        h2[row_span(r), :] = result.astype(BF)
        add_small(4 * per, column_sum(dq[row_span(r), :].astype(F32)))
        add_small(5 * per + 1, column_sum(dy32))
        return 0

    lax.fori_loop(0, rows, norms_back, 0)
    ig_copy = pltpu.make_async_copy(h2, ig_ref, load_sem.at[7])
    ig_copy.start()
    add_small(5 * per, column_sum(d_kv.astype(F32)))
    add_small(6 * per + 1, gub[...])

    for copy in narrow(0):
        copy.start()
    late.finish(1, "chips")
    late.finish(2, "chips")
    advance(2)
    by_rows(2, dot(act[...], wd[...]) + vec_ref[5:6, :])
    for copy in narrow_kv(0):
        copy.wait()
    sums = own_kv[me].astype(F32)
    for m in range(1, n):
        sums = sums + seq_kv[m - 1].astype(F32)
    row_kv[net.row] = sums.astype(BF)
    for copy in narrow_kv(1):
        copy.start()
    for copy in narrow(0):
        copy.wait()
    seq_small[me] = own_small[...]
    sums = seq_small[0]
    for i in range(1, n):
        sums = sums + seq_small[i]
    row_small[net.row] = sums
    for copy in narrow(1):
        copy.start()
    for c in (1, 2):
        for kind in late.stages[2:-1]:
            late.finish(c, kind)
    by_rows(3, dot_tn(mt[...], wo[...]))

    def layer_out(r, _):
        total = x_ref[row_span(r), :].astype(F32) + s_ref[spare(2, r)] + s_ref[spare(3, r)]
        h1[row_span(r), :] = total.astype(BF)
        return 0

    lax.fori_loop(0, rows, layer_out, 0)
    lo_copy = pltpu.make_async_copy(h1, lo_ref, load_sem.at[8])
    lo_copy.start()
    advance(99)
    for c in range(3):
        late.finish(c, "back")
    for copy in narrow(1):
        copy.wait()
    sums = row_small[0]
    for i in range(1, count):
        sums = sums + row_small[i]
    small_ref[...] = sums
    for copy in narrow_kv(1):
        copy.wait()
    sums = row_kv[0].astype(F32)
    for i in range(1, count):
        sums = sums + row_kv[i].astype(F32)
    gkv_ref[...] = sums
    ig_copy.wait()
    lo_copy.wait()


def layer(net_bits, lengths, x, dy, vectors, wq, wkv, wo, wu, wd):
    a, b = net_bits
    n, count = 2**a, 2**b
    toks, width = x.shape
    hidden = wu.shape[1]
    sub = width // n
    rows = toks // BLK
    all_lanes = width // HD * BLK
    lanes = all_lanes // max(1, n // 8)
    n_up, n_down = hidden // CHUNK, width // QUARTER
    early, late = n_up + n_down, 3
    total = early + late
    slots = RING
    low = min(b, 2)
    two = (2,)
    vm = pltpu.VMEM
    dma = pltpu.SemaphoreType.DMA
    n_sems = 1 + 2 * (a - 1) + b + min(b, 2)
    scratch = [
        vm(wq.shape, BF), vm(wkv.shape, BF), vm(wo.shape, BF), vm(wu.shape, BF), vm(wd.shape, BF), dma((9,)),
        vm((8, width), F32), vm((1, hidden), F32),
        vm((toks, width), BF), vm((toks, width), BF),
        vm((toks, hidden), BF), vm((hidden, toks), BF), vm((toks, hidden), BF), vm((1, hidden), F32),
        vm((rows, HD, all_lanes), BF), vm((rows, HD, all_lanes), BF), vm((rows, 2, 8, BLK), F32),
        vm(two * a + (2, rows // 2, BLK, 2 * HD), BF), dma((2 * a,)), dma((2 * a,)),
        vm((n, BLK, lanes), F32), vm((n, BLK, lanes), BF), vm((2 * HD, lanes), BF), vm((2 * HD, lanes), BF),
        vm((8, lanes), F32), vm((8, lanes), F32), vm((HD, lanes), F32), vm((HD, lanes), F32),
        vm((width, toks), BF), vm((toks, width), BF),
        vm(two * a + (rows, BLK, 2 * HD), BF), vm((n - 1, BLK, 2 * HD), BF),
        vm((rows - 1,) + two * (a - 1) + (BLK, 2 * HD), BF), vm((n // 2 - 1, rows - 1, BLK, 2 * HD), BF),
        vm((rows, BLK, 2 * HD), F32), dma((rows, n - 1)), dma((rows, n - 1)),
        vm((SLOTS,) + two * a + (2, 2, sub, 128), BF),
        vm((slots,) + two * (a - 1) + (2, 2, sub, 128), BF),
    ]
    scratch += [vm((slots, 2) + two * (a - 1 - k) + (2, sub, 128), BF) for k in range(1, a)]
    scratch += [vm((slots, 2, sub, 128), BF)] + [vm((slots, sub, 128), BF) for _ in range(1, b)]
    scratch += [
        dma((early, n_sems)), dma((early, n_sems)),
        vm((2,) + two * a + (2, 2, sub, 128), BF),
        vm((late,) + two * (a - 1) + (2, 2, sub, 128), BF),
        vm((late, n // 2 - 1, 2, 2, sub, 128), BF),
        vm((late, 2, 2, sub, 128), BF),
        vm((late, 2**low - 1, sub, 128), BF),
        vm((late, max(count // 4, 1), sub, 128), BF),
        dma((late, n // 2 + count + 2)), dma((late, n // 2 + count + 2)),
        vm((64, 128), F32), vm((n, 64, 128), F32), vm((count, 64, 128), F32),
        vm((n, sub, 2 * HD), BF), vm((n - 1, sub, 2 * HD), BF), vm((count, sub, 2 * HD), BF),
        dma((2 * (n + count),)), dma((2 * (n + count),)),
    ]
    vmem = pl.BlockSpec(memory_space=pltpu.VMEM)
    hbm = pl.BlockSpec(memory_space=pl.ANY)
    shape = jax.ShapeDtypeStruct
    return pl.pallas_call(
        functools.partial(layer_kernel, a, b),
        out_shape=[
            shape((toks, width), BF), shape((toks, width), BF),
            shape((total, 2, 2, sub, 128), BF), shape((64, 128), F32), shape((sub, 2 * HD), F32),
        ],
        in_specs=[pl.BlockSpec(memory_space=pltpu.SMEM)] + [vmem] * (2 + len(vectors)) + [hbm] * 5,
        out_specs=[hbm, hbm, vmem, vmem, vmem],
        scratch_shapes=scratch,
        compiler_params=pltpu.CompilerParams(collective_id=0, has_side_effects=True, vmem_limit_bytes=64 * 2**20),
        name="layer",
    )(lengths, x, dy, *vectors, wq, wkv, wo, wu, wd)


def finish_kernel(n_up, sizes, lo_in, ig_in, fin_in, small_in, gkv_in, lo, ig, gup, gdown, gout, gq, gkv, *rest):
    vectors, (fin, small, vlo, vig, vup, vdown, vout, vq, vkv, sem) = rest[: len(sizes)], rest[len(sizes) :]
    sub, width = gout.shape
    n_down = width // QUARTER
    late = n_up + n_down

    def move(i, src, dst):
        copy = pltpu.make_async_copy(src, dst, sem.at[i])
        copy.start()
        return copy

    loads = [move(0, fin_in, fin), move(1, small_in, small), move(8, gkv_in, vkv)]
    loads += [move(2, lo_in, vlo), move(3, ig_in, vig)]
    for load in loads:
        load.wait()
    moves = [move(9, vlo, lo), move(10, vig, ig)]

    def piece(ch, q):
        return fin[ch, q // 2, q % 2].astype(F32)

    def span(at, q):
        return slice(at + q * QUARTER, at + (q + 1) * QUARTER)

    for q in range(4):
        for f in range(n_up):
            vup[:, span(f * CHUNK, q)] = piece(f, q)
    moves.append(move(4, vup, gup))
    for q in range(4):
        for j in range(n_down):
            vdown[q * sub : (q + 1) * sub, j * QUARTER : (j + 1) * QUARTER] = piece(n_up + j, q)
    moves.append(move(5, vdown, gdown))
    for q in range(4):
        vout[:, span(0, q)] = piece(late, q)
        vq[:, span(0, q)] = piece(late + 1, q)
        if q < 2:
            vout[:, span(CHUNK, q)] = piece(late + 2, q)
            vq[:, span(CHUNK, q)] = piece(late + 2, q + 2)
    moves += [move(6, vout, gout), move(7, vq, gq), move(11, vkv, gkv)]
    at = 0
    for size, ref in zip(sizes[:-1], vectors):
        for i in range(size // 128):
            ref[i * 128 : (i + 1) * 128] = small[at + i, :]
        at += size // 128
    vectors[-1][...] = vectors[-3][...]
    for copy in moves:
        copy.wait()


def finish(lo, ig, fin, small, gkv, sub, width, hidden):
    sizes = [width] * 5 + [2 * HD, width, hidden, width]
    shape = jax.ShapeDtypeStruct
    hbm = pl.BlockSpec(memory_space=pl.ANY)
    grads = [(sub, hidden), (4 * sub, width), (sub, width), (sub, width), (sub, 2 * HD)]
    return pl.pallas_call(
        functools.partial(finish_kernel, hidden // CHUNK, sizes),
        out_shape=[shape(lo.shape, BF), shape(ig.shape, BF)]
        + [shape(g, F32) for g in grads] + [shape((size,), F32) for size in sizes],
        in_specs=[hbm] * 5,
        out_specs=[hbm] * 7 + [pl.BlockSpec(memory_space=pltpu.VMEM)] * len(sizes),
        scratch_shapes=[pltpu.VMEM(fin.shape, BF), pltpu.VMEM(small.shape, F32), pltpu.VMEM(lo.shape, BF), pltpu.VMEM(ig.shape, BF)]
        + [pltpu.VMEM(g, F32) for g in grads] + [pltpu.SemaphoreType.DMA((12,))],
        compiler_params=pltpu.CompilerParams(vmem_limit_bytes=64 * 2**20),
        name="finish",
    )(lo, ig, fin, small, gkv)


def shards(
    hidden, lengths, cotangent, first_gain, first_shift, second_gain, second_shift,
    query_weight, query_bias, keyvalue_weight, keyvalue_bias, output_weight, output_bias,
    up_weight, up_bias, down_weight, down_bias,
):
    rows, block, width = hidden.shape
    toks = rows * block
    n, count = lax.axis_size("seq"), lax.axis_size("rows")
    vectors = (
        first_gain, first_shift, second_gain, second_shift, query_bias, output_bias, down_bias, keyvalue_bias, up_bias,
    )
    lo, ig, fin, small, g_kv = layer(
        (n.bit_length() - 1, count.bit_length() - 1), lengths,
        hidden.reshape(toks, width), cotangent.reshape(toks, width), vectors,
        query_weight, keyvalue_weight, output_weight, up_weight, down_weight,
    )
    lo, ig, g_up, g_down, g_out, g_q, g_kv, *sums = finish(
        lo, ig, fin, small, g_kv, width // n, width, up_weight.shape[1]
    )
    s_fg, s_fs, s_sg, s_ss, s_qb, s_kb, s_ob, s_ub, s_db = sums
    return (
        lo.reshape(hidden.shape), ig.reshape(hidden.shape),
        s_fg, s_fs, s_sg, s_ss, g_q, s_qb, g_kv, s_kb, g_out, s_ob, g_up, s_ub, g_down, s_db,
    )


def solution(mesh):
    tokens = P("rows", "seq", None)
    weight = P("seq", None)
    return jax.shard_map(
        shards,
        mesh=mesh,
        in_specs=(tokens, P("rows", None), tokens) + (P(),) * 14,
        out_specs=(
            tokens, tokens, P(), P(), P(), P(), weight, P(), weight, P(), weight, P(), weight, P(), weight, P(),
        ),
        check_vma=False,
    )
```

```python
import functools

import jax
import jax.numpy as jnp
from jax import lax
from jax.experimental import pallas as pl
from jax.experimental.pallas import tpu as pltpu
from jax.sharding import PartitionSpec as P

HD = 64
PAIR = 4
ROT = 16
BLK = 128
NEG = -1e30
EPS = 1e-05
F32 = jnp.float32
BF = jnp.bfloat16
MESH = pl.DeviceIdType.MESH
CHUNK = 512
QUARTER = 128
SLOTS = 3
RING = 8
WAITS = {"first": 1, "seq": 2}


def dot(a, b):
    return jnp.dot(a, b, preferred_element_type=F32)


def dot_nt(a, b):
    return lax.dot_general(a, b, (((1,), (1,)), ((), ())), preferred_element_type=F32)


def dot_tn(a, b):
    return lax.dot_general(a, b, (((0,), (0,)), ((), ())), preferred_element_type=F32)


def lanes_mean(v):
    return jnp.mean(v, axis=-1, keepdims=True)


def column_sum(v):
    return jnp.sum(v, axis=0, keepdims=True)


def doc_start(place, cuts):
    begin = jnp.where(place >= cuts[0], cuts[0], 0)
    for cut in cuts[1:]:
        begin = jnp.where(place >= cut, cut, begin)
    return begin


def rotate(values, cosine, sine):
    front, behind = values[:8], values[8:16]
    return jnp.concatenate([front * cosine - behind * sine, behind * cosine + front * sine, values[16:]], axis=0)


def gelu_parts(up):
    cdf = 0.5 + 0.5 * lax.erf(up * 0.7071067811865476)
    pdf = jnp.exp(-0.5 * up * up) * 0.3989422804014327
    return cdf, up * pdf


def bits_of(value, count):
    return [value // 2**i % 2 for i in range(count)]


def remote(src, dst, send_sem, recv_sem, peer):
    return pltpu.make_async_remote_copy(
        src_ref=src, dst_ref=dst, send_sem=send_sem, recv_sem=recv_sem, device_id=peer, device_id_type=MESH
    )


class Net:
    def __init__(self, seq_bits, row_bits):
        self.a, self.b = seq_bits, row_bits
        self.me, self.row = lax.axis_index("seq"), lax.axis_index("rows")
        self.sb, self.rb = bits_of(self.me, seq_bits), bits_of(self.row, row_bits)

    def seq_xor(self, mask):
        out = self.me
        for i in range(self.a):
            if mask >> i & 1:
                out = out + (1 - 2 * self.sb[i]) * 2**i
        return {"seq": out}

    def row_xor(self, mask):
        out = self.row
        for i in range(self.b):
            if mask >> i & 1:
                out = out + (1 - 2 * self.rb[i]) * 2**i
        return {"rows": out}

    def peers(self):
        return [self.seq_xor(m) for m in range(1, 2**self.a)] + [self.row_xor(m) for m in range(1, 2**self.b)]

    def pick(self, left, bit, mine):
        own = self.sb[bit]
        return tuple((own if mine else 1 - own) if i == bit else slice(None) for i in left)


class Ring:
    def __init__(self, net, early, grads, recs, recz, fin, send_sem, recv_sem):
        self.net, self.early = net, early
        self.grads, self.recs, self.recz, self.fin = grads, recs, recz, fin
        self.send_sem, self.recv_sem = send_sem, recv_sem
        a, b = net.a, net.b
        self.halves = min(b, 2)
        self.stages = [("first", 0)] + [("seq", k) for k in range(1, a)]
        self.stages += [("split", i) for i in range(self.halves)]
        self.stages += [("whole", i) for i in range(2, b)]
        self.stages += [("back", i) for i in reversed(range(self.halves))]
        self.sem_at, n = [], 0
        self.ticks_to, ticks = [], 0
        for kind, _ in self.stages:
            self.sem_at.append(n)
            n += 2 if kind == "seq" else 1
            ticks += WAITS.get(kind, 2)
            self.ticks_to.append(ticks)

    def moves(self, stage, ch):
        net, a = self.net, self.net.a
        kind, k = self.stages[stage]
        at = (ch % RING,)
        if kind == "first":
            left = range(a - 1, -1, -1)
            slot = (ch % SLOTS,)
            return [(self.grads.at[slot + net.pick(left, 0, False)], self.recs[0].at[at], net.seq_xor(1),
                     (self.grads, slot + net.pick(left, 0, True)), (self.recs[0], at))]
        if kind == "seq":
            out = []
            prev, here = self.recs[k - 1], self.recs[k]
            for half in (0, 1):
                if half == 0:
                    bit, left = k, range(a - 1, k - 1, -1)
                else:
                    bit, left = a - k, range(a - k, 0, -1)
                base, tail = (at, (half,)) if k == 1 else (at + (half,), ())
                out.append((prev.at[base + net.pick(left, bit, False) + tail], here.at[at + (half,)],
                            net.seq_xor(1 << bit), (prev, base + net.pick(left, bit, True) + tail), (here, at + (half,))))
            return out
        if kind == "split":
            prev = self.recs[a - 1] if k == 0 else self.recz[k - 1]
            return [(prev.at[at + (1 - net.rb[k],)], self.recz[k].at[at], net.row_xor(1 << k),
                     (prev, at + (net.rb[k],)), (self.recz[k], at))]
        if kind == "whole":
            prev = self.recz[k - 1]
            return [(prev.at[at], self.recz[k].at[at], net.row_xor(1 << k), (prev, at), (self.recz[k], at))]
        at = (ch,) + tuple(net.rb[: k + 1])
        return [(self.fin.at[at], self.fin.at[at], net.row_xor(1 << k), None, None)]

    def copies(self, stage, ch):
        out = []
        for i, (src, dst, peer, _, _) in enumerate(self.moves(stage, ch)):
            sem = self.sem_at[stage] + i
            out.append(remote(src, dst, self.send_sem.at[ch, sem], self.recv_sem.at[ch, sem], peer))
        return out

    def start(self, stage, ch):
        for copy in self.copies(stage, ch):
            copy.start()

    def finish(self, stage, ch):
        for copy in self.copies(stage, ch):
            copy.wait()
        kind, _ = self.stages[stage]
        if kind != "back":
            last = self.stages[stage + 1][0] == "back"
            for _, _, _, (src, src_at), (dst, dst_at) in self.moves(stage, ch):
                total = src[src_at] + dst[dst_at]
                if last:
                    self.fin[(ch,) + tuple(self.net.rb[: self.halves])] = total
                else:
                    dst[dst_at] = total
        if stage + 1 < len(self.stages):
            self.start(stage + 1, ch)

    def tick(self, t):
        for stage in reversed(range(len(self.stages))):
            ch = t - self.ticks_to[stage]
            if isinstance(ch, int):
                if 0 <= ch < self.early:
                    self.finish(stage, ch)
            else:

                @pl.when((ch >= 0) & (ch < self.early))
                def _():
                    self.finish(stage, ch)

    def last_tick(self):
        return self.early - 1 + self.ticks_to[-1]


class Late:
    def __init__(self, net, first, grads, pair, wide, part, quarter, cross, fin, send_sem, recv_sem):
        self.net, self.first, self.fin = net, first, fin
        self.grads, self.pair, self.wide, self.part = grads, pair, wide, part
        self.quarter, self.cross = quarter, cross
        self.send_sem, self.recv_sem = send_sem, recv_sem
        self.low = min(net.b, 2)
        self.stages = ["core", "chips", "split"] + (["cross"] if net.b > 2 else []) + ["back"]

    def copies(self, c, kind):
        net, a = self.net, self.net.a
        mine = tuple(net.rb[: self.low])
        moves = []
        if kind == "core":
            left = range(a - 1, -1, -1)
            moves.append((self.grads.at[(c % 2,) + net.pick(left, 0, False)], self.pair.at[c], net.seq_xor(1)))
        elif kind == "chips":
            for m in range(1, 2 ** (a - 1)):
                spot = tuple((1 - net.sb[i] if m >> (i - 1) & 1 else net.sb[i]) for i in range(a - 1, 0, -1))
                moves.append((self.pair.at[(c,) + spot], self.wide.at[c, m - 1], net.seq_xor(2 * m)))
        elif kind == "split":
            for m in range(1, 2**self.low):
                spot = tuple((1 - net.rb[i] if m >> i & 1 else net.rb[i]) for i in range(self.low))
                moves.append((self.part.at[(c,) + spot], self.quarter.at[c, m - 1], net.row_xor(m)))
        elif kind == "cross":
            spot = self.cross.at[c, net.row // 4]
            for m in range(1, 2 ** (net.b - 2)):
                moves.append((spot, spot, net.row_xor(4 * m)))
        else:
            spot = self.fin.at[(self.first + c,) + mine]
            for m in range(1, 2**self.low):
                moves.append((spot, spot, net.row_xor(m)))
        base = sum(len(self.copies(c, k)) for k in self.stages[: self.stages.index(kind)])
        return [
            remote(src, dst, self.send_sem.at[c, base + i], self.recv_sem.at[c, base + i], peer)
            for i, (src, dst, peer) in enumerate(moves)
        ]

    def start(self, c, kind="core"):
        for copy in self.copies(c, kind):
            copy.start()

    def finish(self, c, kind):
        net, a = self.net, self.net.a
        for copy in self.copies(c, kind):
            copy.wait()
        mine = tuple(net.rb[: self.low])
        at = self.stages.index(kind)
        if kind == "core":
            self.pair[c] = self.pair[c] + self.grads[(c % 2,) + net.pick(range(a - 1, -1, -1), 0, True)]
        elif kind == "chips":
            total = self.pair[(c,) + tuple(net.sb[i] for i in range(a - 1, 0, -1))].astype(F32)
            for m in range(1, 2 ** (a - 1)):
                total = total + self.wide[c, m - 1].astype(F32)
            self.part[c] = total.astype(BF)
        elif kind == "split":
            total = self.part[(c,) + mine].astype(F32)
            for m in range(1, 2**self.low):
                total = total + self.quarter[c, m - 1].astype(F32)
            if net.b > 2:
                self.cross[c, net.row // 4] = total.astype(BF)
            else:
                self.fin[(self.first + c,) + mine] = total.astype(BF)
        elif kind == "cross":
            total = self.cross[c, 0].astype(F32)
            for i in range(1, 2 ** (net.b - 2)):
                total = total + self.cross[c, i].astype(F32)
            self.fin[(self.first + c,) + mine] = total.astype(BF)
        if at + 1 < len(self.stages):
            self.start(c, self.stages[at + 1])


def layer_kernel(
    seq_bits, row_bits,
    len_ref, x_ref, dy_ref, fg_ref, fs_ref, sg_ref, ss_ref, bq_ref, bo_ref, bd_ref, bkv_ref, bu_ref, wq_hbm, wkv_hbm, wo_hbm, wu_hbm, wd_hbm,
    lo_ref, ig_ref, fin, small_ref, gkv_ref,
    wq, wkv, wo, wu, wd, load_sem, vec_ref, wide_ref,
    h1, h2, act, act_t, dup, gub, q_all, do_all, cs, kv_all, kv_send, kv_recv,
    s_ref, e_ref, qz, dz, m_ref, l_ref, o_ref, dqa, mt, dq, dkv, dkv_in, dkv_core, dkv_chip, dkv_sum, dkv_send, dkv_recv,
    grads, *rest,
):
    a, n, count = seq_bits, 2**seq_bits, 2**row_bits
    recs, rest = rest[:a], rest[a:]
    recz, rest = rest[:row_bits], rest[row_bits:]
    send_sem, recv_sem, rest = rest[0], rest[1], rest[2:]
    late_refs, rest = rest[:8], rest[8:]
    own_small, seq_small, row_small, own_kv, seq_kv, row_kv, m_send, m_recv = rest
    toks, width = x_ref.shape
    hidden = wu.shape[1]
    sub = width // n
    heads = width // HD
    lanes = s_ref.shape[-1]
    groups = heads * BLK // lanes
    near = lanes // BLK
    rows = toks // BLK
    n_up, n_down = hidden // CHUNK, width // QUARTER
    net = Net(seq_bits, row_bits)
    me = net.me
    n_early = n_up + n_down
    ring = Ring(net, n_early, grads, recs, recz, fin, send_sem, recv_sem)
    late = Late(net, n_early, *late_refs[:6], fin, *late_refs[6:])

    barrier = pltpu.get_barrier_semaphore()
    for peer in net.peers():
        pl.semaphore_signal(barrier, inc=1, device_id=peer, device_id_type=MESH)
    loads = {}
    head, tail = slice(0, CHUNK), slice(CHUNK, hidden)
    for i, (name, src, dst) in enumerate((
        ("kv", wkv_hbm, wkv), ("u0", wu_hbm.at[:, head], wu.at[:, head]), ("d0", wd_hbm.at[head], wd.at[head]),
        ("q", wq_hbm, wq), ("o", wo_hbm, wo), ("u", wu_hbm.at[:, tail], wu.at[:, tail]), ("d", wd_hbm.at[tail], wd.at[tail]),
    )):
        loads[name] = pltpu.make_async_copy(src, dst, load_sem.at[i])
        loads[name].start()

    for i, ref in enumerate((fg_ref, fs_ref, sg_ref, ss_ref, bq_ref)):
        vec_ref[i : i + 1, :] = ref[...].reshape(1, width)
    vec_ref[5:6, :] = (bo_ref[...] + bd_ref[...]).reshape(1, width)
    wide_ref[...] = bu_ref[...].reshape(1, hidden)

    def put_chunk(ref, ch, value, quarters=range(4)):
        for owner in range(n):
            at = (ch,) + tuple(reversed(bits_of(owner, a)))
            for i, q in enumerate(quarters):
                piece = value[owner * sub : (owner + 1) * sub, i * QUARTER : (i + 1) * QUARTER]
                ref[at + (q // 2, q % 2)] = piece.astype(BF)

    def row_cuts(r):
        cuts = []
        for i in range(len_ref.shape[1] - 1):
            cuts.append(len_ref[r, i] + (cuts[-1] if cuts else 0))
        return cuts

    place = me * BLK + lax.broadcasted_iota(jnp.int32, (8, BLK), 1)
    which = lax.broadcasted_iota(jnp.int32, (8, BLK), 0)
    freqs = jnp.ones((8, BLK), F32)
    for i in range(1, 8):
        freqs = jnp.where(which == i, 10000.0 ** (-2.0 * i / ROT), freqs)
    for r in range(rows):
        angles = (place - doc_start(place, row_cuts(r))).astype(F32) * freqs
        cs[r, 0] = jnp.cos(angles)
        cs[r, 1] = jnp.sin(angles)

    def row_span(r):
        return pl.ds(pl.multiple_of(r * BLK, BLK), BLK)

    def normalized(r):
        x = x_ref[row_span(r), :].astype(F32)
        centred = x - lanes_mean(x)
        factor = lax.rsqrt(lanes_mean(centred * centred) + EPS)
        return x, centred * factor, factor

    def norms(r, _):
        xhat = normalized(r)[1]
        h1[row_span(r), :] = (xhat * vec_ref[0:1, :] + vec_ref[1:2, :]).astype(BF)
        h2[row_span(r), :] = (xhat * vec_ref[2:3, :] + vec_ref[3:4, :]).astype(BF)
        return 0

    lax.fori_loop(0, rows, norms, 0)

    per_block = lanes // width

    def spare(k, r, cols=None):
        cols = slice(0, width) if cols is None else cols
        at = k % per_block * width
        return k // per_block * rows + r, slice(None), slice(at + cols.start, at + cols.stop)

    def by_rows(k, value):
        for r in range(rows):
            s_ref[spare(k, r)] = value[r * BLK : (r + 1) * BLK]

    loads["kv"].wait()
    kv = dot(h1[...], wkv[...]) + bkv_ref[...].reshape(1, 2 * HD)
    group = rows // 2

    def at_bits(value):
        return tuple(reversed(bits_of(value, a)))

    def kv_at(j, r):
        return at_bits(j) + (r // group, r % group)

    for r in range(rows):
        turned = rotate(kv[r * BLK : (r + 1) * BLK].T, cs[r, 0], cs[r, 1])
        kv_all[kv_at(me, r)] = turned.T.astype(BF)
    pl.semaphore_wait(barrier, n + count - 2)

    def kv_copies(k):
        out = []
        for half in (0, 1):
            order = list(range(1, a)) if half == 0 else list(range(a - 1, 0, -1))
            order.append(0)
            at = tuple(slice(None) if i in order[:k] else net.sb[i] for i in reversed(range(a))) + (half,)
            sem = 2 * k + half
            out.append(remote(kv_all.at[at], kv_all.at[at], kv_send.at[sem], kv_recv.at[sem], net.seq_xor(1 << order[k])))
        return out

    def kv_step(k):
        if k > 0:
            for copy in kv_copies(k - 1):
                copy.wait()
        if k < a:
            for copy in kv_copies(k):
                copy.start()

    kv_step(0)

    def feed(f):
        cols = pl.ds(pl.multiple_of(f * CHUNK, CHUNK), CHUNK)
        up = dot(h2[...], wu[:, cols]) + wide_ref[:, cols]
        d_act = dot_nt(dy_ref[...], wd[cols, :])
        cdf, slope = gelu_parts(up)
        low = (up * cdf).astype(BF)
        d_up = (d_act * (cdf + slope)).astype(BF)
        act[:, cols] = low
        act_t[cols, :] = low.T
        dup[:, cols] = d_up
        gub[:, cols] = column_sum(d_up.astype(F32))
        g = dot_tn(h2[...], d_up)
        put_chunk(grads, f % SLOTS, g)

    def down(j):
        cols = dy_ref[:, pl.ds(pl.multiple_of(j * QUARTER, QUARTER), QUARTER)]
        for owner in range(n):
            g = dot(act_t[owner * 4 * sub : (owner + 1) * 4 * sub, :], cols).astype(BF)
            at = ((n_up + j) % SLOTS,) + at_bits(owner)
            for i in range(4):
                grads[at + (i // 2, i % 2)] = g[i * sub : (i + 1) * sub]

    n_pre = 3
    dkv[...] = jnp.zeros(dkv.shape, BF)

    def feed_step(t, _):
        feed(t)
        ring.start(0, t)
        ring.tick(t)
        return 0

    loads["u0"].wait()
    loads["d0"].wait()
    feed_step(0, 0)

    loads["q"].wait()
    by_rows(0, dot(h1[...], wq[...]) + vec_ref[4:5, :])
    loads["o"].wait()
    by_rows(1, dot_nt(dy_ref[...], wo[...]))
    kv_step(1)

    def heads_apart(r, _):
        for h in range(0, heads, 2):
            pair = s_ref[spare(0, r, slice(h * HD, (h + 2) * HD))].T
            d_pair = s_ref[spare(1, r, slice(h * HD, (h + 2) * HD))].T.astype(BF)
            for i in (0, 1):
                span = slice((h + i) * BLK, (h + i + 1) * BLK)
                turned = rotate(pair[i * HD : (i + 1) * HD], cs[r, 0], cs[r, 1]).astype(BF).astype(F32)
                q_all[r, :, span] = (turned * 0.125).astype(BF)
                do_all[r, :, span] = d_pair[i * HD : (i + 1) * HD]
        return 0

    lax.fori_loop(0, rows, heads_apart, 0)
    kv_step(2)

    loads["u"].wait()
    loads["d"].wait()
    lax.fori_loop(1, n_pre, feed_step, 0)
    for k in range(3, a + 1):
        kv_step(k)

    keys_at_once = PAIR * BLK
    steps = me // PAIR + 1
    key_iota = lax.broadcasted_iota(jnp.int32, (keys_at_once, BLK), 0)
    query_place = me * BLK + lax.broadcasted_iota(jnp.int32, (keys_at_once, BLK), 1)

    def kv_blocks(i, r):
        return jnp.concatenate([kv_all[kv_at(PAIR * i + k, r)] for k in range(PAIR)], axis=0)

    def scores_pass(r, g):
        span = slice(g * lanes, (g + 1) * lanes)
        qz[:HD, :] = q_all[r, :, span]
        qz[HD:, :] = jnp.zeros((HD, lanes), BF)
        dz[HD:, :] = do_all[r, :, span]
        dz[:HD, :] = jnp.zeros((HD, lanes), BF)
        m_ref[...] = jnp.full(m_ref.shape, NEG, F32)
        l_ref[...] = jnp.zeros(l_ref.shape, F32)
        o_ref[...] = jnp.zeros(o_ref.shape, F32)
        dqa[...] = jnp.zeros(dqa.shape, F32)
        begin = doc_start(query_place, row_cuts(r))

        def body(i, _):
            keys = i * keys_at_once + key_iota
            bias = jnp.where((keys <= query_place) & (keys >= begin), 0.0, NEG)
            s = dot(kv_blocks(i, r), qz[...]) + jnp.concatenate([bias] * near, axis=1)
            s_ref[pl.ds(PAIR * i, PAIR)] = s.reshape(PAIR, BLK, lanes)
            m_ref[...] = jnp.maximum(m_ref[...], jnp.max(s.reshape(keys_at_once // 8, 8, lanes), axis=0))
            return 0

        lax.fori_loop(0, steps, body, 0)
        m_ref[0:1, :] = jnp.max(m_ref[...], axis=0, keepdims=True)

    def mix_pass(r, g):
        def body(i, _):
            v_t = kv_blocks(i, r).T[HD:]
            e = jnp.exp(s_ref[pl.ds(PAIR * i, PAIR)].reshape(keys_at_once, lanes) - m_ref[0:1, :])
            l_ref[...] += jnp.sum(e.reshape(keys_at_once // 8, 8, lanes), axis=0)
            e_low = e.astype(BF)
            e_ref[pl.ds(PAIR * i, PAIR)] = e_low.reshape(PAIR, BLK, lanes)
            o_ref[...] += dot(v_t, e_low)
            return 0

        lax.fori_loop(0, steps, body, 0)
        inv = 1.0 / jnp.sum(l_ref[...], axis=0, keepdims=True)
        o = o_ref[...] * inv
        l_ref[0:1, :] = inv
        m_ref[0:1, :] = jnp.sum(o * dz[HD:, :].astype(F32), axis=0, keepdims=True)
        span = row_span(r)
        for h in range(0, near, 2):
            pair = jnp.concatenate(
                [o[:, h * BLK : (h + 1) * BLK], o[:, (h + 1) * BLK : (h + 2) * BLK]], axis=0
            )
            at = slice((g * near + h) * HD, (g * near + h + 2) * HD)
            mt[at, span] = pair.astype(BF)

    def back_pass(r, g, cols=slice(0, lanes), more=False):
        wide = cols.stop - cols.start

        def body(i, _):
            kv = kv_blocks(i, r)
            k_t = kv.T[:HD]
            dp = dot(kv, dz[:, cols])
            p = e_ref[pl.ds(PAIR * i, PAIR), :, cols].reshape(keys_at_once, wide).astype(F32) * l_ref[0:1, cols]
            ds = (p * (dp - m_ref[0:1, cols])).astype(BF)
            total = dot_nt(ds, qz[:, cols]) + dot_nt(p.astype(BF), dz[:, cols])
            for k in range(PAIR):
                block = total[k * BLK : (k + 1) * BLK]
                if g > 0 or more:
                    block = block + dkv[at_bits(PAIR * i + k) + (r,)].astype(F32)
                dkv[at_bits(PAIR * i + k) + (r,)] = block.astype(BF)
            dqa[:, cols] += dot(k_t, ds)
            return 0

        lax.fori_loop(0, steps, body, 0)

    upper = range(a - 1, 0, -1)

    def dkv_pair(r):
        src = dkv.at[net.pick(range(a - 1, -1, -1), 0, False) + (r,)]
        return remote(src, dkv_core.at[r], dkv_send.at[r, 0], dkv_recv.at[r, 0], net.seq_xor(1))

    def dkv_chips(r):
        out = []
        for m in range(1, 2 ** (a - 1)):
            spot = tuple((1 - net.sb[i] if m >> (i - 1) & 1 else net.sb[i]) for i in upper)
            out.append(remote(dkv_core.at[(r,) + spot], dkv_chip.at[m - 1, r], dkv_send.at[r, m], dkv_recv.at[r, m],
                              net.seq_xor(2 * m)))
        return out

    def dkv_on(r):
        dkv_pair(r).wait()
        dkv_core[r] = dkv_core[r] + dkv[net.pick(range(a - 1, -1, -1), 0, True) + (r,)]
        for copy in dkv_chips(r):
            copy.start()

    def dkv_straight():
        out = []
        for m in range(1, n):
            peer = net.seq_xor(m)
            out.append((peer["seq"], remote(
                dkv.at[at_bits(peer["seq"]) + (rows - 1,)], dkv_in.at[m - 1],
                dkv_send.at[rows - 1, m - 1], dkv_recv.at[rows - 1, m - 1], peer)))
        return out

    def dkv_leave(r):
        if isinstance(r, int):
            for other, copy in dkv_straight():

                @pl.when(other < me)
                def _():
                    copy.start()

            dkv_on(r - 1)
        else:
            dkv_pair(r).start()

            @pl.when(r > 0)
            def _():
                dkv_on(r - 1)

    def dq_leave(r, g, first=0, stop=near):
        cosine, sine = cs[r, 0], cs[r, 1]
        span = row_span(r)
        for h in range(first, stop, 2):
            pair = jnp.concatenate(
                [rotate(dqa[:, i * BLK : (i + 1) * BLK], cosine, -sine) for i in (h, h + 1)], axis=0
            )
            dq[span, (g * near + h) * HD : (g * near + h + 2) * HD] = (pair * 0.125).T.astype(BF)

    def leave_pass(r, g):
        if g == groups - 1:
            dkv_leave(r)
        dq_leave(r, g)

    def first_groups(r):
        for g in range(groups - 1):
            scores_pass(r, g)
            mix_pass(r, g)
            back_pass(r, g)
            leave_pass(r, g)

    def chunk_step(t):
        if isinstance(t, int):
            down(t - n_up)
            ring.start(0, t)
            ring.tick(t)
            return

        @pl.when(t < n_up)
        def _():
            feed(t)

        @pl.when(t >= n_up)
        def _():
            down(t - n_up)

        ring.start(0, t)
        ring.tick(t)

    def row_step(r, _):
        t = n_pre + 3 * r
        first_groups(r)
        scores_pass(r, groups - 1)
        chunk_step(t)
        mix_pass(r, groups - 1)
        chunk_step(t + 1)
        back_pass(r, groups - 1)
        leave_pass(r, groups - 1)
        chunk_step(t + 2)
        return 0

    lax.fori_loop(0, rows - 1, row_step, 0)
    r, t = rows - 1, n_up + n_down
    now = [t]

    def advance(count):
        for _ in range(count):
            if now[0] <= ring.last_tick():
                ring.tick(now[0])
                now[0] += 1

    first_groups(r)
    scores_pass(r, groups - 1)
    advance(1)
    mix_pass(r, groups - 1)
    put_chunk(late.grads, 0, dot(mt[...], dy_ref[:, :CHUNK]))
    late.start(0)
    put_chunk(late.grads, 1, dot(mt[...], dy_ref[:, CHUNK : CHUNK + QUARTER]), (3,))
    advance(2)
    near_cols = slice(0, lanes // 2)
    if groups == 1:
        back_pass(r, 0, near_cols)
        dq_leave(r, 0, 0, near // 2)
    late.finish(0, "core")
    put_chunk(late.grads, 1, dot_tn(h1[...], dq[:, : width // 2]), (0, 1, 2))
    late.start(1)
    put_chunk(late.grads, 0, dot(mt[...], dy_ref[:, CHUNK + QUARTER :]), (3,))
    advance(2)
    if groups == 1:
        back_pass(r, 0, slice(lanes // 2, lanes), True)
        dkv_leave(r)
        dq_leave(r, 0, near // 2)
    else:
        back_pass(r, groups - 1)
        leave_pass(r, groups - 1)
    late.finish(1, "core")
    put_chunk(late.grads, 0, dot_tn(h1[...], dq[:, width // 2 :]), (0, 1, 2))
    late.start(2)
    late.finish(2, "core")
    advance(2)
    late.finish(0, "chips")
    by_rows(0, dot_nt(dup[...], wu[...]))
    late.finish(1, "chips")
    for kind in late.stages[2:-1]:
        late.finish(0, kind)
    advance(2)

    def narrow(step):
        if step == 0:
            return [
                remote(own_small, seq_small.at[me], m_send.at[m - 1], m_recv.at[m - 1], net.seq_xor(m)) for m in range(1, n)
            ]
        spot, base = row_small.at[net.row], n - 2
        return [
            remote(spot, spot, m_send.at[base + m], m_recv.at[base + m], net.row_xor(m)) for m in range(1, count)
        ]

    def narrow_kv(step):
        base = n + count - 2
        if step == 0:
            out = []
            for m in range(1, n):
                peer = net.seq_xor(m)
                out.append(remote(own_kv.at[peer["seq"]], seq_kv.at[m - 1],
                                  m_send.at[base + m - 1], m_recv.at[base + m - 1], peer))
            return out
        spot, base = row_kv.at[net.row], base + n - 2
        return [
            remote(spot, spot, m_send.at[base + m], m_recv.at[base + m], net.row_xor(m)) for m in range(1, count)
        ]

    dkv_sum[rows - 1] = dkv[at_bits(me) + (rows - 1,)].astype(F32)
    for r in range(rows - 1):
        total = dkv_core[(r,) + tuple(net.sb[i] for i in upper)].astype(F32)
        for m, copy in enumerate(dkv_chips(r)):
            copy.wait()
            total = total + dkv_chip[m, r].astype(F32)
        dkv_sum[r] = total
    for m, (other, copy) in enumerate(dkv_straight()):

        @pl.when(other < me)
        def _():
            copy.wait_send()

        @pl.when(other > me)
        def _():
            copy.wait_recv()
            dkv_sum[rows - 1] += dkv_in[m].astype(F32)

    d_kv = jnp.concatenate(
        [rotate(dkv_sum[r].T, cs[r, 0], -cs[r, 1]).T.astype(BF) for r in range(rows)], axis=0
    )
    g = dot_tn(h1[...], d_kv)
    for owner in range(n):
        own_kv[owner] = g[owner * sub : (owner + 1) * sub].astype(BF)
    for copy in narrow_kv(0):
        copy.start()

    by_rows(1, dot_nt(dq[...], wq[...]) + dot_nt(d_kv, wkv[...]))
    late.finish(2, "chips")
    own_small[...] = jnp.zeros(own_small.shape, F32)
    per = width // 128

    def add_small(at, vector):
        for i in range(vector.shape[1] // 128):
            own_small[at + i : at + i + 1, :] += vector[:, i * 128 : (i + 1) * 128]

    def norms_back(r, _):
        _, xhat, factor = normalized(r)
        dy32 = dy_ref[row_span(r), :].astype(F32)
        result = dy32
        for k, gain in enumerate((vec_ref[0:1, :], vec_ref[2:3, :])):
            grad = s_ref[spare(1 - k, r)]
            add_small(2 * k * per, column_sum(grad * xhat))
            add_small((2 * k + 1) * per, column_sum(grad))
            g = grad * gain
            result = result + factor * (g - lanes_mean(g) - xhat * lanes_mean(g * xhat))
        h2[row_span(r), :] = result.astype(BF)
        add_small(4 * per, column_sum(dq[row_span(r), :].astype(F32)))
        add_small(5 * per + 1, column_sum(dy32))
        return 0

    lax.fori_loop(0, rows, norms_back, 0)
    ig_copy = pltpu.make_async_copy(h2, ig_ref, load_sem.at[7])
    ig_copy.start()
    add_small(5 * per, column_sum(d_kv.astype(F32)))
    add_small(6 * per + 1, gub[...])

    for copy in narrow(0):
        copy.start()
    for kind in late.stages[2:-1]:
        late.finish(1, kind)
    advance(2)
    by_rows(2, dot(act[...], wd[...]) + vec_ref[5:6, :])
    for kind in late.stages[2:-1]:
        late.finish(2, kind)
    for copy in narrow_kv(0):
        copy.wait()
    sums = own_kv[me].astype(F32)
    for m in range(1, n):
        sums = sums + seq_kv[m - 1].astype(F32)
    row_kv[net.row] = sums.astype(BF)
    for copy in narrow_kv(1):
        copy.start()
    for copy in narrow(0):
        copy.wait()
    seq_small[me] = own_small[...]
    sums = seq_small[0]
    for i in range(1, n):
        sums = sums + seq_small[i]
    row_small[net.row] = sums
    for copy in narrow(1):
        copy.start()
    by_rows(3, dot_tn(mt[...], wo[...]))

    def layer_out(r, _):
        total = x_ref[row_span(r), :].astype(F32) + s_ref[spare(2, r)] + s_ref[spare(3, r)]
        h1[row_span(r), :] = total.astype(BF)
        return 0

    lax.fori_loop(0, rows, layer_out, 0)
    lo_copy = pltpu.make_async_copy(h1, lo_ref, load_sem.at[8])
    lo_copy.start()
    advance(99)
    for c in range(3):
        late.finish(c, "back")
    for copy in narrow(1):
        copy.wait()
    sums = row_small[0]
    for i in range(1, count):
        sums = sums + row_small[i]
    small_ref[...] = sums
    for copy in narrow_kv(1):
        copy.wait()
    sums = row_kv[0].astype(F32)
    for i in range(1, count):
        sums = sums + row_kv[i].astype(F32)
    gkv_ref[...] = sums
    ig_copy.wait()
    lo_copy.wait()


def layer(net_bits, lengths, x, dy, vectors, wq, wkv, wo, wu, wd):
    a, b = net_bits
    n, count = 2**a, 2**b
    toks, width = x.shape
    hidden = wu.shape[1]
    sub = width // n
    rows = toks // BLK
    all_lanes = width // HD * BLK
    lanes = all_lanes // max(1, n // 8)
    n_up, n_down = hidden // CHUNK, width // QUARTER
    early, late = n_up + n_down, 3
    total = early + late
    slots = RING
    low = min(b, 2)
    two = (2,)
    vm = pltpu.VMEM
    dma = pltpu.SemaphoreType.DMA
    n_sems = 1 + 2 * (a - 1) + b + min(b, 2)
    scratch = [
        vm(wq.shape, BF), vm(wkv.shape, BF), vm(wo.shape, BF), vm(wu.shape, BF), vm(wd.shape, BF), dma((9,)),
        vm((8, width), F32), vm((1, hidden), F32),
        vm((toks, width), BF), vm((toks, width), BF),
        vm((toks, hidden), BF), vm((hidden, toks), BF), vm((toks, hidden), BF), vm((1, hidden), F32),
        vm((rows, HD, all_lanes), BF), vm((rows, HD, all_lanes), BF), vm((rows, 2, 8, BLK), F32),
        vm(two * a + (2, rows // 2, BLK, 2 * HD), BF), dma((2 * a,)), dma((2 * a,)),
        vm((n, BLK, lanes), F32), vm((n, BLK, lanes), BF), vm((2 * HD, lanes), BF), vm((2 * HD, lanes), BF),
        vm((8, lanes), F32), vm((8, lanes), F32), vm((HD, lanes), F32), vm((HD, lanes), F32),
        vm((width, toks), BF), vm((toks, width), BF),
        vm(two * a + (rows, BLK, 2 * HD), BF), vm((n - 1, BLK, 2 * HD), BF),
        vm((rows - 1,) + two * (a - 1) + (BLK, 2 * HD), BF), vm((n // 2 - 1, rows - 1, BLK, 2 * HD), BF),
        vm((rows, BLK, 2 * HD), F32), dma((rows, n - 1)), dma((rows, n - 1)),
        vm((SLOTS,) + two * a + (2, 2, sub, 128), BF),
        vm((slots,) + two * (a - 1) + (2, 2, sub, 128), BF),
    ]
    scratch += [vm((slots, 2) + two * (a - 1 - k) + (2, sub, 128), BF) for k in range(1, a)]
    scratch += [vm((slots, 2, sub, 128), BF)] + [vm((slots, sub, 128), BF) for _ in range(1, b)]
    scratch += [
        dma((early, n_sems)), dma((early, n_sems)),
        vm((2,) + two * a + (2, 2, sub, 128), BF),
        vm((late,) + two * (a - 1) + (2, 2, sub, 128), BF),
        vm((late, n // 2 - 1, 2, 2, sub, 128), BF),
        vm((late, 2, 2, sub, 128), BF),
        vm((late, 2**low - 1, sub, 128), BF),
        vm((late, max(count // 4, 1), sub, 128), BF),
        dma((late, n // 2 + count + 2)), dma((late, n // 2 + count + 2)),
        vm((64, 128), F32), vm((n, 64, 128), F32), vm((count, 64, 128), F32),
        vm((n, sub, 2 * HD), BF), vm((n - 1, sub, 2 * HD), BF), vm((count, sub, 2 * HD), BF),
        dma((2 * (n + count),)), dma((2 * (n + count),)),
    ]
    vmem = pl.BlockSpec(memory_space=pltpu.VMEM)
    hbm = pl.BlockSpec(memory_space=pl.ANY)
    shape = jax.ShapeDtypeStruct
    return pl.pallas_call(
        functools.partial(layer_kernel, a, b),
        out_shape=[
            shape((toks, width), BF), shape((toks, width), BF),
            shape((total, 2, 2, sub, 128), BF), shape((64, 128), F32), shape((sub, 2 * HD), F32),
        ],
        in_specs=[pl.BlockSpec(memory_space=pltpu.SMEM)] + [vmem] * (2 + len(vectors)) + [hbm] * 5,
        out_specs=[hbm, hbm, vmem, vmem, vmem],
        scratch_shapes=scratch,
        compiler_params=pltpu.CompilerParams(collective_id=0, has_side_effects=True, vmem_limit_bytes=64 * 2**20),
        name="layer",
    )(lengths, x, dy, *vectors, wq, wkv, wo, wu, wd)


def finish_kernel(n_up, sizes, lo_in, ig_in, fin_in, small_in, gkv_in, lo, ig, gup, gdown, gout, gq, gkv, *rest):
    vectors, (fin, small, vlo, vig, vup, vdown, vout, vq, vkv, sem) = rest[: len(sizes)], rest[len(sizes) :]
    sub, width = gout.shape
    n_down = width // QUARTER
    late = n_up + n_down

    def move(i, src, dst):
        copy = pltpu.make_async_copy(src, dst, sem.at[i])
        copy.start()
        return copy

    loads = [move(0, fin_in, fin), move(1, small_in, small), move(8, gkv_in, vkv)]
    loads += [move(2, lo_in, vlo), move(3, ig_in, vig)]
    loads[0].wait()
    moves = []

    def piece(ch, q):
        return fin[ch, q // 2, q % 2].astype(F32)

    def span(at, q):
        return slice(at + q * QUARTER, at + (q + 1) * QUARTER)

    for q in range(4):
        for f in range(n_up):
            vup[:, span(f * CHUNK, q)] = piece(f, q)
    moves.append(move(4, vup, gup))
    for q in range(4):
        for j in range(n_down):
            vdown[q * sub : (q + 1) * sub, j * QUARTER : (j + 1) * QUARTER] = piece(n_up + j, q)
    moves.append(move(5, vdown, gdown))
    for load in loads[1:]:
        load.wait()
    moves += [move(9, vlo, lo), move(10, vig, ig)]
    for q in range(4):
        vout[:, span(0, q)] = piece(late, q)
        if q < 3:
            vq[:, span(0, q)] = piece(late + 1, q)
            vq[:, span(3 * QUARTER, q)] = piece(late + 2, q)
        else:
            vout[:, span(CHUNK, 0)] = piece(late + 1, q)
            vout[:, span(CHUNK, 1)] = piece(late + 2, q)
    moves += [move(6, vout, gout), move(7, vq, gq), move(11, vkv, gkv)]
    at = 0
    for size, ref in zip(sizes[:-1], vectors):
        for i in range(size // 128):
            ref[i * 128 : (i + 1) * 128] = small[at + i, :]
        at += size // 128
    vectors[-1][...] = vectors[-3][...]
    for copy in moves:
        copy.wait()


def finish(lo, ig, fin, small, gkv, sub, width, hidden):
    sizes = [width] * 5 + [2 * HD, width, hidden, width]
    shape = jax.ShapeDtypeStruct
    hbm = pl.BlockSpec(memory_space=pl.ANY)
    grads = [(sub, hidden), (4 * sub, width), (sub, width), (sub, width), (sub, 2 * HD)]
    return pl.pallas_call(
        functools.partial(finish_kernel, hidden // CHUNK, sizes),
        out_shape=[shape(lo.shape, BF), shape(ig.shape, BF)]
        + [shape(g, F32) for g in grads] + [shape((size,), F32) for size in sizes],
        in_specs=[hbm] * 5,
        out_specs=[hbm] * 7 + [pl.BlockSpec(memory_space=pltpu.VMEM)] * len(sizes),
        scratch_shapes=[pltpu.VMEM(fin.shape, BF), pltpu.VMEM(small.shape, F32), pltpu.VMEM(lo.shape, BF), pltpu.VMEM(ig.shape, BF)]
        + [pltpu.VMEM(g, F32) for g in grads] + [pltpu.SemaphoreType.DMA((12,))],
        compiler_params=pltpu.CompilerParams(vmem_limit_bytes=64 * 2**20),
        name="finish",
    )(lo, ig, fin, small, gkv)


def shards(
    hidden, lengths, cotangent, first_gain, first_shift, second_gain, second_shift,
    query_weight, query_bias, keyvalue_weight, keyvalue_bias, output_weight, output_bias,
    up_weight, up_bias, down_weight, down_bias,
):
    rows, block, width = hidden.shape
    toks = rows * block
    n, count = lax.axis_size("seq"), lax.axis_size("rows")
    vectors = (
        first_gain, first_shift, second_gain, second_shift, query_bias, output_bias, down_bias, keyvalue_bias, up_bias,
    )
    lo, ig, fin, small, g_kv = layer(
        (n.bit_length() - 1, count.bit_length() - 1), lengths,
        hidden.reshape(toks, width), cotangent.reshape(toks, width), vectors,
        query_weight, keyvalue_weight, output_weight, up_weight, down_weight,
    )
    lo, ig, g_up, g_down, g_out, g_q, g_kv, *sums = finish(
        lo, ig, fin, small, g_kv, width // n, width, up_weight.shape[1]
    )
    s_fg, s_fs, s_sg, s_ss, s_qb, s_kb, s_ob, s_ub, s_db = sums
    return (
        lo.reshape(hidden.shape), ig.reshape(hidden.shape),
        s_fg, s_fs, s_sg, s_ss, g_q, s_qb, g_kv, s_kb, g_out, s_ob, g_up, s_ub, g_down, s_db,
    )


def solution(mesh):
    tokens = P("rows", "seq", None)
    weight = P("seq", None)
    return jax.shard_map(
        shards,
        mesh=mesh,
        in_specs=(tokens, P("rows", None), tokens) + (P(),) * 14,
        out_specs=(
            tokens, tokens, P(), P(), P(), P(), weight, P(), weight, P(), weight, P(), weight, P(), weight, P(),
        ),
        check_vma=False,
    )
```

```python
import functools

import jax
import jax.numpy as jnp
from jax import lax
from jax.experimental import pallas as pl
from jax.experimental.pallas import tpu as pltpu
from jax.sharding import PartitionSpec as P

HD = 64
PAIR = 4
ROT = 16
BLK = 128
NEG = -1e30
EPS = 1e-05
F32 = jnp.float32
BF = jnp.bfloat16
MESH = pl.DeviceIdType.MESH
CHUNK = 512
QUARTER = 128
SLOTS = 3
RING = 8
WAITS = {"first": 1, "seq": 2}


def dot(a, b):
    return jnp.dot(a, b, preferred_element_type=F32)


def dot_nt(a, b):
    return lax.dot_general(a, b, (((1,), (1,)), ((), ())), preferred_element_type=F32)


def dot_tn(a, b):
    return lax.dot_general(a, b, (((0,), (0,)), ((), ())), preferred_element_type=F32)


def lanes_mean(v):
    return jnp.mean(v, axis=-1, keepdims=True)


def column_sum(v):
    return jnp.sum(v, axis=0, keepdims=True)


def doc_start(place, cuts):
    begin = jnp.where(place >= cuts[0], cuts[0], 0)
    for cut in cuts[1:]:
        begin = jnp.where(place >= cut, cut, begin)
    return begin


def rotate(values, cosine, sine):
    front, behind = values[:8], values[8:16]
    return jnp.concatenate([front * cosine - behind * sine, behind * cosine + front * sine, values[16:]], axis=0)


def gelu_parts(up):
    cdf = 0.5 + 0.5 * lax.erf(up * 0.7071067811865476)
    pdf = jnp.exp(-0.5 * up * up) * 0.3989422804014327
    return cdf, up * pdf


def bits_of(value, count):
    return [value // 2**i % 2 for i in range(count)]


def remote(src, dst, send_sem, recv_sem, peer):
    return pltpu.make_async_remote_copy(
        src_ref=src, dst_ref=dst, send_sem=send_sem, recv_sem=recv_sem, device_id=peer, device_id_type=MESH
    )


class Net:
    def __init__(self, seq_bits, row_bits):
        self.a, self.b = seq_bits, row_bits
        self.me, self.row = lax.axis_index("seq"), lax.axis_index("rows")
        self.sb, self.rb = bits_of(self.me, seq_bits), bits_of(self.row, row_bits)

    def seq_xor(self, mask):
        out = self.me
        for i in range(self.a):
            if mask >> i & 1:
                out = out + (1 - 2 * self.sb[i]) * 2**i
        return {"seq": out}

    def row_xor(self, mask):
        out = self.row
        for i in range(self.b):
            if mask >> i & 1:
                out = out + (1 - 2 * self.rb[i]) * 2**i
        return {"rows": out}

    def peers(self):
        return [self.seq_xor(m) for m in range(1, 2**self.a)] + [self.row_xor(m) for m in range(1, 2**self.b)]

    def pick(self, left, bit, mine):
        own = self.sb[bit]
        return tuple((own if mine else 1 - own) if i == bit else slice(None) for i in left)


class Ring:
    def __init__(self, net, early, grads, recs, recz, fin, send_sem, recv_sem):
        self.net, self.early = net, early
        self.grads, self.recs, self.recz, self.fin = grads, recs, recz, fin
        self.send_sem, self.recv_sem = send_sem, recv_sem
        a, b = net.a, net.b
        self.halves = min(b, 2)
        self.stages = [("first", 0)] + [("seq", k) for k in range(1, a)]
        self.stages += [("split", i) for i in range(self.halves)]
        self.stages += [("whole", i) for i in range(2, b)]
        self.stages += [("back", i) for i in reversed(range(self.halves))]
        self.sem_at, n = [], 0
        self.ticks_to, ticks = [], 0
        for kind, _ in self.stages:
            self.sem_at.append(n)
            n += 2 if kind == "seq" else 1
            ticks += WAITS.get(kind, 2)
            self.ticks_to.append(ticks)

    def moves(self, stage, ch):
        net, a = self.net, self.net.a
        kind, k = self.stages[stage]
        at = (ch % RING,)
        if kind == "first":
            left = range(a - 1, -1, -1)
            slot = (ch % SLOTS,)
            return [(self.grads.at[slot + net.pick(left, 0, False)], self.recs[0].at[at], net.seq_xor(1),
                     (self.grads, slot + net.pick(left, 0, True)), (self.recs[0], at))]
        if kind == "seq":
            out = []
            prev, here = self.recs[k - 1], self.recs[k]
            for half in (0, 1):
                if half == 0:
                    bit, left = k, range(a - 1, k - 1, -1)
                else:
                    bit, left = a - k, range(a - k, 0, -1)
                base, tail = (at, (half,)) if k == 1 else (at + (half,), ())
                out.append((prev.at[base + net.pick(left, bit, False) + tail], here.at[at + (half,)],
                            net.seq_xor(1 << bit), (prev, base + net.pick(left, bit, True) + tail), (here, at + (half,))))
            return out
        if kind == "split":
            prev = self.recs[a - 1] if k == 0 else self.recz[k - 1]
            return [(prev.at[at + (1 - net.rb[k],)], self.recz[k].at[at], net.row_xor(1 << k),
                     (prev, at + (net.rb[k],)), (self.recz[k], at))]
        if kind == "whole":
            prev = self.recz[k - 1]
            return [(prev.at[at], self.recz[k].at[at], net.row_xor(1 << k), (prev, at), (self.recz[k], at))]
        at = (ch,) + tuple(net.rb[: k + 1])
        return [(self.fin.at[at], self.fin.at[at], net.row_xor(1 << k), None, None)]

    def copies(self, stage, ch):
        out = []
        for i, (src, dst, peer, _, _) in enumerate(self.moves(stage, ch)):
            sem = self.sem_at[stage] + i
            out.append(remote(src, dst, self.send_sem.at[ch, sem], self.recv_sem.at[ch, sem], peer))
        return out

    def start(self, stage, ch):
        for copy in self.copies(stage, ch):
            copy.start()

    def finish(self, stage, ch):
        for copy in self.copies(stage, ch):
            copy.wait()
        kind, _ = self.stages[stage]
        if kind != "back":
            last = self.stages[stage + 1][0] == "back"
            for _, _, _, (src, src_at), (dst, dst_at) in self.moves(stage, ch):
                total = src[src_at] + dst[dst_at]
                if last:
                    self.fin[(ch,) + tuple(self.net.rb[: self.halves])] = total
                else:
                    dst[dst_at] = total
        if stage + 1 < len(self.stages):
            self.start(stage + 1, ch)

    def tick(self, t):
        for stage in reversed(range(len(self.stages))):
            ch = t - self.ticks_to[stage]
            if isinstance(ch, int):
                if 0 <= ch < self.early:
                    self.finish(stage, ch)
            else:

                @pl.when((ch >= 0) & (ch < self.early))
                def _():
                    self.finish(stage, ch)

    def last_tick(self):
        return self.early - 1 + self.ticks_to[-1]


class Late:
    def __init__(self, net, first, grads, pair, wide, part, quarter, cross, fin, send_sem, recv_sem):
        self.net, self.first, self.fin = net, first, fin
        self.grads, self.pair, self.wide, self.part = grads, pair, wide, part
        self.quarter, self.cross = quarter, cross
        self.send_sem, self.recv_sem = send_sem, recv_sem
        self.low = min(net.b, 2)
        self.stages = ["core", "chips", "split"] + (["cross"] if net.b > 2 else []) + ["back"]

    def copies(self, c, kind):
        net, a = self.net, self.net.a
        mine = tuple(net.rb[: self.low])
        moves = []
        if kind == "core":
            left = range(a - 1, -1, -1)
            moves.append((self.grads.at[(c % 2,) + net.pick(left, 0, False)], self.pair.at[c], net.seq_xor(1)))
        elif kind == "chips":
            for m in range(1, 2 ** (a - 1)):
                spot = tuple((1 - net.sb[i] if m >> (i - 1) & 1 else net.sb[i]) for i in range(a - 1, 0, -1))
                moves.append((self.pair.at[(c,) + spot], self.wide.at[c, m - 1], net.seq_xor(2 * m)))
        elif kind == "split":
            for m in range(1, 2**self.low):
                spot = tuple((1 - net.rb[i] if m >> i & 1 else net.rb[i]) for i in range(self.low))
                moves.append((self.part.at[(c,) + spot], self.quarter.at[c, m - 1], net.row_xor(m)))
        elif kind == "cross":
            spot = self.cross.at[c, net.row // 4]
            for m in range(1, 2 ** (net.b - 2)):
                moves.append((spot, spot, net.row_xor(4 * m)))
        else:
            spot = self.fin.at[(self.first + c,) + mine]
            for m in range(1, 2**self.low):
                moves.append((spot, spot, net.row_xor(m)))
        base = sum(len(self.copies(c, k)) for k in self.stages[: self.stages.index(kind)])
        return [
            remote(src, dst, self.send_sem.at[c, base + i], self.recv_sem.at[c, base + i], peer)
            for i, (src, dst, peer) in enumerate(moves)
        ]

    def start(self, c, kind="core"):
        for copy in self.copies(c, kind):
            copy.start()

    def finish(self, c, kind):
        net, a = self.net, self.net.a
        for copy in self.copies(c, kind):
            copy.wait()
        mine = tuple(net.rb[: self.low])
        at = self.stages.index(kind)
        if kind == "core":
            self.pair[c] = self.pair[c] + self.grads[(c % 2,) + net.pick(range(a - 1, -1, -1), 0, True)]
        elif kind == "chips":
            total = self.pair[(c,) + tuple(net.sb[i] for i in range(a - 1, 0, -1))].astype(F32)
            for m in range(1, 2 ** (a - 1)):
                total = total + self.wide[c, m - 1].astype(F32)
            self.part[c] = total.astype(BF)
        elif kind == "split":
            total = self.part[(c,) + mine].astype(F32)
            for m in range(1, 2**self.low):
                total = total + self.quarter[c, m - 1].astype(F32)
            if net.b > 2:
                self.cross[c, net.row // 4] = total.astype(BF)
            else:
                self.fin[(self.first + c,) + mine] = total.astype(BF)
        elif kind == "cross":
            total = self.cross[c, 0].astype(F32)
            for i in range(1, 2 ** (net.b - 2)):
                total = total + self.cross[c, i].astype(F32)
            self.fin[(self.first + c,) + mine] = total.astype(BF)
        if at + 1 < len(self.stages):
            self.start(c, self.stages[at + 1])


def layer_kernel(
    seq_bits, row_bits,
    len_ref, x_ref, dy_ref, fg_ref, fs_ref, sg_ref, ss_ref, bq_ref, bo_ref, bd_ref, bkv_ref, bu_ref, wq_hbm, wkv_hbm, wo_hbm, wu_hbm, wd_hbm,
    lo_ref, ig_ref, fin, small_ref, gkv_ref,
    wq, wkv, wo, wu, wd, load_sem, vec_ref, wide_ref,
    h1, h2, act, act_t, dup, gub, q_all, do_all, cs, kv_all, kv_send, kv_recv,
    s_ref, e_ref, qz, dz, m_ref, l_ref, o_ref, dqa, mt, dq, dkv, dkv_in, dkv_core, dkv_chip, dkv_sum, dkv_send, dkv_recv,
    grads, *rest,
):
    a, n, count = seq_bits, 2**seq_bits, 2**row_bits
    recs, rest = rest[:a], rest[a:]
    recz, rest = rest[:row_bits], rest[row_bits:]
    send_sem, recv_sem, rest = rest[0], rest[1], rest[2:]
    late_refs, rest = rest[:8], rest[8:]
    own_small, seq_small, row_small, own_kv, seq_kv, row_kv, m_send, m_recv = rest
    toks, width = x_ref.shape
    hidden = wu.shape[1]
    sub = width // n
    heads = width // HD
    lanes = s_ref.shape[-1]
    groups = heads * BLK // lanes
    near = lanes // BLK
    rows = toks // BLK
    n_up, n_down = hidden // CHUNK, width // QUARTER
    net = Net(seq_bits, row_bits)
    me = net.me
    n_early = n_up + n_down
    ring = Ring(net, n_early, grads, recs, recz, fin, send_sem, recv_sem)
    late = Late(net, n_early, *late_refs[:6], fin, *late_refs[6:])

    barrier = pltpu.get_barrier_semaphore()
    for peer in net.peers():
        pl.semaphore_signal(barrier, inc=1, device_id=peer, device_id_type=MESH)
    loads = {}
    head, tail = slice(0, CHUNK), slice(CHUNK, hidden)
    for i, (name, src, dst) in enumerate((
        ("kv", wkv_hbm, wkv), ("u0", wu_hbm.at[:, head], wu.at[:, head]), ("d0", wd_hbm.at[head], wd.at[head]),
        ("q", wq_hbm, wq), ("o", wo_hbm, wo), ("u", wu_hbm.at[:, tail], wu.at[:, tail]), ("d", wd_hbm.at[tail], wd.at[tail]),
    )):
        loads[name] = pltpu.make_async_copy(src, dst, load_sem.at[i])
        loads[name].start()

    for i, ref in enumerate((fg_ref, fs_ref, sg_ref, ss_ref, bq_ref)):
        vec_ref[i : i + 1, :] = ref[...].reshape(1, width)
    vec_ref[5:6, :] = (bo_ref[...] + bd_ref[...]).reshape(1, width)
    wide_ref[...] = bu_ref[...].reshape(1, hidden)

    def put_chunk(ref, ch, value, quarters=range(4)):
        for owner in range(n):
            at = (ch,) + tuple(reversed(bits_of(owner, a)))
            for i, q in enumerate(quarters):
                piece = value[owner * sub : (owner + 1) * sub, i * QUARTER : (i + 1) * QUARTER]
                ref[at + (q // 2, q % 2)] = piece.astype(BF)

    def row_cuts(r):
        cuts = []
        for i in range(len_ref.shape[1] - 1):
            cuts.append(len_ref[r, i] + (cuts[-1] if cuts else 0))
        return cuts

    place = me * BLK + lax.broadcasted_iota(jnp.int32, (8, BLK), 1)
    which = lax.broadcasted_iota(jnp.int32, (8, BLK), 0)
    freqs = jnp.ones((8, BLK), F32)
    for i in range(1, 8):
        freqs = jnp.where(which == i, 10000.0 ** (-2.0 * i / ROT), freqs)
    for r in range(rows):
        angles = (place - doc_start(place, row_cuts(r))).astype(F32) * freqs
        cs[r, 0] = jnp.cos(angles)
        cs[r, 1] = jnp.sin(angles)

    def row_span(r):
        return pl.ds(pl.multiple_of(r * BLK, BLK), BLK)

    def normalized(r):
        x = x_ref[row_span(r), :].astype(F32)
        centred = x - lanes_mean(x)
        factor = lax.rsqrt(lanes_mean(centred * centred) + EPS)
        return x, centred * factor, factor

    def norms(r, _):
        xhat = normalized(r)[1]
        h1[row_span(r), :] = (xhat * vec_ref[0:1, :] + vec_ref[1:2, :]).astype(BF)
        h2[row_span(r), :] = (xhat * vec_ref[2:3, :] + vec_ref[3:4, :]).astype(BF)
        return 0

    lax.fori_loop(0, rows, norms, 0)

    per_block = lanes // width

    def spare(k, r, cols=None):
        cols = slice(0, width) if cols is None else cols
        at = k % per_block * width
        return k // per_block * rows + r, slice(None), slice(at + cols.start, at + cols.stop)

    def by_rows(k, value):
        for r in range(rows):
            s_ref[spare(k, r)] = value[r * BLK : (r + 1) * BLK]

    loads["kv"].wait()
    kv = dot(h1[...], wkv[...]) + bkv_ref[...].reshape(1, 2 * HD)
    group = rows // 2

    def at_bits(value):
        return tuple(reversed(bits_of(value, a)))

    def kv_at(j, r):
        return at_bits(j) + (r // group, r % group)

    for r in range(rows):
        turned = rotate(kv[r * BLK : (r + 1) * BLK].T, cs[r, 0], cs[r, 1])
        kv_all[kv_at(me, r)] = turned.T.astype(BF)
    pl.semaphore_wait(barrier, n + count - 2)

    def kv_copies(k):
        out = []
        for half in (0, 1):
            order = list(range(1, a)) if half == 0 else list(range(a - 1, 0, -1))
            order.append(0)
            at = tuple(slice(None) if i in order[:k] else net.sb[i] for i in reversed(range(a))) + (half,)
            sem = 2 * k + half
            out.append(remote(kv_all.at[at], kv_all.at[at], kv_send.at[sem], kv_recv.at[sem], net.seq_xor(1 << order[k])))
        return out

    def kv_step(k):
        if k > 0:
            for copy in kv_copies(k - 1):
                copy.wait()
        if k < a:
            for copy in kv_copies(k):
                copy.start()

    kv_step(0)

    def feed(f):
        cols = pl.ds(pl.multiple_of(f * CHUNK, CHUNK), CHUNK)
        up = dot(h2[...], wu[:, cols]) + wide_ref[:, cols]
        d_act = dot_nt(dy_ref[...], wd[cols, :])
        cdf, slope = gelu_parts(up)
        low = (up * cdf).astype(BF)
        d_up = (d_act * (cdf + slope)).astype(BF)
        act[:, cols] = low
        act_t[cols, :] = low.T
        dup[:, cols] = d_up
        gub[:, cols] = column_sum(d_up.astype(F32))
        g = dot_tn(h2[...], d_up)
        put_chunk(grads, f % SLOTS, g)

    def down(j):
        cols = dy_ref[:, pl.ds(pl.multiple_of(j * QUARTER, QUARTER), QUARTER)]
        for owner in range(n):
            g = dot(act_t[owner * 4 * sub : (owner + 1) * 4 * sub, :], cols).astype(BF)
            at = ((n_up + j) % SLOTS,) + at_bits(owner)
            for i in range(4):
                grads[at + (i // 2, i % 2)] = g[i * sub : (i + 1) * sub]

    n_pre = 3
    dkv[...] = jnp.zeros(dkv.shape, BF)

    def feed_step(t, _):
        feed(t)
        ring.start(0, t)
        ring.tick(t)
        return 0

    loads["u0"].wait()
    loads["d0"].wait()
    feed_step(0, 0)

    loads["q"].wait()
    by_rows(0, dot(h1[...], wq[...]) + vec_ref[4:5, :])
    loads["o"].wait()
    by_rows(1, dot_nt(dy_ref[...], wo[...]))
    kv_step(1)

    def heads_apart(r, _):
        for h in range(0, heads, 2):
            pair = s_ref[spare(0, r, slice(h * HD, (h + 2) * HD))].T
            d_pair = s_ref[spare(1, r, slice(h * HD, (h + 2) * HD))].T.astype(BF)
            for i in (0, 1):
                span = slice((h + i) * BLK, (h + i + 1) * BLK)
                turned = rotate(pair[i * HD : (i + 1) * HD], cs[r, 0], cs[r, 1]).astype(BF).astype(F32)
                q_all[r, :, span] = (turned * 0.125).astype(BF)
                do_all[r, :, span] = d_pair[i * HD : (i + 1) * HD]
        return 0

    lax.fori_loop(0, rows, heads_apart, 0)
    kv_step(2)

    loads["u"].wait()
    loads["d"].wait()
    lax.fori_loop(1, n_pre, feed_step, 0)
    for k in range(3, a + 1):
        kv_step(k)

    keys_at_once = PAIR * BLK
    steps = me // PAIR + 1
    key_iota = lax.broadcasted_iota(jnp.int32, (keys_at_once, BLK), 0)
    query_place = me * BLK + lax.broadcasted_iota(jnp.int32, (keys_at_once, BLK), 1)

    def kv_blocks(i, r):
        return jnp.concatenate([kv_all[kv_at(PAIR * i + k, r)] for k in range(PAIR)], axis=0)

    def scores_pass(r, g):
        span = slice(g * lanes, (g + 1) * lanes)
        qz[:HD, :] = q_all[r, :, span]
        qz[HD:, :] = jnp.zeros((HD, lanes), BF)
        dz[HD:, :] = do_all[r, :, span]
        dz[:HD, :] = jnp.zeros((HD, lanes), BF)
        m_ref[...] = jnp.full(m_ref.shape, NEG, F32)
        l_ref[...] = jnp.zeros(l_ref.shape, F32)
        o_ref[...] = jnp.zeros(o_ref.shape, F32)
        dqa[...] = jnp.zeros(dqa.shape, F32)
        begin = doc_start(query_place, row_cuts(r))

        def body(i, _):
            keys = i * keys_at_once + key_iota
            bias = jnp.where((keys <= query_place) & (keys >= begin), 0.0, NEG)
            s = dot(kv_blocks(i, r), qz[...]) + jnp.concatenate([bias] * near, axis=1)
            s_ref[pl.ds(PAIR * i, PAIR)] = s.reshape(PAIR, BLK, lanes)
            m_ref[...] = jnp.maximum(m_ref[...], jnp.max(s.reshape(keys_at_once // 8, 8, lanes), axis=0))
            return 0

        lax.fori_loop(0, steps, body, 0)
        m_ref[0:1, :] = jnp.max(m_ref[...], axis=0, keepdims=True)

    def mix_pass(r, g):
        def body(i, _):
            v_t = kv_blocks(i, r).T[HD:]
            e = jnp.exp(s_ref[pl.ds(PAIR * i, PAIR)].reshape(keys_at_once, lanes) - m_ref[0:1, :])
            l_ref[...] += jnp.sum(e.reshape(keys_at_once // 8, 8, lanes), axis=0)
            e_low = e.astype(BF)
            e_ref[pl.ds(PAIR * i, PAIR)] = e_low.reshape(PAIR, BLK, lanes)
            o_ref[...] += dot(v_t, e_low)
            return 0

        lax.fori_loop(0, steps, body, 0)
        inv = 1.0 / jnp.sum(l_ref[...], axis=0, keepdims=True)
        o = o_ref[...] * inv
        l_ref[0:1, :] = inv
        m_ref[0:1, :] = jnp.sum(o * dz[HD:, :].astype(F32), axis=0, keepdims=True)
        span = row_span(r)
        for h in range(0, near, 2):
            pair = jnp.concatenate(
                [o[:, h * BLK : (h + 1) * BLK], o[:, (h + 1) * BLK : (h + 2) * BLK]], axis=0
            )
            at = slice((g * near + h) * HD, (g * near + h + 2) * HD)
            mt[at, span] = pair.astype(BF)

    def back_pass(r, g, cols=slice(0, lanes), more=False):
        wide = cols.stop - cols.start

        def body(i, _):
            kv = kv_blocks(i, r)
            k_t = kv.T[:HD]
            dp = dot(kv, dz[:, cols])
            p = e_ref[pl.ds(PAIR * i, PAIR), :, cols].reshape(keys_at_once, wide).astype(F32) * l_ref[0:1, cols]
            ds = (p * (dp - m_ref[0:1, cols])).astype(BF)
            total = dot_nt(ds, qz[:, cols]) + dot_nt(p.astype(BF), dz[:, cols])
            for k in range(PAIR):
                block = total[k * BLK : (k + 1) * BLK]
                if g > 0 or more:
                    block = block + dkv[at_bits(PAIR * i + k) + (r,)].astype(F32)
                dkv[at_bits(PAIR * i + k) + (r,)] = block.astype(BF)
            dqa[:, cols] += dot(k_t, ds)
            return 0

        lax.fori_loop(0, steps, body, 0)

    upper = range(a - 1, 0, -1)

    def dkv_pair(r):
        src = dkv.at[net.pick(range(a - 1, -1, -1), 0, False) + (r,)]
        return remote(src, dkv_core.at[r], dkv_send.at[r, 0], dkv_recv.at[r, 0], net.seq_xor(1))

    def dkv_chips(r):
        out = []
        for m in range(1, 2 ** (a - 1)):
            spot = tuple((1 - net.sb[i] if m >> (i - 1) & 1 else net.sb[i]) for i in upper)
            out.append(remote(dkv_core.at[(r,) + spot], dkv_chip.at[m - 1, r], dkv_send.at[r, m], dkv_recv.at[r, m],
                              net.seq_xor(2 * m)))
        return out

    def dkv_on(r):
        dkv_pair(r).wait()
        dkv_core[r] = dkv_core[r] + dkv[net.pick(range(a - 1, -1, -1), 0, True) + (r,)]
        for copy in dkv_chips(r):
            copy.start()

    def dkv_straight():
        out = []
        for m in range(1, n):
            peer = net.seq_xor(m)
            out.append((peer["seq"], remote(
                dkv.at[at_bits(peer["seq"]) + (rows - 1,)], dkv_in.at[m - 1],
                dkv_send.at[rows - 1, m - 1], dkv_recv.at[rows - 1, m - 1], peer)))
        return out

    def dkv_leave(r):
        if isinstance(r, int):
            for other, copy in dkv_straight():

                @pl.when(other < me)
                def _():
                    copy.start()

            dkv_on(r - 1)
        else:
            dkv_pair(r).start()

            @pl.when(r > 0)
            def _():
                dkv_on(r - 1)

    def dq_leave(r, g, first=0, stop=near):
        cosine, sine = cs[r, 0], cs[r, 1]
        span = row_span(r)
        for h in range(first, stop, 2):
            pair = jnp.concatenate(
                [rotate(dqa[:, i * BLK : (i + 1) * BLK], cosine, -sine) for i in (h, h + 1)], axis=0
            )
            dq[span, (g * near + h) * HD : (g * near + h + 2) * HD] = (pair * 0.125).T.astype(BF)

    def leave_pass(r, g):
        if g == groups - 1:
            dkv_leave(r)
        dq_leave(r, g)

    def first_groups(r):
        for g in range(groups - 1):
            scores_pass(r, g)
            mix_pass(r, g)
            back_pass(r, g)
            leave_pass(r, g)

    def chunk_step(t):
        if isinstance(t, int):
            down(t - n_up)
            ring.start(0, t)
            ring.tick(t)
            return

        @pl.when(t < n_up)
        def _():
            feed(t)

        @pl.when(t >= n_up)
        def _():
            down(t - n_up)

        ring.start(0, t)
        ring.tick(t)

    def row_step(r, _):
        t = n_pre + 3 * r
        first_groups(r)
        scores_pass(r, groups - 1)
        chunk_step(t)
        mix_pass(r, groups - 1)
        chunk_step(t + 1)
        back_pass(r, groups - 1)
        leave_pass(r, groups - 1)
        chunk_step(t + 2)
        return 0

    lax.fori_loop(0, rows - 1, row_step, 0)
    r, t = rows - 1, n_up + n_down
    now = [t]

    def advance(count):
        for _ in range(count):
            if now[0] <= ring.last_tick():
                ring.tick(now[0])
                now[0] += 1

    first_groups(r)
    scores_pass(r, groups - 1)
    advance(1)
    mix_pass(r, groups - 1)
    put_chunk(late.grads, 0, dot(mt[...], dy_ref[:, :CHUNK]))
    late.start(0)
    put_chunk(late.grads, 1, dot(mt[...], dy_ref[:, CHUNK : CHUNK + QUARTER]), (3,))
    advance(2)
    near_cols = slice(0, lanes // 2)
    if groups == 1:
        back_pass(r, 0, near_cols)
        dq_leave(r, 0, 0, near // 2)
    late.finish(0, "core")
    put_chunk(late.grads, 1, dot_tn(h1[...], dq[:, : width // 2]), (0, 1, 2))
    late.start(1)
    put_chunk(late.grads, 0, dot(mt[...], dy_ref[:, CHUNK + QUARTER :]), (3,))
    advance(2)
    if groups == 1:
        back_pass(r, 0, slice(lanes // 2, lanes), True)
        dkv_leave(r)
        dq_leave(r, 0, near // 2)
    else:
        back_pass(r, groups - 1)
        leave_pass(r, groups - 1)
    late.finish(1, "core")
    put_chunk(late.grads, 0, dot_tn(h1[...], dq[:, width // 2 :]), (0, 1, 2))
    late.start(2)
    late.finish(2, "core")
    advance(2)
    late.finish(0, "chips")
    by_rows(0, dot_nt(dup[...], wu[...]))
    late.finish(1, "chips")
    for kind in late.stages[2:-1]:
        late.finish(0, kind)
    advance(2)

    def narrow(step):
        if step == 0:
            return [
                remote(own_small, seq_small.at[me], m_send.at[m - 1], m_recv.at[m - 1], net.seq_xor(m)) for m in range(1, n)
            ]
        spot, base = row_small.at[net.row], n - 2
        return [
            remote(spot, spot, m_send.at[base + m], m_recv.at[base + m], net.row_xor(m)) for m in range(1, count)
        ]

    def narrow_kv(step):
        base = n + count - 2
        if step == 0:
            out = []
            for m in range(1, n):
                peer = net.seq_xor(m)
                out.append(remote(own_kv.at[peer["seq"]], seq_kv.at[m - 1],
                                  m_send.at[base + m - 1], m_recv.at[base + m - 1], peer))
            return out
        spot, base = row_kv.at[net.row], base + n - 2
        return [
            remote(spot, spot, m_send.at[base + m], m_recv.at[base + m], net.row_xor(m)) for m in range(1, count)
        ]

    dkv_sum[rows - 1] = dkv[at_bits(me) + (rows - 1,)].astype(F32)
    for r in range(rows - 1):
        total = dkv_core[(r,) + tuple(net.sb[i] for i in upper)].astype(F32)
        for m, copy in enumerate(dkv_chips(r)):
            copy.wait()
            total = total + dkv_chip[m, r].astype(F32)
        dkv_sum[r] = total
    for m, (other, copy) in enumerate(dkv_straight()):

        @pl.when(other < me)
        def _():
            copy.wait_send()

        @pl.when(other > me)
        def _():
            copy.wait_recv()
            dkv_sum[rows - 1] += dkv_in[m].astype(F32)

    d_kv = jnp.concatenate(
        [rotate(dkv_sum[r].T, cs[r, 0], -cs[r, 1]).T.astype(BF) for r in range(rows)], axis=0
    )
    g = dot_tn(h1[...], d_kv)
    for owner in range(n):
        own_kv[owner] = g[owner * sub : (owner + 1) * sub].astype(BF)
    for copy in narrow_kv(0):
        copy.start()

    by_rows(1, dot_nt(dq[...], wq[...]) + dot_nt(d_kv, wkv[...]))
    late.finish(2, "chips")
    own_small[...] = jnp.zeros(own_small.shape, F32)
    per = width // 128

    def add_small(at, vector):
        for i in range(vector.shape[1] // 128):
            own_small[at + i : at + i + 1, :] += vector[:, i * 128 : (i + 1) * 128]

    def norms_back(r, _):
        _, xhat, factor = normalized(r)
        dy32 = dy_ref[row_span(r), :].astype(F32)
        result = dy32
        for k, gain in enumerate((vec_ref[0:1, :], vec_ref[2:3, :])):
            grad = s_ref[spare(1 - k, r)]
            add_small(2 * k * per, column_sum(grad * xhat))
            add_small((2 * k + 1) * per, column_sum(grad))
            g = grad * gain
            result = result + factor * (g - lanes_mean(g) - xhat * lanes_mean(g * xhat))
        h2[row_span(r), :] = result.astype(BF)
        add_small(4 * per, column_sum(dq[row_span(r), :].astype(F32)))
        add_small(5 * per + 1, column_sum(dy32))
        return 0

    lax.fori_loop(0, rows, norms_back, 0)
    ig_copy = pltpu.make_async_copy(h2, ig_ref, load_sem.at[7])
    ig_copy.start()
    add_small(5 * per, column_sum(d_kv.astype(F32)))
    add_small(6 * per + 1, gub[...])

    for copy in narrow(0):
        copy.start()
    for kind in late.stages[2:-1]:
        late.finish(1, kind)
    advance(2)
    by_rows(2, dot(act[...], wd[...]) + vec_ref[5:6, :])
    for kind in late.stages[2:-1]:
        late.finish(2, kind)
    for copy in narrow_kv(0):
        copy.wait()
    sums = own_kv[me].astype(F32)
    for m in range(1, n):
        sums = sums + seq_kv[m - 1].astype(F32)
    row_kv[net.row] = sums.astype(BF)
    for copy in narrow_kv(1):
        copy.start()
    for copy in narrow(0):
        copy.wait()
    seq_small[me] = own_small[...]
    sums = seq_small[0]
    for i in range(1, n):
        sums = sums + seq_small[i]
    row_small[net.row] = sums
    for copy in narrow(1):
        copy.start()
    by_rows(3, dot_tn(mt[...], wo[...]))

    def layer_out(r, _):
        total = x_ref[row_span(r), :].astype(F32) + s_ref[spare(2, r)] + s_ref[spare(3, r)]
        h1[row_span(r), :] = total.astype(BF)
        return 0

    lax.fori_loop(0, rows, layer_out, 0)
    lo_copy = pltpu.make_async_copy(h1, lo_ref, load_sem.at[8])
    lo_copy.start()
    advance(99)
    for c in range(3):
        late.finish(c, "back")
    for copy in narrow(1):
        copy.wait()
    sums = row_small[0]
    for i in range(1, count):
        sums = sums + row_small[i]
    small_ref[...] = sums
    for copy in narrow_kv(1):
        copy.wait()
    sums = row_kv[0].astype(F32)
    for i in range(1, count):
        sums = sums + row_kv[i].astype(F32)
    gkv_ref[...] = sums
    ig_copy.wait()
    lo_copy.wait()


def layer(net_bits, lengths, x, dy, vectors, wq, wkv, wo, wu, wd):
    a, b = net_bits
    n, count = 2**a, 2**b
    toks, width = x.shape
    hidden = wu.shape[1]
    sub = width // n
    rows = toks // BLK
    all_lanes = width // HD * BLK
    lanes = all_lanes // max(1, n // 8)
    n_up, n_down = hidden // CHUNK, width // QUARTER
    early, late = n_up + n_down, 3
    total = early + late
    slots = RING
    low = min(b, 2)
    two = (2,)
    vm = pltpu.VMEM
    dma = pltpu.SemaphoreType.DMA
    n_sems = 1 + 2 * (a - 1) + b + min(b, 2)
    scratch = [
        vm(wq.shape, BF), vm(wkv.shape, BF), vm(wo.shape, BF), vm(wu.shape, BF), vm(wd.shape, BF), dma((9,)),
        vm((8, width), F32), vm((1, hidden), F32),
        vm((toks, width), BF), vm((toks, width), BF),
        vm((toks, hidden), BF), vm((hidden, toks), BF), vm((toks, hidden), BF), vm((1, hidden), F32),
        vm((rows, HD, all_lanes), BF), vm((rows, HD, all_lanes), BF), vm((rows, 2, 8, BLK), F32),
        vm(two * a + (2, rows // 2, BLK, 2 * HD), BF), dma((2 * a,)), dma((2 * a,)),
        vm((n, BLK, lanes), F32), vm((n, BLK, lanes), BF), vm((2 * HD, lanes), BF), vm((2 * HD, lanes), BF),
        vm((8, lanes), F32), vm((8, lanes), F32), vm((HD, lanes), F32), vm((HD, lanes), F32),
        vm((width, toks), BF), vm((toks, width), BF),
        vm(two * a + (rows, BLK, 2 * HD), BF), vm((n - 1, BLK, 2 * HD), BF),
        vm((rows - 1,) + two * (a - 1) + (BLK, 2 * HD), BF), vm((n // 2 - 1, rows - 1, BLK, 2 * HD), BF),
        vm((rows, BLK, 2 * HD), F32), dma((rows, n - 1)), dma((rows, n - 1)),
        vm((SLOTS,) + two * a + (2, 2, sub, 128), BF),
        vm((slots,) + two * (a - 1) + (2, 2, sub, 128), BF),
    ]
    scratch += [vm((slots, 2) + two * (a - 1 - k) + (2, sub, 128), BF) for k in range(1, a)]
    scratch += [vm((slots, 2, sub, 128), BF)] + [vm((slots, sub, 128), BF) for _ in range(1, b)]
    scratch += [
        dma((early, n_sems)), dma((early, n_sems)),
        vm((2,) + two * a + (2, 2, sub, 128), BF),
        vm((late,) + two * (a - 1) + (2, 2, sub, 128), BF),
        vm((late, n // 2 - 1, 2, 2, sub, 128), BF),
        vm((late, 2, 2, sub, 128), BF),
        vm((late, 2**low - 1, sub, 128), BF),
        vm((late, max(count // 4, 1), sub, 128), BF),
        dma((late, n // 2 + count + 2)), dma((late, n // 2 + count + 2)),
        vm((64, 128), F32), vm((n, 64, 128), F32), vm((count, 64, 128), F32),
        vm((n, sub, 2 * HD), BF), vm((n - 1, sub, 2 * HD), BF), vm((count, sub, 2 * HD), BF),
        dma((2 * (n + count),)), dma((2 * (n + count),)),
    ]
    vmem = pl.BlockSpec(memory_space=pltpu.VMEM)
    hbm = pl.BlockSpec(memory_space=pl.ANY)
    shape = jax.ShapeDtypeStruct
    return pl.pallas_call(
        functools.partial(layer_kernel, a, b),
        out_shape=[
            shape((toks, width), BF), shape((toks, width), BF),
            shape((total, 2, 2, sub, 128), BF), shape((64, 128), F32), shape((sub, 2 * HD), F32),
        ],
        in_specs=[pl.BlockSpec(memory_space=pltpu.SMEM)] + [vmem] * (2 + len(vectors)) + [hbm] * 5,
        out_specs=[hbm, hbm, vmem, vmem, vmem],
        scratch_shapes=scratch,
        compiler_params=pltpu.CompilerParams(collective_id=0, has_side_effects=True, vmem_limit_bytes=64 * 2**20),
        name="layer",
    )(lengths, x, dy, *vectors, wq, wkv, wo, wu, wd)


def finish_kernel(n_up, sizes, lo_in, ig_in, fin_in, small_in, gkv_in, lo, ig, gup, gdown, gout, gq, gkv, *rest):
    k = len(sizes)
    vectors, held, (fin, small, vlo, vig, vup, vdown, vout, vq, vkv, sem) = rest[:k], rest[k : 2 * k], rest[2 * k :]
    sub, width = gout.shape
    n_down = width // QUARTER
    late = n_up + n_down

    def move(i, src, dst):
        copy = pltpu.make_async_copy(src, dst, sem.at[i])
        copy.start()
        return copy

    loads = [move(1, small_in, small), move(0, fin_in, fin), move(8, gkv_in, vkv)]
    loads += [move(2, lo_in, vlo), move(3, ig_in, vig)]
    loads[0].wait()
    at = 0
    for size, ref in zip(sizes[:-1], held):
        for i in range(size // 128):
            ref[i * 128 : (i + 1) * 128] = small[at + i, :]
        at += size // 128
    held[-1][...] = held[-3][...]
    moves = [move(12 + i, src, dst) for i, (src, dst) in enumerate(zip(held, vectors))]
    loads[1].wait()

    def piece(ch, q):
        return fin[ch, q // 2, q % 2].astype(F32)

    def span(at, q):
        return slice(at + q * QUARTER, at + (q + 1) * QUARTER)

    for q in range(4):
        for f in range(n_up):
            vup[:, span(f * CHUNK, q)] = piece(f, q)
    moves.append(move(4, vup, gup))
    for q in range(4):
        for j in range(n_down):
            vdown[q * sub : (q + 1) * sub, j * QUARTER : (j + 1) * QUARTER] = piece(n_up + j, q)
    moves.append(move(5, vdown, gdown))
    for load in loads[2:]:
        load.wait()
    moves += [move(9, vlo, lo), move(10, vig, ig)]
    for q in range(4):
        vout[:, span(0, q)] = piece(late, q)
        if q < 3:
            vq[:, span(0, q)] = piece(late + 1, q)
            vq[:, span(3 * QUARTER, q)] = piece(late + 2, q)
        else:
            vout[:, span(CHUNK, 0)] = piece(late + 1, q)
            vout[:, span(CHUNK, 1)] = piece(late + 2, q)
    moves += [move(6, vout, gout), move(7, vq, gq), move(11, vkv, gkv)]
    for copy in moves:
        copy.wait()


def finish(lo, ig, fin, small, gkv, sub, width, hidden):
    sizes = [width] * 5 + [2 * HD, width, hidden, width]
    shape = jax.ShapeDtypeStruct
    hbm = pl.BlockSpec(memory_space=pl.ANY)
    grads = [(sub, hidden), (4 * sub, width), (sub, width), (sub, width), (sub, 2 * HD)]
    return pl.pallas_call(
        functools.partial(finish_kernel, hidden // CHUNK, sizes),
        out_shape=[shape(lo.shape, BF), shape(ig.shape, BF)]
        + [shape(g, F32) for g in grads] + [shape((size,), F32) for size in sizes],
        in_specs=[hbm] * 5,
        out_specs=[hbm] * (7 + len(sizes)),
        scratch_shapes=[pltpu.VMEM((size,), F32) for size in sizes]
        + [pltpu.VMEM(fin.shape, BF), pltpu.VMEM(small.shape, F32), pltpu.VMEM(lo.shape, BF), pltpu.VMEM(ig.shape, BF)]
        + [pltpu.VMEM(g, F32) for g in grads] + [pltpu.SemaphoreType.DMA((12 + len(sizes),))],
        compiler_params=pltpu.CompilerParams(vmem_limit_bytes=64 * 2**20),
        name="finish",
    )(lo, ig, fin, small, gkv)


def shards(
    hidden, lengths, cotangent, first_gain, first_shift, second_gain, second_shift,
    query_weight, query_bias, keyvalue_weight, keyvalue_bias, output_weight, output_bias,
    up_weight, up_bias, down_weight, down_bias,
):
    rows, block, width = hidden.shape
    toks = rows * block
    n, count = lax.axis_size("seq"), lax.axis_size("rows")
    vectors = (
        first_gain, first_shift, second_gain, second_shift, query_bias, output_bias, down_bias, keyvalue_bias, up_bias,
    )
    lo, ig, fin, small, g_kv = layer(
        (n.bit_length() - 1, count.bit_length() - 1), lengths,
        hidden.reshape(toks, width), cotangent.reshape(toks, width), vectors,
        query_weight, keyvalue_weight, output_weight, up_weight, down_weight,
    )
    lo, ig, g_up, g_down, g_out, g_q, g_kv, *sums = finish(
        lo, ig, fin, small, g_kv, width // n, width, up_weight.shape[1]
    )
    s_fg, s_fs, s_sg, s_ss, s_qb, s_kb, s_ob, s_ub, s_db = sums
    return (
        lo.reshape(hidden.shape), ig.reshape(hidden.shape),
        s_fg, s_fs, s_sg, s_ss, g_q, s_qb, g_kv, s_kb, g_out, s_ob, g_up, s_ub, g_down, s_db,
    )


def solution(mesh):
    tokens = P("rows", "seq", None)
    weight = P("seq", None)
    return jax.shard_map(
        shards,
        mesh=mesh,
        in_specs=(tokens, P("rows", None), tokens) + (P(),) * 14,
        out_specs=(
            tokens, tokens, P(), P(), P(), P(), weight, P(), weight, P(), weight, P(), weight, P(), weight, P(),
        ),
        check_vma=False,
    )
```
